32 devices in a mesh: groups: 2 (over y), dp: 4 (over z), feat: 2 (over x), sub: 2 (over core).
Axes of the slice: x: 2, y: 2, z: 4, core: 2. Of those that a mesh axis runs over, the one named last changes fastest.
Arguments:
- bins: int32 [32768, 1024], P(('groups', 'dp', 'sub'), 'feat'), parts along dimension 0, may hold values from 0 to 127
- grads: bfloat16 [32768, 32], P(('groups', 'dp', 'sub')), parts along dimension 0, may hold values from -6 to 6
- hess: bfloat16 [32768], P(('groups', 'dp', 'sub')), parts along dimension 0, may hold values from 0.25 to 4
- node_side: int32 [32768], P(('groups', 'dp', 'sub')), parts along dimension 0, may hold values from 0 to 1
- signs: int32 [2048], P('groups'), parts along dimension 0, may hold values from -1 to 1
- child_owner: int32 [16], P('groups'), parts along dimension 0, may hold values from 0 to 7, each once
- parent_owner: int32 [16], P('groups'), parts along dimension 0, may hold values from 0 to 7, each once
- parent_grad: float32 [16, 128, 4096], P(('groups', 'dp', 'sub'), 'feat'), parts along dimension 0, may hold values from -48 to 48
- parent_hess: float32 [16, 128, 128], P(('groups', 'dp', 'sub'), 'feat'), parts along dimension 0, may hold values from 33 to 516
- node_low: int32 [4], P('groups'), parts along dimension 0, may hold values from -40 to -5
- node_high: int32 [4], P('groups'), parts along dimension 0, may hold values from 5 to 40
Outputs:
- gains: float32 [16, 128, 2, 128], P(('groups', 'dp', 'sub'), 'feat'), parts along dimension 0
The draws below stay inside these ranges and needn't reach their ends.
There are 2 independent parts, one for each index of `groups`. The reference program is written for one: setup_inputs(seed, part) draws one part's arguments, and reference() takes and returns one part's arrays. A program takes and returns all parts, laid end to end along the dimension named above; each array names one. Nothing has to cross between parts.
Inputs may be any that keep to these rules, and one draw needn't show every extreme that they name: `child_owner`: each slot number appears once. `parent_owner`: each slot number appears once.
All inputs are finite; a program needn't handle non-finite values.
Results may differ from the reference program's by a relative error of at most 0.0003.
Values sent between devices are 32-bit elements; how exact they have to be, the bound alone decides.
No kernel may reach another device: no remote copies, remote signals or barrier semaphores. Data moves between devices by JAX's collectives and lax.ppermute only.
A program may use at most 128 MiB of HBM per device.

```python
import math
import jax
import jax.numpy as jnp
from jax import lax

K = 32
BINS = 128
F = 1024
ROWS = 16384
OWN = 8
FS = 64
N_FEAT = 2


def with_ends(entries, key, low, top_value):
    longest = entries.shape.index(max(entries.shape))
    spots = []
    for shift in (0, 1):
        where = [jax.random.randint(jax.random.fold_in(key, axis), (), 0, length) for axis, length in enumerate(entries.shape)]
        where[longest] = (where[longest] + shift) % entries.shape[longest]
        spots.append(tuple(where))
    return entries.at[spots[0]].set(low).at[spots[1]].set(top_value)


def level_of(key, shape, split, low, largest):
    def one(position, shards_of):
        draws = jax.random.uniform(jax.random.fold_in(jax.random.fold_in(key, 6), position), (shards_of,), jnp.float32, low / len(split), largest / len(split))
        return jnp.repeat(jnp.exp(draws), shape[position] // shards_of).reshape((-1,) + (1,) * (len(shape) - position - 1))

    level = one(*split[0])
    for cut in split[1:]:
        level = level * one(*cut)
    return level


def bell_draw(stream_key, dims, deviation, bound, split=(), held_as=jnp.bfloat16):
    values = deviation * jax.random.normal(stream_key, dims, jnp.float32)
    if split:
        values = values * level_of(stream_key, dims, split, -0.22, 0.18)
    return jnp.clip(values, -bound, bound).astype(held_as)


def setup_inputs(seed: int = 0, part: int = 0) -> dict:
    splits = jax.random.split(jax.random.key(seed), 12)
    part_keys = jax.random.split(jax.random.fold_in(splits[11], part), 12)
    return {
        "bins": with_ends(jax.random.randint(part_keys[0], (ROWS, F), 0, BINS), jax.random.fold_in(part_keys[0], 1), 0, BINS - 1).astype(jnp.int32),
        "grads": bell_draw(part_keys[1], (ROWS, K), 1.0, 6.0, ((0, 8),)),
        "hess": jnp.clip(jnp.exp(math.log(4.0) - 2.7725887 * jax.random.uniform(part_keys[2], (ROWS,), jnp.float32) ** level_of(part_keys[2], (ROWS,), ((0, 8),), -0.2, 0.2)), 0.25, 4.0).astype(jnp.bfloat16),
        "node_side": with_ends(jax.random.randint(part_keys[3], (ROWS,), 0, 2), jax.random.fold_in(part_keys[3], 1), 0, 1).astype(jnp.int32),
        "signs": with_ends(jax.random.randint(part_keys[4], (F,), -1, 2), jax.random.fold_in(part_keys[4], 1), -1, 1).astype(jnp.int32),
        "child_owner": jax.random.permutation(part_keys[5], OWN).astype(jnp.int32),
        "parent_owner": jax.random.permutation(part_keys[6], OWN).astype(jnp.int32),
        "parent_grad": bell_draw(part_keys[7], (OWN, F // OWN, BINS * K), ((ROWS // 256 + 1) ** 0.5), 48.0, ((0, 8), (1, 2)), jnp.float32),
        "parent_hess": jnp.clip(jnp.exp(math.log(516.0) - 2.7495992 * jax.random.uniform(part_keys[8], (OWN, F // OWN, BINS), jnp.float32) ** level_of(part_keys[8], (OWN, F // OWN, BINS), ((0, 8), (1, 2)), -0.2, 0.2)), 33.0, 516.0),
        "node_low": jax.random.randint(part_keys[9], (2,), -40, -4).astype(jnp.int32),
        "node_high": jax.random.randint(part_keys[10], (2,), 5, 41).astype(jnp.int32),
    }


reg_lambda = 1.0


def side_score(grad_sum, hess_sum, low, high):
    denom = jnp.maximum(hess_sum, 0.0) + reg_lambda
    weight = jnp.clip(-grad_sum / denom[..., None], low[..., None], high[..., None])
    return -jnp.mean(2.0 * grad_sum * weight + denom[..., None] * weight * weight, axis=-1)


def split_gains(grad_hist, hess_hist, sign_vec, low, high):
    left_grad = jnp.cumsum(grad_hist, axis=1)
    left_hess = jnp.cumsum(hess_hist, axis=1)
    right_grad = left_grad[:, -1:, :] - left_grad
    right_hess = left_hess[:, -1:] - left_hess
    middle = 0.5 * (low + high)
    sign_col = sign_vec[:, None]
    ones_like = jnp.ones_like(left_hess)
    low_left = jnp.where(sign_col < 0, middle, low) * ones_like
    high_left = jnp.where(sign_col > 0, middle, high) * ones_like
    low_right = jnp.where(sign_col > 0, middle, low) * ones_like
    high_right = jnp.where(sign_col < 0, middle, high) * ones_like
    return side_score(left_grad, left_hess, low_left, high_left) + side_score(right_grad, right_hess, low_right, high_right)


def reference(bins, grads, hess, node_side, signs, child_owner, parent_owner, parent_grad, parent_hess, node_low, node_high):
    inside = node_side == 1
    masked = jnp.where(inside[:, None], grads.astype(jnp.float32), jnp.float32(0.0))
    hmask = jnp.where(inside, hess.astype(jnp.float32), jnp.float32(0.0))

    def one_feature(column):
        grad_part = jax.ops.segment_sum(masked, column, num_segments=BINS)
        hess_part = jax.ops.segment_sum(hmask, column, num_segments=BINS)
        return grad_part, hess_part

    small_grad, small_hess = lax.map(one_feature, bins.T)
    by_slab = parent_grad[parent_owner].reshape(OWN, N_FEAT, FS, BINS, K)
    par_grad = jnp.transpose(by_slab, (1, 0, 2, 3, 4)).reshape(F, BINS, K)
    hess_slab = parent_hess[parent_owner].reshape(OWN, N_FEAT, FS, BINS)
    par_hess = jnp.transpose(hess_slab, (1, 0, 2, 3)).reshape(F, BINS)
    large_grad = par_grad - small_grad
    large_hess = par_hess - small_hess
    low = node_low.astype(jnp.float32) / 1024.0
    high = node_high.astype(jnp.float32) / 1024.0
    first = split_gains(small_grad, small_hess, signs, low[0], high[0])
    second = split_gains(large_grad, large_hess, signs, low[1], high[1])
    gain = jnp.stack([first, second], axis=1)
    packed = jnp.transpose(gain.reshape(N_FEAT, OWN, FS, 2, BINS), (1, 0, 2, 3, 4)).reshape(OWN, F // OWN, 2, BINS)
    return jnp.zeros_like(packed).at[child_owner].set(packed)
```

```python
import functools

import jax
import jax.numpy as jnp
from jax import lax
from jax.experimental import pallas as pl
from jax.experimental.pallas import tpu as pltpu
from jax.sharding import PartitionSpec as P

reg_lambda = 1.0
CHUNKS = 2
TILE = 256
MIB = 1024 * 1024
VMEM_SPEC = pl.BlockSpec(memory_space=pltpu.VMEM)
SMEM_SPEC = pl.BlockSpec(memory_space=pltpu.SMEM)


def plan_of(line):
    roles = []
    for z in range(line):
        mine = []
        for step in range(line - 1):
            if z <= step:
                mine.append(("R", step, line - 1 - step + z))
            if line - 1 - z <= step:
                mine.append(("L", step, step - (line - 1 - z)))
        mine.append(("F", line - 1, z))
        roles.append(mine)
    return roles


def prep_kernel(line, slab, place_ref, owner_ref, bins_ref, grads_ref, hess_ref, side_ref, own_ref, send_ref, wt_ref, wt_send_ref, perm_ref):
    f_dev = bins_ref.shape[1]
    half = f_dev // 2
    kdim = grads_ref.shape[1]

    @pl.when(pl.program_id(0) == 0)
    def _():
        z, core = place_ref[0], place_ref[1]
        column = lax.broadcasted_iota(jnp.int32, (1, f_dev), 1)
        position = lax.rem(column, half) // slab
        table = plan_of(line)
        chip = jnp.zeros_like(column)
        for p in range(line):
            target = jnp.int32(0)
            for zz in range(line):
                target = jnp.where(z == zz, jnp.int32(table[zz][p][2]), target)
            chip = jnp.where(position == p, target, chip)
        owner = 2 * chip + jnp.where(column < half, core, 1 - core)
        source = jnp.zeros_like(column)
        for q in range(2 * line):
            source = jnp.where(owner == owner_ref[q], q, source)
        source = source * slab + lax.rem(column, slab)
        rows = lax.broadcasted_iota(jnp.int32, (f_dev, f_dev), 0)
        perm_ref[...] = jnp.where(rows == source, 1.0, 0.0).astype(jnp.bfloat16)

    binned = bins_ref[...].astype(jnp.float32).astype(jnp.bfloat16)
    moved = jnp.dot(binned, perm_ref[...], preferred_element_type=jnp.float32)
    own_ref[...] = moved[:, :half].astype(jnp.bfloat16)
    send_ref[...] = moved[:, half:]
    eye_r = lax.broadcasted_iota(jnp.int32, (kdim, kdim), 0)
    eye_c = lax.broadcasted_iota(jnp.int32, (kdim, kdim), 1)
    eye = jnp.where(eye_r == eye_c, 1.0, 0.0).astype(jnp.bfloat16)
    grads_t = lax.dot_general(eye, grads_ref[...], (((1,), (1,)), ((), ())), preferred_element_type=jnp.float32)
    hess_row = jnp.broadcast_to(hess_ref[...].astype(jnp.float32), (8, hess_ref.shape[1]))
    first = lax.broadcasted_iota(jnp.int32, hess_row.shape, 0) == 0
    stacked = jnp.concatenate([grads_t, jnp.where(first, hess_row, 0.0)], axis=0)
    masked = jnp.where(side_ref[...] == 1, stacked, 0.0)
    wt_send_ref[...] = masked
    wt_ref[...] = jnp.concatenate([masked, jnp.zeros((8, masked.shape[1]), jnp.float32)], axis=0).astype(jnp.bfloat16)


def prep(line, slab, place, owners, bins, grads, hess, side):
    rows, f_dev = bins.shape
    kdim = grads.shape[1]
    block = min(rows, 512)
    half = f_dev // 2
    return pl.pallas_call(
        functools.partial(prep_kernel, line, slab),
        grid=(rows // block,),
        in_specs=[
            SMEM_SPEC,
            SMEM_SPEC,
            pl.BlockSpec((block, f_dev), lambda i: (i, 0)),
            pl.BlockSpec((block, kdim), lambda i: (i, 0)),
            pl.BlockSpec((1, block), lambda i: (0, i)),
            pl.BlockSpec((1, block), lambda i: (0, i)),
        ],
        out_specs=[
            pl.BlockSpec((block, half), lambda i: (i, 0)),
            pl.BlockSpec((block, half), lambda i: (i, 0)),
            pl.BlockSpec((kdim + 16, block), lambda i: (0, i)),
            pl.BlockSpec((kdim + 8, block), lambda i: (0, i)),
        ],
        out_shape=[
            jax.ShapeDtypeStruct((rows, half), jnp.bfloat16),
            jax.ShapeDtypeStruct((rows, half), jnp.float32),
            jax.ShapeDtypeStruct((kdim + 16, rows), jnp.bfloat16),
            jax.ShapeDtypeStruct((kdim + 8, rows), jnp.float32),
        ],
        scratch_shapes=[pltpu.VMEM((f_dev, f_dev), jnp.bfloat16)],
        compiler_params=pltpu.CompilerParams(vmem_limit_bytes=24 * MIB),
        cost_estimate=pl.CostEstimate(flops=2 * rows * f_dev * f_dev, bytes_accessed=8 * rows * f_dev, transcendentals=0),
        name="prep",
    )(place, owners, bins, grads, hess, side)


def hist_kernel(first_column, width, levels, parts, kdim, has_init, *refs):
    refs = list(refs)
    lanes = refs[-3].shape[1]
    pairs = [(refs[2 * i], refs[2 * i + 1]) for i in range(parts)]
    init_ref = refs[2 * parts] if has_init else None
    out_ref, rel_ref, wt_ref = refs[-3:]
    half = pairs[0][0].shape[1]
    rows = pairs[0][0].shape[0]
    src = lax.broadcasted_iota(jnp.int32, (half, lanes), 0)
    dst = lax.broadcasted_iota(jnp.int32, (half, lanes), 1)
    spread = jnp.where(src == first_column + lax.rem(dst, width), 1.0, 0.0).astype(jnp.bfloat16)
    lane = lax.broadcasted_iota(jnp.int32, (1, lanes), 1)
    shift = ((lane // width) * levels).astype(jnp.float32)
    for i, (bins_ref, w_ref) in enumerate(pairs):
        for r in range(0, rows, TILE):
            block = bins_ref[r : r + TILE, :].astype(jnp.bfloat16)
            moved = jnp.dot(block, spread, preferred_element_type=jnp.float32)
            rel_ref[i * rows + r : i * rows + r + TILE, :] = (moved - shift).astype(jnp.bfloat16)
        if w_ref.dtype == jnp.bfloat16:
            wt_ref[:, i * rows : (i + 1) * rows] = w_ref[...]
        else:
            part = jnp.concatenate([w_ref[...], jnp.zeros((8, rows), jnp.float32)], axis=0)
            wt_ref[:, i * rows : (i + 1) * rows] = part.astype(jnp.bfloat16)
    tiles = parts * rows // TILE
    one = jnp.ones((TILE, lanes), jnp.bfloat16)
    zero = jnp.zeros((TILE, lanes), jnp.bfloat16)

    def level(b, carry):
        value = jnp.full((TILE, lanes), b.astype(jnp.float32), jnp.float32).astype(jnp.bfloat16)
        total = jnp.zeros((wt_ref.shape[0], lanes), jnp.float32)
        for t in range(tiles):
            hit = rel_ref[t * TILE : (t + 1) * TILE, :] == value
            onehot = jnp.where(hit, one, zero)
            total = total + jnp.dot(wt_ref[:, t * TILE : (t + 1) * TILE], onehot, preferred_element_type=jnp.float32)
        start = pl.multiple_of(b * kdim, kdim)
        grad = total[:kdim, :]
        hess = total[kdim : kdim + 1, :]
        if has_init:
            grad = grad + init_ref[pl.ds(start, kdim), :]
            hess = hess + init_ref[pl.ds(levels * kdim + b, 1), :]
        out_ref[pl.ds(start, kdim), :] = grad
        out_ref[pl.ds(levels * kdim + b, 1), :] = hess
        return carry

    lax.fori_loop(0, levels, level, 0)


def hist(first_column, width, levels, lanes, kdim, pairs, init=None):
    rows = pairs[0][0].shape[0]
    parts = len(pairs)
    operands = [x for pair in pairs for x in pair]
    if init is not None:
        operands.append(init)
    height = levels * (kdim + 1)
    return pl.pallas_call(
        functools.partial(hist_kernel, first_column, width, levels, parts, kdim, init is not None),
        in_specs=[VMEM_SPEC] * len(operands),
        out_specs=VMEM_SPEC,
        out_shape=jax.ShapeDtypeStruct((height, lanes), jnp.float32),
        scratch_shapes=[
            pltpu.VMEM((parts * rows, lanes), jnp.bfloat16),
            pltpu.VMEM((kdim + 16, parts * rows), jnp.bfloat16),
        ],
        compiler_params=pltpu.CompilerParams(vmem_limit_bytes=24 * MIB),
        cost_estimate=pl.CostEstimate(
            flops=2 * 256 * parts * rows * levels * lanes, bytes_accessed=parts * rows * lanes * 4, transcendentals=0
        ),
        name="hist",
    )(*operands)


def parent_kernel(width, levels, kdim, chunks, parent_ref, *out_refs):
    lanes = out_refs[0].shape[1]
    per_tile = 128 // width
    step = 128 // kdim
    for c in range(chunks):
        for tile in range(lanes // 128):
            for b in range(0, levels, step):
                rows = []
                for jj in range(per_tile):
                    bin_at = (tile * per_tile + jj) * levels + b
                    rows.append(parent_ref[c * width : (c + 1) * width, bin_at * kdim : bin_at * kdim + 128])
                block = jnp.concatenate(rows, axis=0) if per_tile > 1 else rows[0]
                out_refs[c][b * kdim : b * kdim + 128, tile * 128 : (tile + 1) * 128] = block.T


def parent_layout(width, levels, lanes, kdim, chunks, parent):
    shape = jax.ShapeDtypeStruct((levels * kdim, lanes), jnp.float32)
    return pl.pallas_call(
        functools.partial(parent_kernel, width, levels, kdim, chunks),
        in_specs=[VMEM_SPEC],
        out_specs=[VMEM_SPEC] * chunks,
        out_shape=[shape] * chunks,
        compiler_params=pltpu.CompilerParams(vmem_limit_bytes=16 * MIB),
        cost_estimate=pl.CostEstimate(flops=0, bytes_accessed=2 * parent.size * 4, transcendentals=0),
        name="parent_layout",
    )(parent)


def lane_prefix(total, width):
    lanes = total.shape[1]
    lane = lax.broadcasted_iota(jnp.int32, total.shape, 1)
    running = total
    reach = width
    while reach < lanes:
        running = running + jnp.where(lane >= reach, pltpu.roll(running, reach, 1), 0.0)
        reach *= 2
    whole = total
    reach = width
    while reach < lanes:
        whole = whole + pltpu.roll(whole, reach, 1)
        reach *= 2
    return running - total, running, whole


def gain_kernel(width, levels, kdim, last_ref, right_ref, left_ref, par_grad_ref, par_hess_ref, sign_ref, bound_ref, out_ref, grad_ref, hess_ref):
    hess_at = levels * kdim
    lanes = out_ref.shape[2]

    def small_at(start, size):
        return last_ref[pl.ds(start, size), :] + right_ref[pl.ds(start, size), :] + left_ref[pl.ds(start, size), :]

    sign = sign_ref[...]
    small_hess = small_at(hess_at, levels)
    hess_ref[0] = small_hess
    hess_ref[1] = par_hess_ref[...] - small_hess

    def add_up(b, carry):
        g0, g1, h0, h1 = carry
        start = pl.multiple_of(b * kdim, kdim)
        small = small_at(start, kdim)
        g0 = g0 + small
        g1 = g1 + (par_grad_ref[pl.ds(start, kdim), :] - small)
        h0 = h0 + hess_ref[0, pl.ds(b, 1), :]
        h1 = h1 + hess_ref[1, pl.ds(b, 1), :]
        grad_ref[0, pl.ds(start, kdim), :] = g0
        grad_ref[1, pl.ds(start, kdim), :] = g1
        hess_ref[0, pl.ds(b, 1), :] = h0
        hess_ref[1, pl.ds(b, 1), :] = h1
        return g0, g1, h0, h1

    zero_g = jnp.zeros((kdim, lanes), jnp.float32)
    zero_h = jnp.zeros((1, lanes), jnp.float32)
    ends = lax.fori_loop(0, levels, add_up, (zero_g, zero_g, zero_h, zero_h))
    for c in range(2):
        low = bound_ref[0, c].astype(jnp.float32) / 1024.0
        high = bound_ref[1, c].astype(jnp.float32) / 1024.0
        middle = 0.5 * (low + high)
        low_left = jnp.where(sign < 0, middle, low)
        high_left = jnp.where(sign > 0, middle, high)
        low_right = jnp.where(sign > 0, middle, low)
        high_right = jnp.where(sign < 0, middle, high)
        grad_before, _, grad_all = lane_prefix(ends[c], width)
        hess_rows = jnp.broadcast_to(ends[2 + c], (8, lanes))
        hess_before, _, hess_all = lane_prefix(hess_rows, width)
        hess_before, hess_all = hess_before[:1], hess_all[:1]

        def score(grad, hess, lower, upper):
            denom = jnp.maximum(hess, 0.0) + reg_lambda
            weight = jnp.clip(-grad / denom, lower, upper)
            return jnp.sum((2.0 * grad + denom * weight) * weight, axis=0, keepdims=True)

        def one_bin(b, carry):
            start = pl.multiple_of(b * kdim, kdim)
            grad_left = grad_ref[c, pl.ds(start, kdim), :] + grad_before
            hess_left = hess_ref[c, pl.ds(b, 1), :] + hess_before
            left = score(grad_left, hess_left, low_left, high_left)
            right = score(grad_all - grad_left, hess_all - hess_left, low_right, high_right)
            out_ref[c, pl.ds(b, 1), :] = (left + right) * (-1.0 / kdim)
            return carry

        lax.fori_loop(0, levels, one_bin, 0)


def gains_of(width, levels, lanes, kdim, last, right, left, par_grad, par_hess, sign, bounds):
    return pl.pallas_call(
        functools.partial(gain_kernel, width, levels, kdim),
        in_specs=[VMEM_SPEC] * 6 + [SMEM_SPEC],
        out_specs=VMEM_SPEC,
        out_shape=jax.ShapeDtypeStruct((2, levels, lanes), jnp.float32),
        scratch_shapes=[
            pltpu.VMEM((2, levels * kdim, lanes), jnp.float32),
            pltpu.VMEM((2, levels, lanes), jnp.float32),
        ],
        compiler_params=pltpu.CompilerParams(vmem_limit_bytes=24 * MIB),
        cost_estimate=pl.CostEstimate(flops=50 * levels * kdim * lanes, bytes_accessed=16 * levels * kdim * lanes, transcendentals=0),
        name="gains",
    )(last, right, left, par_grad, par_hess, sign, bounds)


def inverse_of(owner, slots):
    return jnp.sum(jnp.where(owner[None, :] == slots[:, None], slots[None, :], 0), axis=1)


def one_of(z, members):
    hit = z == members[0]
    for m in members[1:]:
        hit = hit | (z == m)
    return hit


def per_device(bins, grads, hess, node_side, signs, child_owner, parent_owner, parent_grad, parent_hess, node_low, node_high):
    line = lax.axis_size("dp")
    owners = line * lax.axis_size("sub")
    z = lax.axis_index("dp")
    core = lax.axis_index("sub")
    place = lax.axis_index(("dp", "sub"))
    column = lax.axis_index("feat")
    rows, f_dev = bins.shape
    kdim = grads.shape[1]
    nbins = parent_hess.shape[2]
    slab = parent_grad.shape[1]
    chunks = CHUNKS if slab >= 32 else 1
    width = slab // chunks
    lanes = min(256, width * nbins * kdim // 128)
    groups = lanes // width
    levels = nbins // groups
    plan = plan_of(line)

    where = jnp.stack([z, core]).astype(jnp.int32)
    own, send, wt, wt_send = prep(
        line, slab, where, parent_owner, bins, grads, hess.reshape(1, rows), node_side.reshape(1, rows)
    )
    swap = [(0, 1), (1, 0)]
    other = lax.ppermute(send, "sub", swap)
    wt_other = lax.ppermute(wt_send, "sub", swap)

    units = {}
    for c in range(chunks):
        units[0, c] = hist(c * width, width, levels, lanes, kdim, [(own, wt)])
    for c in range(chunks):
        units[0, c] = hist(c * width, width, levels, lanes, kdim, [(other, wt_other)], units[0, c])

    def pick(kind, step, c):
        where_at = {}
        for zz in range(line):
            for p, role in enumerate(plan[zz]):
                if role[:2] == (kind, step):
                    where_at.setdefault(p, []).append(zz)
        spots = sorted(where_at)
        value = units[spots[0], c]
        for p in spots[1:]:
            value = jnp.where(one_of(z, where_at[p]), units[p, c], value)
        return value

    slots = jnp.arange(owners, dtype=jnp.int32)
    parent_inv = inverse_of(parent_owner, slots)
    my_slab = parent_inv[place]
    ids = column * f_dev + my_slab * slab
    my_signs = lax.dynamic_slice(signs, (ids,), (slab,)).reshape(chunks, 1, width)
    my_signs = jnp.tile(my_signs, (1, 1, groups))
    bounds = jnp.stack([node_low, node_high])
    par_hess = jnp.transpose(parent_hess[0].reshape(chunks, width, groups, levels), (0, 3, 2, 1)).reshape(chunks, levels, lanes)
    par_grad = parent_layout(width, levels, lanes, kdim, chunks, parent_grad[0])

    from_left = [None] * chunks
    from_right = [None] * chunks
    for step in range(line - 1):
        if step > 0:
            for c in range(chunks):
                units[step, c] = hist(step * slab + c * width, width, levels, lanes, kdim, [(own, wt), (other, wt_other)])
        for c in range(chunks):
            to_right = pick("R", step, c)
            to_left = pick("L", step, c)
            if step > 0:
                to_right = to_right + from_left[c]
                to_left = to_left + from_right[c]
            from_left[c] = lax.ppermute(to_right, "dp", [(i, i + 1) for i in range(step + 1)])
            from_right[c] = lax.ppermute(to_left, "dp", [(line - 1 - i, line - 2 - i) for i in range(step + 1)])
    last = line - 1
    for c in range(chunks):
        units[last, c] = hist(last * slab + c * width, width, levels, lanes, kdim, [(own, wt), (other, wt_other)])

    child_inv = inverse_of(child_owner, slots)
    source_of = jnp.sum(jnp.where(child_inv[:, None] == slots[None, :], parent_owner[None, :], 0), axis=1)
    pair = 2 * z
    my_source = source_of[place]
    twin_source = source_of[pair + 1 - core]
    done = []
    for c in range(chunks):
        gain = gains_of(width, levels, lanes, kdim, units[last, c], from_left[c], from_right[c], par_grad[c], par_hess[c], my_signs[c], bounds)
        got = [gain] + [lax.ppermute(gain, "dp", [(i, (i + s) % line) for i in range(line)]) for s in range(1, line)]

        def choose(source):
            chip = source // 2
            value = got[0]
            for s in range(1, line):
                value = jnp.where(lax.rem(z - chip + line, line) == s, got[s], value)
            return value

        crossed = lax.ppermute(choose(twin_source), "sub", swap)
        gain = jnp.where(lax.rem(my_source, 2) == core, choose(my_source), crossed)
        gain = jnp.transpose(gain.reshape(2, levels, groups, width), (3, 0, 2, 1))
        done.append(gain.reshape(width, 2, nbins))
    return jnp.concatenate(done, axis=0)[None]


def solution(mesh):
    return jax.shard_map(
        per_device,
        mesh=mesh,
        in_specs=(
            P(("groups", "dp", "sub"), "feat"),
            P(("groups", "dp", "sub"), None),
            P(("groups", "dp", "sub")),
            P(("groups", "dp", "sub")),
            P("groups"),
            P("groups"),
            P("groups"),
            P(("groups", "dp", "sub"), "feat", None),
            P(("groups", "dp", "sub"), "feat", None),
            P("groups"),
            P("groups"),
        ),
        out_specs=P(("groups", "dp", "sub"), "feat", None, None),
        check_vma=False,
    )
```

```python
import functools

import jax
import jax.numpy as jnp
from jax import lax
from jax.experimental import pallas as pl
from jax.experimental.pallas import tpu as pltpu
from jax.sharding import PartitionSpec as P

reg_lambda = 1.0
CHUNKS = 2
LOW_SCALE = 16.0
F8 = jnp.float8_e4m3fn
TILE = 256
MIB = 1024 * 1024
VMEM_SPEC = pl.BlockSpec(memory_space=pltpu.VMEM)
SMEM_SPEC = pl.BlockSpec(memory_space=pltpu.SMEM)


def plan_of(line):
    roles = []
    for z in range(line):
        mine = []
        for step in range(line - 1):
            if z <= step:
                mine.append(("R", step, line - 1 - step + z))
            if line - 1 - z <= step:
                mine.append(("L", step, step - (line - 1 - z)))
        mine.append(("F", line - 1, z))
        roles.append(mine)
    return roles


def prep_kernel(line, slab, place_ref, owner_ref, bins_ref, grads_ref, hess_ref, side_ref, own_ref, send_ref, wt_ref, undo_ref, wt_send_ref, perm_ref):
    f_dev = bins_ref.shape[1]
    half = f_dev // 2
    kdim = grads_ref.shape[1]

    @pl.when(pl.program_id(0) == 0)
    def _():
        z, core = place_ref[0], place_ref[1]
        column = lax.broadcasted_iota(jnp.int32, (1, f_dev), 1)
        position = lax.rem(column, half) // slab
        table = plan_of(line)
        chip = jnp.zeros_like(column)
        for p in range(line):
            target = jnp.int32(0)
            for zz in range(line):
                target = jnp.where(z == zz, jnp.int32(table[zz][p][2]), target)
            chip = jnp.where(position == p, target, chip)
        owner = 2 * chip + jnp.where(column < half, core, 1 - core)
        source = jnp.zeros_like(column)
        for q in range(2 * line):
            source = jnp.where(owner == owner_ref[q], q, source)
        source = source * slab + lax.rem(column, slab)
        rows = lax.broadcasted_iota(jnp.int32, (f_dev, f_dev), 0)
        perm_ref[...] = jnp.where(rows == source, 1.0, 0.0).astype(jnp.bfloat16)

        eye_r = lax.broadcasted_iota(jnp.int32, (kdim, kdim), 0)
        eye_c = lax.broadcasted_iota(jnp.int32, (kdim, kdim), 1)
        eye = jnp.where(eye_r == eye_c, 1.0, 0.0).astype(jnp.bfloat16)
        grads_t = lax.dot_general(eye, grads_ref[...], (((1,), (1,)), ((), ())), preferred_element_type=jnp.float32)
        hess_row = jnp.broadcast_to(hess_ref[...].astype(jnp.float32), (8, hess_ref.shape[1]))
        first = lax.broadcasted_iota(jnp.int32, hess_row.shape, 0) == 0
        stacked = jnp.concatenate([grads_t, jnp.where(first, hess_row, 0.0)], axis=0)
        masked = jnp.where(side_ref[...] == 1, stacked, 0.0)
        wt_send_ref[...] = masked
        wt_ref[...], undo_ref[...] = split_weights(masked)

    binned = bins_ref[...].astype(jnp.float32).astype(jnp.bfloat16)
    moved = jnp.dot(binned, perm_ref[...], preferred_element_type=jnp.float32)
    own_ref[...] = moved[:, :half].astype(jnp.bfloat16)
    send_ref[...] = moved[:, half:]


def split_weights(masked):
    kdim = masked.shape[0] - 8
    largest = jnp.max(jnp.abs(masked), axis=1, keepdims=True)
    scale = jnp.full(largest.shape, 32.0, jnp.float32)
    undo = jnp.full(largest.shape, 1.0 / 32.0, jnp.float32)
    for e in (32, 16, 8, 4, 2, 1):
        fits = largest * (scale * 2.0**e) < 256.0
        scale = jnp.where(fits, scale * 2.0**e, scale)
        undo = jnp.where(fits, undo * 2.0**-e, undo)
    scaled = masked * scale
    high = scaled.astype(F8).astype(jnp.float32)
    low = (scaled - high) * LOW_SCALE
    rest = jnp.zeros((16, masked.shape[1]), jnp.float32)
    parts = jnp.concatenate([high[:kdim], low[:kdim], high[kdim:], low[kdim:], rest], axis=0)
    return parts.astype(F8), jnp.broadcast_to(undo, (kdim + 8, 128))


def split_kernel(masked_ref, wt_ref, undo_ref):
    wt_ref[...], undo_ref[...] = split_weights(masked_ref[...])


def split(masked):
    height, rows = masked.shape
    return pl.pallas_call(
        split_kernel,
        in_specs=[VMEM_SPEC],
        out_specs=[VMEM_SPEC] * 2,
        out_shape=[jax.ShapeDtypeStruct((2 * height + 16, rows), F8), jax.ShapeDtypeStruct((height, 128), jnp.float32)],
        cost_estimate=pl.CostEstimate(flops=20 * height * rows, bytes_accessed=6 * height * rows, transcendentals=0),
        name="split",
    )(masked)


def prep(line, slab, place, owners, bins, grads, hess, side):
    rows, f_dev = bins.shape
    kdim = grads.shape[1]
    block = min(rows, 512)
    half = f_dev // 2
    return pl.pallas_call(
        functools.partial(prep_kernel, line, slab),
        grid=(rows // block,),
        in_specs=[
            SMEM_SPEC,
            SMEM_SPEC,
            pl.BlockSpec((block, f_dev), lambda i: (i, 0)),
            pl.BlockSpec((rows, kdim), lambda i: (0, 0)),
            pl.BlockSpec((1, rows), lambda i: (0, 0)),
            pl.BlockSpec((1, rows), lambda i: (0, 0)),
        ],
        out_specs=[
            pl.BlockSpec((block, half), lambda i: (i, 0)),
            pl.BlockSpec((block, half), lambda i: (i, 0)),
            pl.BlockSpec((2 * kdim + 32, rows), lambda i: (0, 0)),
            pl.BlockSpec((kdim + 8, 128), lambda i: (0, 0)),
            pl.BlockSpec((kdim + 8, rows), lambda i: (0, 0)),
        ],
        out_shape=[
            jax.ShapeDtypeStruct((rows, half), jnp.bfloat16),
            jax.ShapeDtypeStruct((rows, half), jnp.float32),
            jax.ShapeDtypeStruct((2 * kdim + 32, rows), F8),
            jax.ShapeDtypeStruct((kdim + 8, 128), jnp.float32),
            jax.ShapeDtypeStruct((kdim + 8, rows), jnp.float32),
        ],
        scratch_shapes=[pltpu.VMEM((f_dev, f_dev), jnp.bfloat16)],
        compiler_params=pltpu.CompilerParams(vmem_limit_bytes=56 * MIB),
        cost_estimate=pl.CostEstimate(flops=2 * rows * f_dev * f_dev, bytes_accessed=8 * rows * f_dev, transcendentals=0),
        name="prep",
    )(place, owners, bins, grads, hess, side)


def hist_kernel(first_column, width, levels, parts, kdim, has_init, *refs):
    parts_in = [refs[3 * i : 3 * i + 3] for i in range(parts)]
    init_ref = refs[3 * parts] if has_init else None
    out_ref, rel_ref = refs[-2:]
    lanes = out_ref.shape[1]
    rows, half = parts_in[0][0].shape
    src = lax.broadcasted_iota(jnp.int32, (half, lanes), 0)
    dst = lax.broadcasted_iota(jnp.int32, (half, lanes), 1)
    spread = jnp.where(src == first_column + lax.rem(dst, width), 1.0, 0.0).astype(jnp.bfloat16)
    lane = lax.broadcasted_iota(jnp.int32, (1, lanes), 1)
    shift = ((lane // width) * levels).astype(jnp.float32)
    for i, (bins_ref, _, _) in enumerate(parts_in):
        for r in range(0, rows, TILE):
            block = bins_ref[r : r + TILE, :].astype(jnp.bfloat16)
            moved = jnp.dot(block, spread, preferred_element_type=jnp.float32)
            rel_ref[i * rows + r : i * rows + r + TILE, :] = (moved - shift).astype(jnp.bfloat16)
    one = jnp.ones((TILE, lanes), jnp.bfloat16)
    zero = jnp.zeros((TILE, lanes), jnp.bfloat16)

    def level(b, carry):
        value = jnp.full((TILE, lanes), b.astype(jnp.float32), jnp.float32).astype(jnp.bfloat16)
        start = pl.multiple_of(b * kdim, kdim)
        hess_at = levels * kdim + b
        if has_init:
            grad, hess = init_ref[pl.ds(start, kdim), :], init_ref[pl.ds(hess_at, 1), :]
        else:
            grad, hess = jnp.zeros((kdim, lanes), jnp.float32), jnp.zeros((1, lanes), jnp.float32)
        for i, (_, wt_ref, undo_ref) in enumerate(parts_in):
            total = jnp.zeros((wt_ref.shape[0], lanes), jnp.float32)
            for r in range(0, rows, TILE):
                hit = rel_ref[i * rows + r : i * rows + r + TILE, :] == value
                onehot = jnp.where(hit, one, zero).astype(F8)
                total = total + jnp.dot(wt_ref[:, r : r + TILE], onehot, preferred_element_type=jnp.float32)
            grad_part = total[:kdim] + total[kdim : 2 * kdim] * (1.0 / LOW_SCALE)
            hess_part = total[2 * kdim : 2 * kdim + 1] + total[2 * kdim + 8 : 2 * kdim + 9] * (1.0 / LOW_SCALE)
            grad = grad + grad_part * undo_ref[:kdim, :1]
            hess = hess + hess_part * undo_ref[kdim : kdim + 1, :1]
        out_ref[pl.ds(start, kdim), :] = grad
        out_ref[pl.ds(hess_at, 1), :] = hess
        return carry

    lax.fori_loop(0, levels, level, 0)


def hist(first_column, width, levels, lanes, kdim, pairs, init=None):
    rows = pairs[0][0].shape[0]
    parts = len(pairs)
    operands = [x for pair in pairs for x in pair]
    if init is not None:
        operands.append(init)
    height = levels * (kdim + 1)
    return pl.pallas_call(
        functools.partial(hist_kernel, first_column, width, levels, parts, kdim, init is not None),
        in_specs=[VMEM_SPEC] * len(operands),
        out_specs=VMEM_SPEC,
        out_shape=jax.ShapeDtypeStruct((height, lanes), jnp.float32),
        scratch_shapes=[pltpu.VMEM((parts * rows, lanes), jnp.bfloat16)],
        compiler_params=pltpu.CompilerParams(vmem_limit_bytes=24 * MIB),
        cost_estimate=pl.CostEstimate(
            flops=2 * 256 * parts * rows * levels * lanes, bytes_accessed=parts * rows * lanes * 4, transcendentals=0
        ),
        name="hist",
    )(*operands)


def parent_kernel(width, levels, kdim, chunks, parent_ref, *out_refs):
    lanes = out_refs[0].shape[1]
    per_tile = 128 // width
    step = 128 // kdim
    for c in range(chunks):
        for tile in range(lanes // 128):
            for b in range(0, levels, step):
                rows = []
                for jj in range(per_tile):
                    bin_at = (tile * per_tile + jj) * levels + b
                    rows.append(parent_ref[c * width : (c + 1) * width, bin_at * kdim : bin_at * kdim + 128])
                block = jnp.concatenate(rows, axis=0) if per_tile > 1 else rows[0]
                out_refs[c][b * kdim : b * kdim + 128, tile * 128 : (tile + 1) * 128] = block.T


def parent_layout(width, levels, lanes, kdim, chunks, parent):
    shape = jax.ShapeDtypeStruct((levels * kdim, lanes), jnp.float32)
    return pl.pallas_call(
        functools.partial(parent_kernel, width, levels, kdim, chunks),
        in_specs=[VMEM_SPEC],
        out_specs=[VMEM_SPEC] * chunks,
        out_shape=[shape] * chunks,
        compiler_params=pltpu.CompilerParams(vmem_limit_bytes=16 * MIB),
        cost_estimate=pl.CostEstimate(flops=0, bytes_accessed=2 * parent.size * 4, transcendentals=0),
        name="parent_layout",
    )(parent)


def lane_prefix(total, width):
    lanes = total.shape[1]
    lane = lax.broadcasted_iota(jnp.int32, total.shape, 1)
    running = total
    reach = width
    while reach < lanes:
        running = running + jnp.where(lane >= reach, pltpu.roll(running, reach, 1), 0.0)
        reach *= 2
    whole = total
    reach = width
    while reach < lanes:
        whole = whole + pltpu.roll(whole, reach, 1)
        reach *= 2
    return running - total, running, whole


def gain_kernel(width, levels, kdim, last_ref, right_ref, left_ref, par_grad_ref, par_hess_ref, sign_ref, bound_ref, out_ref, grad_ref, hess_ref):
    hess_at = levels * kdim
    lanes = out_ref.shape[2]

    def small_at(start, size):
        return last_ref[pl.ds(start, size), :] + right_ref[pl.ds(start, size), :] + left_ref[pl.ds(start, size), :]

    sign = sign_ref[...]
    small_hess = small_at(hess_at, levels)
    hess_ref[0] = small_hess
    hess_ref[1] = par_hess_ref[...] - small_hess

    def add_up(b, carry):
        g0, g1, h0, h1 = carry
        start = pl.multiple_of(b * kdim, kdim)
        small = small_at(start, kdim)
        g0 = g0 + small
        g1 = g1 + (par_grad_ref[pl.ds(start, kdim), :] - small)
        h0 = h0 + hess_ref[0, pl.ds(b, 1), :]
        h1 = h1 + hess_ref[1, pl.ds(b, 1), :]
        grad_ref[0, pl.ds(start, kdim), :] = g0
        grad_ref[1, pl.ds(start, kdim), :] = g1
        hess_ref[0, pl.ds(b, 1), :] = h0
        hess_ref[1, pl.ds(b, 1), :] = h1
        return g0, g1, h0, h1

    zero_g = jnp.zeros((kdim, lanes), jnp.float32)
    zero_h = jnp.zeros((1, lanes), jnp.float32)
    ends = lax.fori_loop(0, levels, add_up, (zero_g, zero_g, zero_h, zero_h))
    for c in range(2):
        low = bound_ref[0, c].astype(jnp.float32) / 1024.0
        high = bound_ref[1, c].astype(jnp.float32) / 1024.0
        middle = 0.5 * (low + high)
        low_left = jnp.where(sign < 0, middle, low)
        high_left = jnp.where(sign > 0, middle, high)
        low_right = jnp.where(sign > 0, middle, low)
        high_right = jnp.where(sign < 0, middle, high)
        grad_before, _, grad_all = lane_prefix(ends[c], width)
        hess_rows = jnp.broadcast_to(ends[2 + c], (8, lanes))
        hess_before, _, hess_all = lane_prefix(hess_rows, width)
        hess_before, hess_all = hess_before[:1], hess_all[:1]

        def score(grad, hess, lower, upper):
            denom = jnp.maximum(hess, 0.0) + reg_lambda
            weight = jnp.clip(-grad / denom, lower, upper)
            return jnp.sum((2.0 * grad + denom * weight) * weight, axis=0, keepdims=True)

        def one_bin(b, carry):
            start = pl.multiple_of(b * kdim, kdim)
            grad_left = grad_ref[c, pl.ds(start, kdim), :] + grad_before
            hess_left = hess_ref[c, pl.ds(b, 1), :] + hess_before
            left = score(grad_left, hess_left, low_left, high_left)
            right = score(grad_all - grad_left, hess_all - hess_left, low_right, high_right)
            out_ref[c, pl.ds(b, 1), :] = (left + right) * (-1.0 / kdim)
            return carry

        lax.fori_loop(0, levels, one_bin, 0)


def gains_of(width, levels, lanes, kdim, last, right, left, par_grad, par_hess, sign, bounds):
    return pl.pallas_call(
        functools.partial(gain_kernel, width, levels, kdim),
        in_specs=[VMEM_SPEC] * 6 + [SMEM_SPEC],
        out_specs=VMEM_SPEC,
        out_shape=jax.ShapeDtypeStruct((2, levels, lanes), jnp.float32),
        scratch_shapes=[
            pltpu.VMEM((2, levels * kdim, lanes), jnp.float32),
            pltpu.VMEM((2, levels, lanes), jnp.float32),
        ],
        compiler_params=pltpu.CompilerParams(vmem_limit_bytes=24 * MIB),
        cost_estimate=pl.CostEstimate(flops=50 * levels * kdim * lanes, bytes_accessed=16 * levels * kdim * lanes, transcendentals=0),
        name="gains",
    )(last, right, left, par_grad, par_hess, sign, bounds)


def inverse_of(owner, slots):
    return jnp.sum(jnp.where(owner[None, :] == slots[:, None], slots[None, :], 0), axis=1)


def one_of(z, members):
    hit = z == members[0]
    for m in members[1:]:
        hit = hit | (z == m)
    return hit


def per_device(bins, grads, hess, node_side, signs, child_owner, parent_owner, parent_grad, parent_hess, node_low, node_high):
    line = lax.axis_size("dp")
    owners = line * lax.axis_size("sub")
    z = lax.axis_index("dp")
    core = lax.axis_index("sub")
    place = lax.axis_index(("dp", "sub"))
    column = lax.axis_index("feat")
    rows, f_dev = bins.shape
    kdim = grads.shape[1]
    nbins = parent_hess.shape[2]
    slab = parent_grad.shape[1]
    chunks = CHUNKS if slab >= 32 else 1
    width = slab // chunks
    lanes = min(256, width * nbins * kdim // 128)
    groups = lanes // width
    levels = nbins // groups
    plan = plan_of(line)

    where = jnp.stack([z, core]).astype(jnp.int32)
    own, send, wt, undo, wt_send = prep(
        line, slab, where, parent_owner, bins, grads, hess.reshape(1, rows), node_side.reshape(1, rows)
    )
    swap = [(0, 1), (1, 0)]
    wt_other = lax.ppermute(wt_send, "sub", swap)
    other = lax.ppermute(send, "sub", swap)
    mine = (own, wt, undo)
    theirs = (other, *split(wt_other))

    units = {}
    for c in range(chunks):
        units[0, c] = hist(c * width, width, levels, lanes, kdim, [mine])
    for c in range(chunks):
        units[0, c] = hist(c * width, width, levels, lanes, kdim, [theirs], units[0, c])

    def pick(kind, step, c):
        where_at = {}
        for zz in range(line):
            for p, role in enumerate(plan[zz]):
                if role[:2] == (kind, step):
                    where_at.setdefault(p, []).append(zz)
        spots = sorted(where_at)
        value = units[spots[0], c]
        for p in spots[1:]:
            value = jnp.where(one_of(z, where_at[p]), units[p, c], value)
        return value

    from_left = [None] * chunks
    from_right = [None] * chunks
    arrived = {}

    def after(step, c):
        if (step, c) not in arrived:
            return [mine, theirs]
        held, _ = lax.optimization_barrier((own, arrived[step, c]))
        return [(held, wt, undo), theirs]

    for step in range(line - 1):
        if step > 0:
            for c in range(chunks):
                units[step, c] = hist(step * slab + c * width, width, levels, lanes, kdim, after(step - 2, c))
        for c in range(chunks):
            to_right = pick("R", step, c)
            to_left = pick("L", step, c)
            if step > 0:
                to_right = to_right + from_left[c]
                to_left = to_left + from_right[c]
            from_left[c] = lax.ppermute(to_right, "dp", [(i, i + 1) for i in range(step + 1)])
            from_right[c] = lax.ppermute(to_left, "dp", [(line - 1 - i, line - 2 - i) for i in range(step + 1)])
            arrived[step, c] = from_left[c]
    last = line - 1
    for c in range(chunks):
        units[last, c] = hist(last * slab + c * width, width, levels, lanes, kdim, after(last - 2, c))

    signs, child_owner, parent_owner, node_low, node_high, parent_grad, parent_hess, _ = lax.optimization_barrier(
        (signs, child_owner, parent_owner, node_low, node_high, parent_grad, parent_hess, arrived[max(line - 3, 0), 0])
    )
    slots = jnp.arange(owners, dtype=jnp.int32)
    parent_inv = inverse_of(parent_owner, slots)
    my_slab = parent_inv[place]
    ids = column * f_dev + my_slab * slab
    my_signs = lax.dynamic_slice(signs, (ids,), (slab,)).reshape(chunks, 1, width)
    my_signs = jnp.tile(my_signs, (1, 1, groups))
    bounds = jnp.stack([node_low, node_high])
    par_hess = jnp.transpose(parent_hess[0].reshape(chunks, width, groups, levels), (0, 3, 2, 1)).reshape(chunks, levels, lanes)
    par_grad = parent_layout(width, levels, lanes, kdim, chunks, parent_grad[0])

    child_inv = inverse_of(child_owner, slots)
    source_of = jnp.sum(jnp.where(child_inv[:, None] == slots[None, :], parent_owner[None, :], 0), axis=1)
    pair = 2 * z
    my_source = source_of[place]
    twin_source = source_of[pair + 1 - core]
    done = []
    for c in range(chunks):
        gain = gains_of(width, levels, lanes, kdim, units[last, c], from_left[c], from_right[c], par_grad[c], par_hess[c], my_signs[c], bounds)
        got = [gain] + [lax.ppermute(gain, "dp", [(i, (i + s) % line) for i in range(line)]) for s in range(1, line)]

        def choose(source):
            chip = source // 2
            value = got[0]
            for s in range(1, line):
                value = jnp.where(lax.rem(z - chip + line, line) == s, got[s], value)
            return value

        crossed = lax.ppermute(choose(twin_source), "sub", swap)
        gain = jnp.where(lax.rem(my_source, 2) == core, choose(my_source), crossed)
        gain = jnp.transpose(gain.reshape(2, levels, groups, width), (3, 0, 2, 1))
        done.append(gain.reshape(width, 2, nbins))
    return jnp.concatenate(done, axis=0)[None]


def solution(mesh):
    return jax.shard_map(
        per_device,
        mesh=mesh,
        in_specs=(
            P(("groups", "dp", "sub"), "feat"),
            P(("groups", "dp", "sub"), None),
            P(("groups", "dp", "sub")),
            P(("groups", "dp", "sub")),
            P("groups"),
            P("groups"),
            P("groups"),
            P(("groups", "dp", "sub"), "feat", None),
            P(("groups", "dp", "sub"), "feat", None),
            P("groups"),
            P("groups"),
        ),
        out_specs=P(("groups", "dp", "sub"), "feat", None, None),
        check_vma=False,
    )
```

```python
import functools

import jax
import jax.numpy as jnp
from jax import lax
from jax.experimental import pallas as pl
from jax.experimental.pallas import tpu as pltpu
from jax.sharding import PartitionSpec as P

reg_lambda = 1.0
CHUNKS = 2
TILE = 256
PACK = 128
MIB = 1024 * 1024
VMEM_SPEC = pl.BlockSpec(memory_space=pltpu.VMEM)
SMEM_SPEC = pl.BlockSpec(memory_space=pltpu.SMEM)


def plan_of(line):
    roles = []
    for z in range(line):
        mine = []
        for step in range(line - 1):
            if z <= step:
                mine.append(("R", step, line - 1 - step + z))
            if line - 1 - z <= step:
                mine.append(("L", step, step - (line - 1 - z)))
        mine.append(("F", line - 1, z))
        roles.append(mine)
    return roles


def prep_kernel(line, slab, owner_ref, bins_ref, grads_ref, hess_ref, side_ref, own_ref, send_ref, wt_ref, wt_send_ref, buf_ref, sems, acc_ref, acc_w_ref):
    rows, f_dev = bins_ref.shape
    half = f_dev // 2
    kdim = grads_ref.shape[0]
    reach = TILE + PACK
    copies = []
    for i in range(rows // TILE):
        part = pl.ds(i * TILE, TILE)
        copies.append(pltpu.make_async_copy(bins_ref.at[part, :], buf_ref.at[part, :], sems.at[i]))
        copies[-1].start()

    z, core = lax.axis_index("dp"), lax.axis_index("sub")
    column = lax.broadcasted_iota(jnp.int32, (1, f_dev), 1)
    position = lax.rem(column, half) // slab
    table = plan_of(line)
    chip = jnp.zeros_like(column)
    for p in range(line):
        target = jnp.int32(0)
        for zz in range(line):
            target = jnp.where(z == zz, jnp.int32(table[zz][p][2]), target)
        chip = jnp.where(position == p, target, chip)
    owner = 2 * chip + jnp.where(column < half, core, 1 - core)
    source = jnp.zeros_like(column)
    for q in range(2 * line):
        source = jnp.where(owner == owner_ref[q], q, source)
    source = source * slab + lax.rem(column, slab)
    perm = jnp.where(lax.broadcasted_iota(jnp.int32, (f_dev, f_dev), 0) == source, 1.0, 0.0).astype(jnp.bfloat16)

    before = lax.broadcasted_iota(jnp.int32, (TILE, TILE), 0) < lax.broadcasted_iota(jnp.int32, (TILE, TILE), 1)
    before = jnp.where(before, 1.0, 0.0).astype(jnp.bfloat16)
    slot = lax.broadcasted_iota(jnp.int32, (reach, TILE), 0)
    acc_ref[...] = jnp.zeros_like(acc_ref)
    acc_w_ref[...] = jnp.zeros_like(acc_w_ref)
    base = jnp.int32(0)
    for i in range(rows // TILE):
        part = slice(i * TILE, (i + 1) * TILE)
        chosen = side_ref[:, part] == 1
        ones = jnp.where(chosen, 1.0, 0.0)
        ahead = jnp.dot(jnp.broadcast_to(ones, (8, TILE)).astype(jnp.bfloat16), before, preferred_element_type=jnp.float32)[:1]
        start = pl.multiple_of((base // PACK) * PACK, PACK)
        goal = jnp.where(chosen, ahead.astype(jnp.int32) + (base - start), -1)
        pack = jnp.where(slot == goal, 1.0, 0.0).astype(jnp.bfloat16)
        base = base + jnp.sum(ones).astype(jnp.int32)
        hess = jnp.broadcast_to(hess_ref[:, part], (16, TILE))
        first = lax.broadcasted_iota(jnp.int32, hess.shape, 0) == 0
        weights = jnp.concatenate([grads_ref[:, part].astype(jnp.float32), jnp.where(first, hess, 0.0)], axis=0)
        packed_w = lax.dot_general(weights.astype(jnp.bfloat16), pack, (((1,), (1,)), ((), ())), preferred_element_type=jnp.float32)
        acc_w_ref[:, pl.ds(start, reach)] += packed_w
        copies[i].wait()
        binned = buf_ref[part, :].astype(jnp.float32).astype(jnp.bfloat16)
        acc_ref[pl.ds(start, reach), :] += jnp.dot(pack, binned, preferred_element_type=jnp.float32)

    def move(t, carry):
        part = pl.ds(pl.multiple_of(t * TILE, TILE), TILE)
        moved = jnp.dot(acc_ref[part, :].astype(jnp.bfloat16), perm, preferred_element_type=jnp.float32)
        own_ref[part, :] = moved[:, :half].astype(jnp.bfloat16)
        send_ref[part, :] = moved[:, half:]
        return carry

    lax.fori_loop(0, (base + TILE - 1) // TILE, move, 0)
    packed = acc_w_ref[:, :rows]
    count = ((base + PACK - 1) // PACK).astype(jnp.float32)
    packed = jnp.where(lax.broadcasted_iota(jnp.int32, packed.shape, 0) == kdim + 1, count, packed)
    wt_ref[...] = packed.astype(jnp.bfloat16)
    wt_send_ref[...] = packed[: kdim + 8]


def prep(line, slab, owners, bins, grads, hess, side):
    rows, f_dev = bins.shape
    kdim = grads.shape[1]
    half = f_dev // 2
    return pl.pallas_call(
        functools.partial(prep_kernel, line, slab),
        in_specs=[SMEM_SPEC, pl.BlockSpec(memory_space=pltpu.HBM), VMEM_SPEC, VMEM_SPEC, VMEM_SPEC],
        out_specs=[VMEM_SPEC] * 4,
        out_shape=[
            jax.ShapeDtypeStruct((rows, half), jnp.bfloat16),
            jax.ShapeDtypeStruct((rows, half), jnp.float32),
            jax.ShapeDtypeStruct((kdim + 16, rows), jnp.bfloat16),
            jax.ShapeDtypeStruct((kdim + 8, rows), jnp.float32),
        ],
        scratch_shapes=[
            pltpu.VMEM((rows, f_dev), jnp.int32),
            pltpu.SemaphoreType.DMA((rows // TILE,)),
            pltpu.VMEM((rows + TILE + PACK, f_dev), jnp.float32),
            pltpu.VMEM((kdim + 16, rows + TILE + PACK), jnp.float32),
        ],
        compiler_params=pltpu.CompilerParams(vmem_limit_bytes=24 * MIB),
        cost_estimate=pl.CostEstimate(flops=4 * rows * f_dev * f_dev, bytes_accessed=8 * rows * f_dev, transcendentals=0),
        name="prep",
    )(owners, bins, grads.T, hess.astype(jnp.float32).reshape(1, rows), side.reshape(1, rows))


def tiles_in(wt_ref, kdim):
    return jnp.max(wt_ref[:, :128].astype(jnp.float32)[kdim + 1 : kdim + 2]).astype(jnp.int32)


def hist_kernel(first_column, width, levels, parts, kdim, has_init, *refs):
    pairs = [refs[2 * i : 2 * i + 2] for i in range(parts)]
    init_ref = refs[2 * parts] if has_init else None
    out_ref, rel_ref, wt_ref = refs[-3:]
    lanes = out_ref.shape[1]
    rows, half = pairs[0][0].shape
    src = lax.broadcasted_iota(jnp.int32, (half, lanes), 0)
    dst = lax.broadcasted_iota(jnp.int32, (half, lanes), 1)
    spread = jnp.where(src == first_column + lax.rem(dst, width), 1.0, 0.0).astype(jnp.bfloat16)
    lane = lax.broadcasted_iota(jnp.int32, (1, lanes), 1)
    shift = ((lane // width) * levels).astype(jnp.float32)
    one = jnp.ones((TILE, lanes), jnp.bfloat16)
    zero = jnp.zeros((TILE, lanes), jnp.bfloat16)

    def run(size):
        height = size * PACK
        for i, (bins_ref, w_ref) in enumerate(pairs):
            for r in range(0, height, PACK):
                block = bins_ref[r : r + PACK, :].astype(jnp.bfloat16)
                moved = jnp.dot(block, spread, preferred_element_type=jnp.float32)
                rel_ref[i * height + r : i * height + r + PACK, :] = (moved - shift).astype(jnp.bfloat16)
            weights = w_ref[:, :height]
            if w_ref.dtype != jnp.bfloat16:
                weights = jnp.concatenate([weights, jnp.zeros((8, height), jnp.float32)], axis=0).astype(jnp.bfloat16)
            wt_ref[:, i * height : (i + 1) * height] = weights
        tiles = parts * height // TILE

        def level(b, carry):
            value = jnp.full((TILE, lanes), b.astype(jnp.float32), jnp.float32).astype(jnp.bfloat16)
            total = jnp.zeros((wt_ref.shape[0], lanes), jnp.float32)
            for t in range(tiles):
                hit = rel_ref[t * TILE : (t + 1) * TILE, :] == value
                onehot = jnp.where(hit, one, zero)
                total = total + jnp.dot(wt_ref[:, t * TILE : (t + 1) * TILE], onehot, preferred_element_type=jnp.float32)
            start = pl.multiple_of(b * kdim, kdim)
            grad = total[:kdim, :]
            hess = total[kdim : kdim + 1, :]
            if has_init:
                grad = grad + init_ref[pl.ds(start, kdim), :]
                hess = hess + init_ref[pl.ds(levels * kdim + b, 1), :]
            out_ref[pl.ds(start, kdim), :] = grad
            out_ref[pl.ds(levels * kdim + b, 1), :] = hess
            return carry

        lax.fori_loop(0, levels, level, 0)

    needed = tiles_in(pairs[0][1], kdim)
    for _, w_ref in pairs[1:]:
        needed = jnp.maximum(needed, tiles_in(w_ref, kdim))
    most = rows // PACK
    sizes = [v for v in (4, 8, 10, 12, most) if v <= most]
    if parts == 2:
        sizes = sorted(sizes + [9])
    floor = -1
    for size in sizes:
        pl.when((needed > floor) & (needed <= size))(functools.partial(run, size))
        floor = size


def hist(first_column, width, levels, lanes, kdim, pairs, init=None):
    rows = pairs[0][0].shape[0]
    parts = len(pairs)
    operands = [x for pair in pairs for x in pair]
    if init is not None:
        operands.append(init)
    height = levels * (kdim + 1)
    return pl.pallas_call(
        functools.partial(hist_kernel, first_column, width, levels, parts, kdim, init is not None),
        in_specs=[VMEM_SPEC] * len(operands),
        out_specs=VMEM_SPEC,
        out_shape=jax.ShapeDtypeStruct((height, lanes), jnp.float32),
        scratch_shapes=[
            pltpu.VMEM((parts * rows, lanes), jnp.bfloat16),
            pltpu.VMEM((kdim + 16, parts * rows), jnp.bfloat16),
        ],
        compiler_params=pltpu.CompilerParams(vmem_limit_bytes=24 * MIB),
        cost_estimate=pl.CostEstimate(
            flops=2 * 256 * parts * rows * levels * lanes, bytes_accessed=parts * rows * lanes * 4, transcendentals=0
        ),
        name="hist",
    )(*operands)


def parent_kernel(width, levels, kdim, chunks, parent_ref, *out_refs):
    lanes = out_refs[0].shape[1]
    per_tile = 128 // width
    step = 128 // kdim
    for c in range(chunks):
        for tile in range(lanes // 128):
            for b in range(0, levels, step):
                rows = []
                for jj in range(per_tile):
                    bin_at = (tile * per_tile + jj) * levels + b
                    rows.append(parent_ref[c * width : (c + 1) * width, bin_at * kdim : bin_at * kdim + 128])
                block = jnp.concatenate(rows, axis=0) if per_tile > 1 else rows[0]
                out_refs[c][b * kdim : b * kdim + 128, tile * 128 : (tile + 1) * 128] = block.T


def parent_layout(width, levels, lanes, kdim, chunks, parent):
    shape = jax.ShapeDtypeStruct((levels * kdim, lanes), jnp.float32)
    return pl.pallas_call(
        functools.partial(parent_kernel, width, levels, kdim, chunks),
        in_specs=[VMEM_SPEC],
        out_specs=[VMEM_SPEC] * chunks,
        out_shape=[shape] * chunks,
        compiler_params=pltpu.CompilerParams(vmem_limit_bytes=16 * MIB),
        cost_estimate=pl.CostEstimate(flops=0, bytes_accessed=2 * parent.size * 4, transcendentals=0),
        name="parent_layout",
    )(parent)


def lane_prefix(total, width):
    lanes = total.shape[1]
    lane = lax.broadcasted_iota(jnp.int32, total.shape, 1)
    running = total
    reach = width
    while reach < lanes:
        running = running + jnp.where(lane >= reach, pltpu.roll(running, reach, 1), 0.0)
        reach *= 2
    whole = total
    reach = width
    while reach < lanes:
        whole = whole + pltpu.roll(whole, reach, 1)
        reach *= 2
    return running - total, running, whole


def gain_kernel(width, levels, kdim, last_ref, right_ref, left_ref, par_grad_ref, par_hess_ref, sign_ref, bound_ref, out_ref, grad_ref, hess_ref):
    hess_at = levels * kdim
    lanes = out_ref.shape[2]

    def small_at(start, size):
        return last_ref[pl.ds(start, size), :] + right_ref[pl.ds(start, size), :] + left_ref[pl.ds(start, size), :]

    sign = sign_ref[...]
    small_hess = small_at(hess_at, levels)
    hess_ref[0] = small_hess
    hess_ref[1] = par_hess_ref[...] - small_hess

    def add_up(b, carry):
        g0, g1, h0, h1 = carry
        start = pl.multiple_of(b * kdim, kdim)
        small = small_at(start, kdim)
        g0 = g0 + small
        g1 = g1 + (par_grad_ref[pl.ds(start, kdim), :] - small)
        h0 = h0 + hess_ref[0, pl.ds(b, 1), :]
        h1 = h1 + hess_ref[1, pl.ds(b, 1), :]
        grad_ref[0, pl.ds(start, kdim), :] = g0
        grad_ref[1, pl.ds(start, kdim), :] = g1
        hess_ref[0, pl.ds(b, 1), :] = h0
        hess_ref[1, pl.ds(b, 1), :] = h1
        return g0, g1, h0, h1

    zero_g = jnp.zeros((kdim, lanes), jnp.float32)
    zero_h = jnp.zeros((1, lanes), jnp.float32)
    ends = lax.fori_loop(0, levels, add_up, (zero_g, zero_g, zero_h, zero_h))
    for c in range(2):
        low = bound_ref[0, c].astype(jnp.float32) / 1024.0
        high = bound_ref[1, c].astype(jnp.float32) / 1024.0
        middle = 0.5 * (low + high)
        low_left = jnp.where(sign < 0, middle, low)
        high_left = jnp.where(sign > 0, middle, high)
        low_right = jnp.where(sign > 0, middle, low)
        high_right = jnp.where(sign < 0, middle, high)
        grad_before, _, grad_all = lane_prefix(ends[c], width)
        hess_rows = jnp.broadcast_to(ends[2 + c], (8, lanes))
        hess_before, _, hess_all = lane_prefix(hess_rows, width)
        hess_before, hess_all = hess_before[:1], hess_all[:1]

        def score(grad, hess, lower, upper):
            denom = jnp.maximum(hess, 0.0) + reg_lambda
            weight = jnp.clip(-grad / denom, lower, upper)
            return jnp.sum((2.0 * grad + denom * weight) * weight, axis=0, keepdims=True)

        def one_bin(b, carry):
            start = pl.multiple_of(b * kdim, kdim)
            grad_left = grad_ref[c, pl.ds(start, kdim), :] + grad_before
            hess_left = hess_ref[c, pl.ds(b, 1), :] + hess_before
            left = score(grad_left, hess_left, low_left, high_left)
            right = score(grad_all - grad_left, hess_all - hess_left, low_right, high_right)
            out_ref[c, pl.ds(b, 1), :] = (left + right) * (-1.0 / kdim)
            return carry

        lax.fori_loop(0, levels, one_bin, 0)


def gains_of(width, levels, lanes, kdim, last, right, left, par_grad, par_hess, sign, bounds):
    return pl.pallas_call(
        functools.partial(gain_kernel, width, levels, kdim),
        in_specs=[VMEM_SPEC] * 6 + [SMEM_SPEC],
        out_specs=VMEM_SPEC,
        out_shape=jax.ShapeDtypeStruct((2, levels, lanes), jnp.float32),
        scratch_shapes=[
            pltpu.VMEM((2, levels * kdim, lanes), jnp.float32),
            pltpu.VMEM((2, levels, lanes), jnp.float32),
        ],
        compiler_params=pltpu.CompilerParams(vmem_limit_bytes=24 * MIB),
        cost_estimate=pl.CostEstimate(flops=50 * levels * kdim * lanes, bytes_accessed=16 * levels * kdim * lanes, transcendentals=0),
        name="gains",
    )(last, right, left, par_grad, par_hess, sign, bounds)


def inverse_of(owner, slots):
    return jnp.sum(jnp.where(owner[None, :] == slots[:, None], slots[None, :], 0), axis=1)


def one_of(z, members):
    hit = z == members[0]
    for m in members[1:]:
        hit = hit | (z == m)
    return hit


def per_device(bins, grads, hess, node_side, signs, child_owner, parent_owner, parent_grad, parent_hess, node_low, node_high):
    line = lax.axis_size("dp")
    owners = line * lax.axis_size("sub")
    z = lax.axis_index("dp")
    core = lax.axis_index("sub")
    place = lax.axis_index(("dp", "sub"))
    column = lax.axis_index("feat")
    rows, f_dev = bins.shape
    kdim = grads.shape[1]
    nbins = parent_hess.shape[2]
    slab = parent_grad.shape[1]
    chunks = CHUNKS if slab >= 32 else 1
    width = slab // chunks
    lanes = min(256, width * nbins * kdim // 128)
    groups = lanes // width
    levels = nbins // groups
    plan = plan_of(line)

    own, send, wt, wt_send = prep(line, slab, parent_owner, bins, grads, hess, node_side)
    swap = [(0, 1), (1, 0)]
    wt_other = lax.ppermute(wt_send, "sub", swap)
    other = lax.ppermute(send, "sub", swap)
    mine = (own, wt)
    theirs = (other, wt_other)

    units = {}
    for c in range(chunks):
        units[0, c] = hist(c * width, width, levels, lanes, kdim, [mine])
    for c in range(chunks):
        units[0, c] = hist(c * width, width, levels, lanes, kdim, [theirs], units[0, c])

    def pick(kind, step, c):
        where_at = {}
        for zz in range(line):
            for p, role in enumerate(plan[zz]):
                if role[:2] == (kind, step):
                    where_at.setdefault(p, []).append(zz)
        spots = sorted(where_at)
        value = units[spots[0], c]
        for p in spots[1:]:
            value = jnp.where(one_of(z, where_at[p]), units[p, c], value)
        return value

    from_left = [None] * chunks
    from_right = [None] * chunks
    arrived = {}

    def after(step, c):
        if (step, c) not in arrived:
            return [mine, theirs]
        held, _ = lax.optimization_barrier((own, arrived[step, c]))
        return [(held, wt), theirs]

    for step in range(line - 1):
        if step > 0:
            for c in range(chunks):
                units[step, c] = hist(step * slab + c * width, width, levels, lanes, kdim, after(step - 2, c))
        for c in range(chunks):
            to_right = pick("R", step, c)
            to_left = pick("L", step, c)
            if step > 0:
                to_right = to_right + from_left[c]
                to_left = to_left + from_right[c]
            from_left[c] = lax.ppermute(to_right, "dp", [(i, i + 1) for i in range(step + 1)])
            from_right[c] = lax.ppermute(to_left, "dp", [(line - 1 - i, line - 2 - i) for i in range(step + 1)])
            arrived[step, c] = from_left[c]
    last = line - 1
    for c in range(chunks):
        units[last, c] = hist(last * slab + c * width, width, levels, lanes, kdim, after(last - 2, c))

    signs, child_owner, parent_owner, node_low, node_high, parent_grad, parent_hess, _ = lax.optimization_barrier(
        (signs, child_owner, parent_owner, node_low, node_high, parent_grad, parent_hess, arrived[max(line - 3, 0), 0])
    )
    slots = jnp.arange(owners, dtype=jnp.int32)
    parent_inv = inverse_of(parent_owner, slots)
    my_slab = parent_inv[place]
    ids = column * f_dev + my_slab * slab
    my_signs = lax.dynamic_slice(signs, (ids,), (slab,)).reshape(chunks, 1, width)
    my_signs = jnp.tile(my_signs, (1, 1, groups))
    bounds = jnp.stack([node_low, node_high])
    par_hess = jnp.transpose(parent_hess[0].reshape(chunks, width, groups, levels), (0, 3, 2, 1)).reshape(chunks, levels, lanes)
    par_grad = parent_layout(width, levels, lanes, kdim, chunks, parent_grad[0])

    child_inv = inverse_of(child_owner, slots)
    source_of = jnp.sum(jnp.where(child_inv[:, None] == slots[None, :], parent_owner[None, :], 0), axis=1)
    pair = 2 * z
    my_source = source_of[place]
    twin_source = source_of[pair + 1 - core]
    done = []
    for c in range(chunks):
        gain = gains_of(width, levels, lanes, kdim, units[last, c], from_left[c], from_right[c], par_grad[c], par_hess[c], my_signs[c], bounds)
        got = [gain] + [lax.ppermute(gain, "dp", [(i, (i + s) % line) for i in range(line)]) for s in range(1, line)]

        def choose(source):
            chip = source // 2
            value = got[0]
            for s in range(1, line):
                value = jnp.where(lax.rem(z - chip + line, line) == s, got[s], value)
            return value

        crossed = lax.ppermute(choose(twin_source), "sub", swap)
        gain = jnp.where(lax.rem(my_source, 2) == core, choose(my_source), crossed)
        gain = jnp.transpose(gain.reshape(2, levels, groups, width), (3, 0, 2, 1))
        done.append(gain.reshape(width, 2, nbins))
    return jnp.concatenate(done, axis=0)[None]


def solution(mesh):
    return jax.shard_map(
        per_device,
        mesh=mesh,
        in_specs=(
            P(("groups", "dp", "sub"), "feat"),
            P(("groups", "dp", "sub"), None),
            P(("groups", "dp", "sub")),
            P(("groups", "dp", "sub")),
            P("groups"),
            P("groups"),
            P("groups"),
            P(("groups", "dp", "sub"), "feat", None),
            P(("groups", "dp", "sub"), "feat", None),
            P("groups"),
            P("groups"),
        ),
        out_specs=P(("groups", "dp", "sub"), "feat", None, None),
        check_vma=False,
    )
```

```python
import functools

import jax
import jax.numpy as jnp
from jax import lax
from jax.experimental import pallas as pl
from jax.experimental.pallas import tpu as pltpu
from jax.sharding import PartitionSpec as P

reg_lambda = 1.0
CHUNKS = 2
TILE = 256
PACK = 128
FAST = 9
PREP_MIB = 56
MIB = 1024 * 1024
VMEM_SPEC = pl.BlockSpec(memory_space=pltpu.VMEM)
SMEM_SPEC = pl.BlockSpec(memory_space=pltpu.SMEM)


def plan_of(line):
    roles = []
    for z in range(line):
        mine = []
        for step in range(line - 1):
            if z <= step:
                mine.append(("R", step, line - 1 - step + z))
            if line - 1 - z <= step:
                mine.append(("L", step, step - (line - 1 - z)))
        mine.append(("F", line - 1, z))
        roles.append(mine)
    return roles


def prep_kernel(line, slab, owner_ref, bins_ref, grads_ref, hess_ref, side_ref, own_ref, send_ref, wt_ref, wt_send_ref, buf_ref, sems, acc_ref, acc_w_ref):
    rows, f_dev = bins_ref.shape
    half = f_dev // 2
    kdim = grads_ref.shape[0]
    reach = TILE + PACK
    blocks = rows // TILE
    copies = []
    for i in range(blocks):
        part = pl.ds(i * TILE, TILE)
        copies.append(pltpu.make_async_copy(bins_ref.at[part, :], buf_ref.at[part, :], sems.at[i]))
        copies[-1].start()

    ones = [jnp.where(side_ref[:, i * TILE : (i + 1) * TILE] == 1, 1.0, 0.0) for i in range(blocks)]
    counts = [jnp.sum(x).astype(jnp.int32) for x in ones]
    bases = [jnp.int32(0)]
    for count in counts:
        bases.append(bases[-1] + count)
    starts = [pl.multiple_of((base // PACK) * PACK, PACK) for base in bases]
    marks = jnp.concatenate(ones, axis=0)
    before = lax.broadcasted_iota(jnp.int32, (TILE, TILE), 0) < lax.broadcasted_iota(jnp.int32, (TILE, TILE), 1)
    before = jnp.where(before, 1.0, 0.0).astype(jnp.bfloat16)
    ahead = jnp.dot(marks.astype(jnp.bfloat16), before, preferred_element_type=jnp.float32).astype(jnp.int32)
    slot = lax.broadcasted_iota(jnp.int32, (reach, TILE), 0)
    acc_ref[:PACK, :] = jnp.zeros((PACK, f_dev), jnp.bfloat16)
    acc_w_ref[:, :PACK] = jnp.zeros((acc_w_ref.shape[0], PACK), jnp.float32)

    z, core = lax.axis_index("dp"), lax.axis_index("sub")
    column = lax.broadcasted_iota(jnp.int32, (1, f_dev), 1)
    position = lax.rem(column, half) // slab
    table = plan_of(line)
    chip = jnp.zeros_like(column)
    for p in range(line):
        target = jnp.int32(0)
        for zz in range(line):
            target = jnp.where(z == zz, jnp.int32(table[zz][p][2]), target)
        chip = jnp.where(position == p, target, chip)
    owner = 2 * chip + jnp.where(column < half, core, 1 - core)
    source = jnp.zeros_like(column)
    for q in range(2 * line):
        source = jnp.where(owner == owner_ref[q], q, source)
    source = source * slab + lax.rem(column, slab)
    perm = jnp.where(lax.broadcasted_iota(jnp.int32, (f_dev, f_dev), 0) == source, 1.0, 0.0).astype(jnp.bfloat16)

    for i in range(blocks):
        part = slice(i * TILE, (i + 1) * TILE)
        goal = jnp.where(ones[i] > 0.5, ahead[i : i + 1] + (bases[i] - starts[i]), -1)
        pack = jnp.where(slot == goal, 1.0, 0.0).astype(jnp.bfloat16)
        hess = jnp.broadcast_to(hess_ref[:, part], (16, TILE))
        first = lax.broadcasted_iota(jnp.int32, hess.shape, 0) == 0
        weights = jnp.concatenate([grads_ref[:, part].astype(jnp.float32), jnp.where(first, hess, 0.0)], axis=0)
        packed_w = lax.dot_general(weights.astype(jnp.bfloat16), pack, (((1,), (1,)), ((), ())), preferred_element_type=jnp.float32)
        acc_w_ref[:, pl.ds(starts[i], PACK)] += packed_w[:, :PACK]
        acc_w_ref[:, pl.ds(starts[i] + PACK, TILE)] = packed_w[:, PACK:]
        copies[i].wait()
        binned = buf_ref[part, :].astype(jnp.float32).astype(jnp.bfloat16)
        packed = jnp.dot(pack, binned, preferred_element_type=jnp.float32).astype(jnp.bfloat16)
        acc_ref[pl.ds(starts[i], PACK), :] += packed[:PACK]
        acc_ref[pl.ds(starts[i] + PACK, TILE), :] = packed[PACK:]

    def move(t, carry):
        part = pl.ds(pl.multiple_of(t * TILE, TILE), TILE)
        moved = jnp.dot(acc_ref[part, :], perm, preferred_element_type=jnp.float32)
        own_ref[part, :] = moved[:, :half].astype(jnp.bfloat16)
        send_ref[part, :] = moved[:, half:]
        return carry

    total = bases[blocks]
    lax.fori_loop(0, (total + TILE - 1) // TILE, move, 0)
    lane = lax.broadcasted_iota(jnp.int32, (acc_w_ref.shape[0], rows), 1)
    row = lax.broadcasted_iota(jnp.int32, lane.shape, 0)
    packed = jnp.where(lane < total, acc_w_ref[:, :rows], 0.0)
    packs = ((total + PACK - 1) // PACK).astype(jnp.float32)
    packed = jnp.where(row == kdim + 1, packs, packed)
    wt_ref[...] = packed.astype(jnp.bfloat16)
    wt_send_ref[...] = packed[: kdim + 8]


def prep(line, slab, owners, bins, grads, hess, side):
    rows, f_dev = bins.shape
    kdim = grads.shape[1]
    half = f_dev // 2
    return pl.pallas_call(
        functools.partial(prep_kernel, line, slab),
        in_specs=[SMEM_SPEC, pl.BlockSpec(memory_space=pl.ANY), VMEM_SPEC, VMEM_SPEC, VMEM_SPEC],
        out_specs=[VMEM_SPEC] * 4,
        out_shape=[
            jax.ShapeDtypeStruct((rows, half), jnp.bfloat16),
            jax.ShapeDtypeStruct((rows, half), jnp.float32),
            jax.ShapeDtypeStruct((kdim + 16, rows), jnp.bfloat16),
            jax.ShapeDtypeStruct((kdim + 8, rows), jnp.float32),
        ],
        scratch_shapes=[
            pltpu.VMEM((rows, f_dev), jnp.int32),
            pltpu.SemaphoreType.DMA((rows // TILE,)),
            pltpu.VMEM((rows + TILE + PACK, f_dev), jnp.bfloat16),
            pltpu.VMEM((kdim + 16, rows + TILE + PACK), jnp.float32),
        ],
        compiler_params=pltpu.CompilerParams(vmem_limit_bytes=PREP_MIB * MIB),
        cost_estimate=pl.CostEstimate(flops=4 * rows * f_dev * f_dev, bytes_accessed=8 * rows * f_dev, transcendentals=0),
        name="prep",
    )(owners, bins, grads.T, hess.astype(jnp.float32).reshape(1, rows), side.reshape(1, rows))


def tiles_in(wt_ref, kdim):
    return jnp.max(wt_ref[:, :128].astype(jnp.float32)[kdim + 1 : kdim + 2]).astype(jnp.int32)


def hist_kernel(first_column, width, levels, parts, kdim, has_init, *refs):
    pairs = [refs[2 * i : 2 * i + 2] for i in range(parts)]
    init_ref = refs[2 * parts] if has_init else None
    out_ref, rel_ref, wt_ref = refs[-3:]
    lanes = out_ref.shape[1]
    rows, half = pairs[0][0].shape
    src = lax.broadcasted_iota(jnp.int32, (half, lanes), 0)
    dst = lax.broadcasted_iota(jnp.int32, (half, lanes), 1)
    spread = jnp.where(src == first_column + lax.rem(dst, width), 1.0, 0.0).astype(jnp.bfloat16)
    lane = lax.broadcasted_iota(jnp.int32, (1, lanes), 1)
    shift = ((lane // width) * levels).astype(jnp.float32)
    one = jnp.ones((TILE, lanes), jnp.bfloat16)
    zero = jnp.zeros((TILE, lanes), jnp.bfloat16)

    def place_rows(bins_ref, source, target):
        block = bins_ref[pl.ds(source, PACK), :].astype(jnp.bfloat16)
        moved = jnp.dot(block, spread, preferred_element_type=jnp.float32)
        rel_ref[pl.ds(target, PACK), :] = (moved - shift).astype(jnp.bfloat16)

    def place_weights(height):
        for i, (_, w_ref) in enumerate(pairs):
            weights = w_ref[:, :height]
            if w_ref.dtype != jnp.bfloat16:
                weights = jnp.concatenate([weights, jnp.zeros((8, height), jnp.float32)], axis=0).astype(jnp.bfloat16)
            wt_ref[:, i * height : (i + 1) * height] = weights

    def sums_of(b, tiles):
        value = jnp.full((TILE, lanes), b.astype(jnp.float32), jnp.float32).astype(jnp.bfloat16)
        total = jnp.zeros((wt_ref.shape[0], lanes), jnp.float32)
        for first, size in tiles:
            hit = rel_ref[pl.ds(first, size), :] == value[:size]
            onehot = jnp.where(hit, one[:size], zero[:size])
            total = total + jnp.dot(wt_ref[:, pl.ds(first, size)], onehot, preferred_element_type=jnp.float32)
        return total[:kdim], total[kdim : kdim + 1]

    def spots_of(b):
        return pl.ds(pl.multiple_of(b * kdim, kdim), kdim), pl.ds(levels * kdim + b, 1)

    def fast():
        height = FAST * PACK
        for i, (bins_ref, _) in enumerate(pairs):
            for r in range(0, height, PACK):
                place_rows(bins_ref, r, i * height + r)
        place_weights(height)
        tiles = [(r, min(TILE, parts * height - r)) for r in range(0, parts * height, TILE)]

        def level(b, carry):
            grad, hess = sums_of(b, tiles)
            grad_spot, hess_spot = spots_of(b)
            if has_init:
                grad, hess = grad + init_ref[grad_spot, :], hess + init_ref[hess_spot, :]
            out_ref[grad_spot, :] = grad
            out_ref[hess_spot, :] = hess
            return carry

        lax.fori_loop(0, levels, level, 0)

    def general():
        for i, (bins_ref, _) in enumerate(pairs):

            def one_pack(p, carry):
                r = pl.multiple_of(p * PACK, PACK)
                place_rows(bins_ref, r, i * rows + r)
                return carry

            lax.fori_loop(0, rows // PACK, one_pack, 0)
        place_weights(rows)
        out_ref[...] = init_ref[...] if has_init else jnp.zeros(out_ref.shape, jnp.float32)
        step = 2 * TILE

        def group(g, carry):
            first = pl.multiple_of(g * step, step)

            def level(b, carry):
                grad, hess = sums_of(b, [(first, TILE), (first + TILE, TILE)])
                grad_spot, hess_spot = spots_of(b)
                out_ref[grad_spot, :] += grad
                out_ref[hess_spot, :] += hess
                return carry

            return lax.fori_loop(0, levels, level, carry)

        lax.fori_loop(0, parts * rows // step, group, 0)

    needed = tiles_in(pairs[0][1], kdim)
    for _, w_ref in pairs[1:]:
        needed = jnp.maximum(needed, tiles_in(w_ref, kdim))
    if FAST * PACK < rows:
        pl.when(needed <= FAST)(fast)
        pl.when(needed > FAST)(general)
    else:
        general()


def hist(first_column, width, levels, lanes, kdim, pairs, init=None, tie=()):
    rows = pairs[0][0].shape[0]
    parts = len(pairs)
    operands = [x for pair in pairs for x in pair]
    if init is not None:
        operands.append(init)
    specs = [VMEM_SPEC] * len(operands) + [pl.BlockSpec(memory_space=pl.ANY)] * len(tie)
    height = levels * (kdim + 1)
    return pl.pallas_call(
        functools.partial(hist_kernel, first_column, width, levels, parts, kdim, init is not None),
        in_specs=specs,
        out_specs=VMEM_SPEC,
        out_shape=jax.ShapeDtypeStruct((height, lanes), jnp.float32),
        scratch_shapes=[
            pltpu.VMEM((parts * rows, lanes), jnp.bfloat16),
            pltpu.VMEM((kdim + 16, parts * rows), jnp.bfloat16),
        ],
        compiler_params=pltpu.CompilerParams(vmem_limit_bytes=20 * MIB),
        cost_estimate=pl.CostEstimate(
            flops=2 * 128 * parts * rows * levels * lanes, bytes_accessed=parts * rows * lanes * 4, transcendentals=0
        ),
        name="hist",
    )(*operands, *tie)


def repeat_lanes(x, width, lanes):
    if lanes > x.shape[1]:
        x = jnp.concatenate([x] * (lanes // x.shape[1]), axis=1)
    x = jnp.where(lax.broadcasted_iota(jnp.int32, x.shape, 1) < width, x[:, :lanes], 0)
    reach = width
    while reach < lanes:
        x = x + pltpu.roll(x, reach, 1)
        reach *= 2
    return x


def layout_kernel(width, levels, kdim, chunks, owner_ref, sign_ref, parent_ref, hess_ref, tie_ref, *out_refs):
    del tie_ref
    grad_refs, hess_refs, sign_refs = out_refs[:chunks], out_refs[chunks : 2 * chunks], out_refs[2 * chunks :]
    lanes = grad_refs[0].shape[1]
    slab = width * chunks
    owners = owner_ref.shape[0]
    place = 2 * lax.axis_index("dp") + lax.axis_index("sub")
    slab_at = jnp.int32(0)
    for q in range(owners):
        slab_at = jnp.where(owner_ref[q] == place, q, slab_at)
    offset = lax.axis_index("feat") * (owners * slab) + slab_at * slab
    features = sign_ref.shape[1]
    signs = jnp.broadcast_to(sign_ref[...], (8, features))
    per_tile = 128 // width
    step = 128 // kdim
    for c in range(chunks):
        turned = pltpu.roll(signs, lax.rem(features - offset - c * width + features, features), 1)
        sign_refs[c][...] = repeat_lanes(turned[:, :128], width, lanes)
        rows = hess_ref[c * width : (c + 1) * width, :]
        turned = jnp.concatenate([rows] * (128 // width), axis=0).T
        total = jnp.zeros((levels, lanes), jnp.float32)
        for j in range(lanes // width):
            piece = turned[j * levels : (j + 1) * levels, :]
            piece = jnp.concatenate([piece] * (lanes // 128), axis=1)
            group = lax.broadcasted_iota(jnp.int32, piece.shape, 1) // width
            total = jnp.where(group == j, piece, total)
        hess_refs[c][...] = total
        for tile in range(lanes // 128):
            for b in range(0, levels, step):
                rows = []
                for jj in range(per_tile):
                    bin_at = (tile * per_tile + jj) * levels + b
                    rows.append(parent_ref[c * width : (c + 1) * width, bin_at * kdim : bin_at * kdim + 128])
                block = jnp.concatenate(rows, axis=0) if per_tile > 1 else rows[0]
                grad_refs[c][b * kdim : b * kdim + 128, tile * 128 : (tile + 1) * 128] = block.T


def parent_layout(width, levels, lanes, kdim, chunks, owners, signs, parent, hess, tie):
    shapes = [jax.ShapeDtypeStruct((levels * kdim, lanes), jnp.float32)] * chunks
    shapes += [jax.ShapeDtypeStruct((levels, lanes), jnp.float32)] * chunks
    shapes += [jax.ShapeDtypeStruct((8, lanes), jnp.int32)] * chunks
    out = pl.pallas_call(
        functools.partial(layout_kernel, width, levels, kdim, chunks),
        in_specs=[SMEM_SPEC] + [VMEM_SPEC] * 3 + [pl.BlockSpec(memory_space=pl.ANY)],
        out_specs=[VMEM_SPEC] * (3 * chunks),
        out_shape=shapes,
        compiler_params=pltpu.CompilerParams(vmem_limit_bytes=16 * MIB),
        cost_estimate=pl.CostEstimate(flops=0, bytes_accessed=2 * parent.size * 4, transcendentals=0),
        name="parent_layout",
    )(owners, signs.reshape(1, -1), parent, hess, tie)
    return out[:chunks], out[chunks : 2 * chunks], out[2 * chunks :]


def lane_prefix(total, width):
    lanes = total.shape[1]
    lane = lax.broadcasted_iota(jnp.int32, total.shape, 1)
    running = total
    reach = width
    while reach < lanes:
        running = running + jnp.where(lane >= reach, pltpu.roll(running, reach, 1), 0.0)
        reach *= 2
    whole = total
    reach = width
    while reach < lanes:
        whole = whole + pltpu.roll(whole, reach, 1)
        reach *= 2
    return running - total, running, whole


def gain_kernel(width, levels, kdim, last_ref, right_ref, left_ref, par_grad_ref, par_hess_ref, sign_ref, low_ref, high_ref, out_ref, grad_ref, hess_ref):
    hess_at = levels * kdim
    lanes = out_ref.shape[2]

    def small_at(start, size):
        return last_ref[pl.ds(start, size), :] + right_ref[pl.ds(start, size), :] + left_ref[pl.ds(start, size), :]

    sign = sign_ref[:1, :]
    small_hess = small_at(hess_at, levels)
    hess_ref[0] = small_hess
    hess_ref[1] = par_hess_ref[...] - small_hess

    def add_up(b, carry):
        g0, g1, h0, h1 = carry
        start = pl.multiple_of(b * kdim, kdim)
        small = small_at(start, kdim)
        g0 = g0 + small
        g1 = g1 + (par_grad_ref[pl.ds(start, kdim), :] - small)
        h0 = h0 + hess_ref[0, pl.ds(b, 1), :]
        h1 = h1 + hess_ref[1, pl.ds(b, 1), :]
        grad_ref[0, pl.ds(start, kdim), :] = g0
        grad_ref[1, pl.ds(start, kdim), :] = g1
        hess_ref[0, pl.ds(b, 1), :] = h0
        hess_ref[1, pl.ds(b, 1), :] = h1
        return g0, g1, h0, h1

    zero_g = jnp.zeros((kdim, lanes), jnp.float32)
    zero_h = jnp.zeros((1, lanes), jnp.float32)
    ends = lax.fori_loop(0, levels, add_up, (zero_g, zero_g, zero_h, zero_h))
    for c in range(2):
        low = low_ref[c].astype(jnp.float32) / 1024.0
        high = high_ref[c].astype(jnp.float32) / 1024.0
        middle = 0.5 * (low + high)
        low_left = jnp.where(sign < 0, middle, low)
        high_left = jnp.where(sign > 0, middle, high)
        low_right = jnp.where(sign > 0, middle, low)
        high_right = jnp.where(sign < 0, middle, high)
        grad_before, _, grad_all = lane_prefix(ends[c], width)
        hess_rows = jnp.broadcast_to(ends[2 + c], (8, lanes))
        hess_before, _, hess_all = lane_prefix(hess_rows, width)
        hess_before, hess_all = hess_before[:1], hess_all[:1]

        def score(grad, hess, lower, upper):
            denom = jnp.maximum(hess, 0.0) + reg_lambda
            weight = jnp.clip(-grad / denom, lower, upper)
            return jnp.sum((2.0 * grad + denom * weight) * weight, axis=0, keepdims=True)

        def one_bin(b, carry):
            start = pl.multiple_of(b * kdim, kdim)
            grad_left = grad_ref[c, pl.ds(start, kdim), :] + grad_before
            hess_left = hess_ref[c, pl.ds(b, 1), :] + hess_before
            left = score(grad_left, hess_left, low_left, high_left)
            right = score(grad_all - grad_left, hess_all - hess_left, low_right, high_right)
            out_ref[c, pl.ds(b, 1), :] = (left + right) * (-1.0 / kdim)
            return carry

        lax.fori_loop(0, levels, one_bin, 0)


def gains_of(width, levels, lanes, kdim, last, right, left, par_grad, par_hess, sign, node_low, node_high):
    return pl.pallas_call(
        functools.partial(gain_kernel, width, levels, kdim),
        in_specs=[VMEM_SPEC] * 6 + [SMEM_SPEC] * 2,
        out_specs=VMEM_SPEC,
        out_shape=jax.ShapeDtypeStruct((2, levels, lanes), jnp.float32),
        scratch_shapes=[
            pltpu.VMEM((2, levels * kdim, lanes), jnp.float32),
            pltpu.VMEM((2, levels, lanes), jnp.float32),
        ],
        compiler_params=pltpu.CompilerParams(vmem_limit_bytes=24 * MIB),
        cost_estimate=pl.CostEstimate(flops=50 * levels * kdim * lanes, bytes_accessed=16 * levels * kdim * lanes, transcendentals=0),
        name="gains",
    )(last, right, left, par_grad, par_hess, sign, node_low, node_high)


def source_of(place, child_ref, parent_ref):
    source = jnp.int32(0)
    for q in range(child_ref.shape[0]):
        source = jnp.where(child_ref[q] == place, parent_ref[q], source)
    return source


def choose_kernel(line, child_ref, parent_ref, *refs):
    z, core = lax.axis_index("dp"), lax.axis_index("sub")
    chip = source_of(2 * z + 1 - core, child_ref, parent_ref) // 2
    out_ref = refs[-1]
    for s in range(line):

        @pl.when(lax.rem(z - chip + line, line) == s)
        def _():
            out_ref[...] = refs[s][...]


def choose(line, child_owner, parent_owner, got):
    return pl.pallas_call(
        functools.partial(choose_kernel, line),
        in_specs=[SMEM_SPEC] * 2 + [VMEM_SPEC] * line,
        out_specs=VMEM_SPEC,
        out_shape=jax.ShapeDtypeStruct(got[0].shape, jnp.float32),
        name="choose",
    )(child_owner, parent_owner, *got)


def finish_kernel(line, chunks, width, child_ref, parent_ref, *refs):
    out_ref, held_ref = refs[-2:]
    z, core = lax.axis_index("dp"), lax.axis_index("sub")
    source = source_of(2 * z + core, child_ref, parent_ref)
    same = lax.rem(source, 2) == core
    shift = lax.rem(z - source // 2 + line, line)
    for c in range(chunks):
        got = refs[c * (line + 1) : (c + 1) * (line + 1)]
        for s in range(line):

            @pl.when(same & (shift == s))
            def _():
                held_ref[c] = got[s][...]

        @pl.when(jnp.logical_not(same))
        def _():
            held_ref[c] = got[line][...]

    slab = width * chunks
    lanes = held_ref.shape[3]
    total = jnp.zeros((128, 128), jnp.float32)
    column = lax.broadcasted_iota(jnp.int32, (128, 128), 1)
    for child in range(2):
        for c in range(chunks):
            gain = held_ref[c, child]
            at = child * slab + c * width
            pieces = []
            for j in range(lanes // width):
                turn = (at - j * width) % lanes
                turned = pltpu.roll(gain, turn, 1) if turn else gain
                pieces.append(turned[:, :128])
            stack = jnp.concatenate(pieces, axis=0)
            total = jnp.where((column >= at) & (column < at + width), stack, total)
    turned = total.T
    for child in range(2):
        out_ref[:, child, :] = turned[child * slab : (child + 1) * slab]


def finish(line, chunks, width, nbins, child_owner, parent_owner, parts):
    shape = parts[0][0].shape
    flat = [x for part in parts for x in part]
    return pl.pallas_call(
        functools.partial(finish_kernel, line, chunks, width),
        in_specs=[SMEM_SPEC] * 2 + [VMEM_SPEC] * len(flat),
        out_specs=VMEM_SPEC,
        out_shape=jax.ShapeDtypeStruct((width * chunks, 2, nbins), jnp.float32),
        scratch_shapes=[pltpu.VMEM((chunks, *shape), jnp.float32)],
        name="finish",
    )(child_owner, parent_owner, *flat)


def one_of(z, members):
    hit = z == members[0]
    for m in members[1:]:
        hit = hit | (z == m)
    return hit


def per_device(bins, grads, hess, node_side, signs, child_owner, parent_owner, parent_grad, parent_hess, node_low, node_high):
    line = lax.axis_size("dp")
    z = lax.axis_index("dp")
    kdim = grads.shape[1]
    nbins = parent_hess.shape[2]
    slab = parent_grad.shape[1]
    chunks = CHUNKS if slab >= 32 else 1
    width = slab // chunks
    lanes = min(256, width * nbins * kdim // 128)
    levels = nbins // (lanes // width)
    plan = plan_of(line)

    own, send, wt, wt_send = prep(line, slab, parent_owner, bins, grads, hess, node_side)
    swap = [(0, 1), (1, 0)]
    wt_other = lax.ppermute(wt_send, "sub", swap)
    other = lax.ppermute(send, "sub", swap)
    mine = (own, wt)
    theirs = (other, wt_other)

    units = {}
    for c in range(chunks):
        units[0, c] = hist(c * width, width, levels, lanes, kdim, [mine])
    for c in range(chunks):
        units[0, c] = hist(c * width, width, levels, lanes, kdim, [theirs], units[0, c])

    def pick(kind, step, c):
        where_at = {}
        for zz in range(line):
            for p, role in enumerate(plan[zz]):
                if role[:2] == (kind, step):
                    where_at.setdefault(p, []).append(zz)
        spots = sorted(where_at)
        value = units[spots[0], c]
        for p in spots[1:]:
            value = jnp.where(one_of(z, where_at[p]), units[p, c], value)
        return value

    from_left = [None] * chunks
    from_right = [None] * chunks
    arrived = []

    def tie_of(step, c):
        at = min(step * chunks + c - 3, (line - 2) * chunks - 1)
        return (arrived[at],) if at >= 0 else (units[0, chunks - 1],)

    last = line - 1
    for step in range(line - 1):
        for c in range(chunks):
            if step > 0:
                units[step, c] = hist(step * slab + c * width, width, levels, lanes, kdim, [mine, theirs], tie=tie_of(step, c))
            to_right = pick("R", step, c)
            to_left = pick("L", step, c)
            if step > 0:
                to_right = to_right + from_left[c]
                to_left = to_left + from_right[c]
            from_left[c] = lax.ppermute(to_right, "dp", [(i, i + 1) for i in range(step + 1)])
            from_right[c] = lax.ppermute(to_left, "dp", [(line - 1 - i, line - 2 - i) for i in range(step + 1)])
            arrived.append(from_left[c])
    par_grad, par_hess, sign = parent_layout(
        width, levels, lanes, kdim, chunks, parent_owner, signs, parent_grad[0], parent_hess[0], tie_of(last, 0)[0]
    )
    for c in range(chunks):
        units[last, c] = hist(last * slab + c * width, width, levels, lanes, kdim, [mine, theirs], tie=tie_of(last, c))

    done = []
    for c in range(chunks):
        gain = gains_of(
            width, levels, lanes, kdim, units[last, c], from_left[c], from_right[c], par_grad[c], par_hess[c], sign[c], node_low, node_high
        )
        got = [gain] + [lax.ppermute(gain, "dp", [(i, (i + s) % line) for i in range(line)]) for s in range(1, line)]
        got.append(lax.ppermute(choose(line, child_owner, parent_owner, got), "sub", swap))
        done.append(got)
    return finish(line, chunks, width, nbins, child_owner, parent_owner, done)[None]


def solution(mesh):
    return jax.shard_map(
        per_device,
        mesh=mesh,
        in_specs=(
            P(("groups", "dp", "sub"), "feat"),
            P(("groups", "dp", "sub"), None),
            P(("groups", "dp", "sub")),
            P(("groups", "dp", "sub")),
            P("groups"),
            P("groups"),
            P("groups"),
            P(("groups", "dp", "sub"), "feat", None),
            P(("groups", "dp", "sub"), "feat", None),
            P("groups"),
            P("groups"),
        ),
        out_specs=P(("groups", "dp", "sub"), "feat", None, None),
        check_vma=False,
    )
```

```python
import functools

import jax
import jax.numpy as jnp
from jax import lax
from jax.experimental import pallas as pl
from jax.experimental.pallas import tpu as pltpu
from jax.sharding import PartitionSpec as P

reg_lambda = 1.0
CHUNKS = 2
TILE = 256
PACK = 128
FAST = 9
PREP_MIB = 56
MIB = 1024 * 1024
VMEM_SPEC = pl.BlockSpec(memory_space=pltpu.VMEM)
SMEM_SPEC = pl.BlockSpec(memory_space=pltpu.SMEM)


def plan_of(line):
    roles = []
    for z in range(line):
        mine = []
        for step in range(line - 1):
            now = []
            if z <= step:
                now.append(("R", step, line - 1 - step + z))
            if line - 1 - z <= step:
                now.append(("L", step, step - (line - 1 - z)))
            mine.extend(now if 2 * z < line else now[::-1])
        mine.append(("F", line - 1, z))
        roles.append(mine)
    return roles


def prep_kernel(line, slab, owner_ref, bins_ref, grads_ref, hess_ref, side_ref, own_ref, send_ref, wt_ref, wt_send_ref, buf_ref, sems, acc_ref, acc_w_ref):
    rows, f_dev = bins_ref.shape
    half = f_dev // 2
    kdim = grads_ref.shape[0]
    reach = TILE + PACK
    blocks = rows // TILE
    copies = []
    for i in range(blocks):
        part = pl.ds(i * TILE, TILE)
        copies.append(pltpu.make_async_copy(bins_ref.at[part, :], buf_ref.at[part, :], sems.at[i]))
        copies[-1].start()

    hess_row = hess_ref[...].astype(jnp.float32).reshape(1, rows)
    ones = [jnp.where(side_ref[:, i * TILE : (i + 1) * TILE] == 1, 1.0, 0.0) for i in range(blocks)]
    counts = [jnp.sum(x).astype(jnp.int32) for x in ones]
    bases = [jnp.int32(0)]
    for count in counts:
        bases.append(bases[-1] + count)
    starts = [pl.multiple_of((base // PACK) * PACK, PACK) for base in bases]
    marks = jnp.concatenate(ones, axis=0)
    before = lax.broadcasted_iota(jnp.int32, (TILE, TILE), 0) < lax.broadcasted_iota(jnp.int32, (TILE, TILE), 1)
    before = jnp.where(before, 1.0, 0.0).astype(jnp.bfloat16)
    ahead = jnp.dot(marks.astype(jnp.bfloat16), before, preferred_element_type=jnp.float32).astype(jnp.int32)
    slot = lax.broadcasted_iota(jnp.int32, (reach, TILE), 0)
    acc_ref[:PACK, :] = jnp.zeros((PACK, f_dev), jnp.bfloat16)
    acc_w_ref[:, :PACK] = jnp.zeros((acc_w_ref.shape[0], PACK), jnp.float32)

    z, core = lax.axis_index("dp"), lax.axis_index("sub")
    column = lax.broadcasted_iota(jnp.int32, (1, f_dev), 1)
    position = lax.rem(column, half) // slab
    table = plan_of(line)
    chip = jnp.zeros_like(column)
    for p in range(line):
        target = jnp.int32(0)
        for zz in range(line):
            target = jnp.where(z == zz, jnp.int32(table[zz][p][2]), target)
        chip = jnp.where(position == p, target, chip)
    owner = 2 * chip + jnp.where(column < half, core, 1 - core)
    source = jnp.zeros_like(column)
    for q in range(2 * line):
        source = jnp.where(owner == owner_ref[q], q, source)
    source = source * slab + lax.rem(column, slab)
    perm = jnp.where(lax.broadcasted_iota(jnp.int32, (f_dev, f_dev), 0) == source, 1.0, 0.0).astype(jnp.bfloat16)

    for i in range(blocks):
        part = slice(i * TILE, (i + 1) * TILE)
        goal = jnp.where(ones[i] > 0.5, ahead[i : i + 1] + (bases[i] - starts[i]), -1)
        pack = jnp.where(slot == goal, 1.0, 0.0).astype(jnp.bfloat16)
        hess = jnp.broadcast_to(hess_row[:, part], (16, TILE))
        first = lax.broadcasted_iota(jnp.int32, hess.shape, 0) == 0
        weights = jnp.concatenate([grads_ref[:, part].astype(jnp.float32), jnp.where(first, hess, 0.0)], axis=0)
        packed_w = lax.dot_general(weights.astype(jnp.bfloat16), pack, (((1,), (1,)), ((), ())), preferred_element_type=jnp.float32)
        acc_w_ref[:, pl.ds(starts[i], PACK)] += packed_w[:, :PACK]
        acc_w_ref[:, pl.ds(starts[i] + PACK, TILE)] = packed_w[:, PACK:]
        copies[i].wait()
        binned = buf_ref[part, :].astype(jnp.float32).astype(jnp.bfloat16)
        packed = jnp.dot(pack, binned, preferred_element_type=jnp.float32).astype(jnp.bfloat16)
        acc_ref[pl.ds(starts[i], PACK), :] += packed[:PACK]
        acc_ref[pl.ds(starts[i] + PACK, TILE), :] = packed[PACK:]

    def move(t, carry):
        part = pl.ds(pl.multiple_of(t * TILE, TILE), TILE)
        moved = jnp.dot(acc_ref[part, :], perm, preferred_element_type=jnp.float32)
        own_ref[part, :] = moved[:, :half].astype(jnp.bfloat16)
        send_ref[part, :] = moved[:, half:]
        return carry

    total = bases[blocks]
    lax.fori_loop(0, (total + TILE - 1) // TILE, move, 0)
    lane = lax.broadcasted_iota(jnp.int32, (acc_w_ref.shape[0], rows), 1)
    row = lax.broadcasted_iota(jnp.int32, lane.shape, 0)
    packed = jnp.where(lane < total, acc_w_ref[:, :rows], 0.0)
    packs = ((total + PACK - 1) // PACK).astype(jnp.float32)
    packed = jnp.where(row == kdim + 1, packs, packed)
    wt_ref[...] = packed.astype(jnp.bfloat16)
    wt_send_ref[...] = packed[: kdim + 8]


def prep(line, slab, owners, bins, grads, hess, side):
    rows, f_dev = bins.shape
    kdim = grads.shape[1]
    half = f_dev // 2
    return pl.pallas_call(
        functools.partial(prep_kernel, line, slab),
        in_specs=[SMEM_SPEC, pl.BlockSpec(memory_space=pl.ANY), VMEM_SPEC, VMEM_SPEC, VMEM_SPEC],
        out_specs=[VMEM_SPEC] * 4,
        out_shape=[
            jax.ShapeDtypeStruct((rows, half), jnp.bfloat16),
            jax.ShapeDtypeStruct((rows, half), jnp.float32),
            jax.ShapeDtypeStruct((kdim + 16, rows), jnp.bfloat16),
            jax.ShapeDtypeStruct((kdim + 8, rows), jnp.float32),
        ],
        scratch_shapes=[
            pltpu.VMEM((rows, f_dev), jnp.int32),
            pltpu.SemaphoreType.DMA((rows // TILE,)),
            pltpu.VMEM((rows + TILE + PACK, f_dev), jnp.bfloat16),
            pltpu.VMEM((kdim + 16, rows + TILE + PACK), jnp.float32),
        ],
        compiler_params=pltpu.CompilerParams(vmem_limit_bytes=PREP_MIB * MIB),
        cost_estimate=pl.CostEstimate(flops=4 * rows * f_dev * f_dev, bytes_accessed=8 * rows * f_dev, transcendentals=0),
        name="prep",
    )(owners, bins, grads.T, hess, side.reshape(1, rows))


def tiles_in(wt_ref, kdim):
    return jnp.max(wt_ref[:, :128].astype(jnp.float32)[kdim + 1 : kdim + 2]).astype(jnp.int32)


def hist_kernel(first_column, width, levels, parts, kdim, has_init, *refs):
    pairs = [refs[2 * i : 2 * i + 2] for i in range(parts)]
    init_ref = refs[2 * parts] if has_init else None
    out_ref, rel_ref, wt_ref = refs[-3:]
    lanes = out_ref.shape[1]
    rows, half = pairs[0][0].shape
    src = lax.broadcasted_iota(jnp.int32, (half, lanes), 0)
    dst = lax.broadcasted_iota(jnp.int32, (half, lanes), 1)
    spread = jnp.where(src == first_column + lax.rem(dst, width), 1.0, 0.0).astype(jnp.bfloat16)
    lane = lax.broadcasted_iota(jnp.int32, (1, lanes), 1)
    shift = ((lane // width) * levels).astype(jnp.float32)
    one = jnp.ones((TILE, lanes), jnp.bfloat16)
    zero = jnp.zeros((TILE, lanes), jnp.bfloat16)

    def place_rows(bins_ref, source, target, size):
        block = bins_ref[pl.ds(source, size), :].astype(jnp.bfloat16)
        moved = jnp.dot(block, spread, preferred_element_type=jnp.float32)
        rel_ref[pl.ds(target, size), :] = (moved - shift).astype(jnp.bfloat16)

    def place_weights(height):
        for i, (_, w_ref) in enumerate(pairs):
            weights = w_ref[:, :height]
            if w_ref.dtype != jnp.bfloat16:
                weights = jnp.concatenate([weights, jnp.zeros((8, height), jnp.float32)], axis=0).astype(jnp.bfloat16)
            wt_ref[:, i * height : (i + 1) * height] = weights

    def sums_of(b, tiles):
        value = jnp.full((TILE, lanes), b.astype(jnp.float32), jnp.float32).astype(jnp.bfloat16)
        total = jnp.zeros((wt_ref.shape[0], lanes), jnp.float32)
        for first, size in tiles:
            hit = rel_ref[pl.ds(first, size), :] == value[:size]
            onehot = jnp.where(hit, one[:size], zero[:size])
            total = total + jnp.dot(wt_ref[:, pl.ds(first, size)], onehot, preferred_element_type=jnp.float32)
        return total[:kdim], total[kdim : kdim + 1]

    def spots_of(b):
        return pl.ds(pl.multiple_of(b * kdim, kdim), kdim), pl.ds(levels * kdim + b, 1)

    def fast():
        height = FAST * PACK
        for i, (bins_ref, _) in enumerate(pairs):
            for r in range(0, height, 3 * PACK):
                place_rows(bins_ref, r, i * height + r, 3 * PACK)
        place_weights(height)
        tiles = [(r, min(TILE, parts * height - r)) for r in range(0, parts * height, TILE)]

        def level(b, carry):
            grad, hess = sums_of(b, tiles)
            grad_spot, hess_spot = spots_of(b)
            if has_init:
                grad, hess = grad + init_ref[grad_spot, :], hess + init_ref[hess_spot, :]
            out_ref[grad_spot, :] = grad
            out_ref[hess_spot, :] = hess
            return carry

        lax.fori_loop(0, levels, level, 0)

    def general():
        for i, (bins_ref, _) in enumerate(pairs):

            def one_pack(p, carry):
                r = pl.multiple_of(p * PACK, PACK)
                place_rows(bins_ref, r, i * rows + r, PACK)
                return carry

            lax.fori_loop(0, rows // PACK, one_pack, 0)
        place_weights(rows)
        out_ref[...] = init_ref[...] if has_init else jnp.zeros(out_ref.shape, jnp.float32)
        step = 2 * TILE

        def group(g, carry):
            first = pl.multiple_of(g * step, step)

            def level(b, carry):
                grad, hess = sums_of(b, [(first, TILE), (first + TILE, TILE)])
                grad_spot, hess_spot = spots_of(b)
                out_ref[grad_spot, :] += grad
                out_ref[hess_spot, :] += hess
                return carry

            return lax.fori_loop(0, levels, level, carry)

        lax.fori_loop(0, parts * rows // step, group, 0)

    needed = tiles_in(pairs[0][1], kdim)
    for _, w_ref in pairs[1:]:
        needed = jnp.maximum(needed, tiles_in(w_ref, kdim))
    if FAST * PACK < rows:
        pl.when(needed <= FAST)(fast)
        pl.when(needed > FAST)(general)
    else:
        general()


def hist(first_column, width, levels, lanes, kdim, pairs, init=None, tie=()):
    rows = pairs[0][0].shape[0]
    parts = len(pairs)
    operands = [x for pair in pairs for x in pair]
    if init is not None:
        operands.append(init)
    specs = [VMEM_SPEC] * len(operands) + [pl.BlockSpec(memory_space=pl.ANY)] * len(tie)
    height = levels * (kdim + 1)
    return pl.pallas_call(
        functools.partial(hist_kernel, first_column, width, levels, parts, kdim, init is not None),
        in_specs=specs,
        out_specs=VMEM_SPEC,
        out_shape=jax.ShapeDtypeStruct((height, lanes), jnp.float32),
        scratch_shapes=[
            pltpu.VMEM((parts * rows, lanes), jnp.bfloat16),
            pltpu.VMEM((kdim + 16, parts * rows), jnp.bfloat16),
        ],
        compiler_params=pltpu.CompilerParams(vmem_limit_bytes=20 * MIB),
        cost_estimate=pl.CostEstimate(
            flops=2 * 128 * parts * rows * levels * lanes, bytes_accessed=parts * rows * lanes * 4, transcendentals=0
        ),
        name="hist",
    )(*operands, *tie)


def source_of(place, child_ref, parent_ref):
    source = jnp.int32(0)
    for q in range(child_ref.shape[0]):
        source = jnp.where(child_ref[q] == place, parent_ref[q], source)
    return source


def repeat_lanes(x, width, lanes):
    if lanes > x.shape[1]:
        x = jnp.concatenate([x] * (lanes // x.shape[1]), axis=1)
    x = jnp.where(lax.broadcasted_iota(jnp.int32, x.shape, 1) < width, x[:, :lanes], 0)
    reach = width
    while reach < lanes:
        x = x + pltpu.roll(x, reach, 1)
        reach *= 2
    return x


def layout_kernel(width, levels, kdim, chunks, line, child_ref, owner_ref, sign_ref, parent_ref, hess_ref, tie_ref, *out_refs):
    del tie_ref
    grad_refs, hess_refs, sign_refs = out_refs[:chunks], out_refs[chunks : 2 * chunks], out_refs[2 * chunks : 3 * chunks]
    lanes = grad_refs[0].shape[1]
    slab = width * chunks
    owners = owner_ref.shape[0]
    z, core = lax.axis_index("dp"), lax.axis_index("sub")
    place = 2 * z + core
    mine = source_of(place, child_ref, owner_ref)
    twin = source_of(2 * z + 1 - core, child_ref, owner_ref)
    row = lax.broadcasted_iota(jnp.int32, (8, 128), 0)
    route = jnp.where(row == 0, lax.rem(z - mine // 2 + line, line), lax.rem(z - twin // 2 + line, line))
    out_refs[-1][...] = jnp.where(row == 2, jnp.where(lax.rem(mine, 2) == core, 1, 0), route)
    slab_at = jnp.int32(0)
    for q in range(owners):
        slab_at = jnp.where(owner_ref[q] == place, q, slab_at)
    offset = lax.axis_index("feat") * (owners * slab) + slab_at * slab
    features = sign_ref.shape[1]
    signs = jnp.broadcast_to(sign_ref[...], (8, features))
    per_tile = 128 // width
    step = 128 // kdim
    for c in range(chunks):
        turned = pltpu.roll(signs, lax.rem(features - offset - c * width + features, features), 1)
        sign_refs[c][...] = repeat_lanes(turned[:, :128], width, lanes)
        rows = hess_ref[c * width : (c + 1) * width, :]
        turned = jnp.concatenate([rows] * (128 // width), axis=0).T
        total = jnp.zeros((levels, lanes), jnp.float32)
        for j in range(lanes // width):
            piece = turned[j * levels : (j + 1) * levels, :]
            piece = jnp.concatenate([piece] * (lanes // 128), axis=1)
            group = lax.broadcasted_iota(jnp.int32, piece.shape, 1) // width
            total = jnp.where(group == j, piece, total)
        hess_refs[c][...] = total
        for tile in range(lanes // 128):
            for b in range(0, levels, step):
                rows = []
                for jj in range(per_tile):
                    bin_at = (tile * per_tile + jj) * levels + b
                    rows.append(parent_ref[c * width : (c + 1) * width, bin_at * kdim : bin_at * kdim + 128])
                block = jnp.concatenate(rows, axis=0) if per_tile > 1 else rows[0]
                grad_refs[c][b * kdim : b * kdim + 128, tile * 128 : (tile + 1) * 128] = block.T


def parent_layout(width, levels, lanes, kdim, chunks, line, child_owner, owners, signs, parent, hess, tie):
    shapes = [jax.ShapeDtypeStruct((levels * kdim, lanes), jnp.float32)] * chunks
    shapes += [jax.ShapeDtypeStruct((levels, lanes), jnp.float32)] * chunks
    shapes += [jax.ShapeDtypeStruct((8, lanes), jnp.int32)] * chunks
    shapes += [jax.ShapeDtypeStruct((8, 128), jnp.int32)]
    out = pl.pallas_call(
        functools.partial(layout_kernel, width, levels, kdim, chunks, line),
        in_specs=[SMEM_SPEC] * 2 + [VMEM_SPEC] * 3 + [pl.BlockSpec(memory_space=pl.ANY)],
        out_specs=[VMEM_SPEC] * (3 * chunks + 1),
        out_shape=shapes,
        compiler_params=pltpu.CompilerParams(vmem_limit_bytes=16 * MIB),
        cost_estimate=pl.CostEstimate(flops=0, bytes_accessed=2 * parent.size * 4, transcendentals=0),
        name="parent_layout",
    )(child_owner, owners, signs.reshape(1, -1), parent, hess, tie)
    return out[:chunks], out[chunks : 2 * chunks], out[2 * chunks : 3 * chunks], out[-1]


def lane_prefix(total, width):
    lanes = total.shape[1]
    lane = lax.broadcasted_iota(jnp.int32, total.shape, 1)
    running = total
    reach = width
    while reach < lanes:
        running = running + jnp.where(lane >= reach, pltpu.roll(running, reach, 1), 0.0)
        reach *= 2
    whole = total
    reach = width
    while reach < lanes:
        whole = whole + pltpu.roll(whole, reach, 1)
        reach *= 2
    return running - total, running, whole


def gain_kernel(width, levels, kdim, last_ref, right_ref, left_ref, par_grad_ref, par_hess_ref, sign_ref, low_ref, high_ref, out_ref, grad_ref, hess_ref):
    hess_at = levels * kdim
    lanes = out_ref.shape[2]

    def small_at(start, size):
        return last_ref[pl.ds(start, size), :] + right_ref[pl.ds(start, size), :] + left_ref[pl.ds(start, size), :]

    sign = sign_ref[:1, :]
    small_hess = small_at(hess_at, levels)
    hess_ref[0] = small_hess
    hess_ref[1] = par_hess_ref[...] - small_hess

    def add_up(b, carry):
        g0, g1, h0, h1 = carry
        start = pl.multiple_of(b * kdim, kdim)
        small = small_at(start, kdim)
        g0 = g0 + small
        g1 = g1 + (par_grad_ref[pl.ds(start, kdim), :] - small)
        h0 = h0 + hess_ref[0, pl.ds(b, 1), :]
        h1 = h1 + hess_ref[1, pl.ds(b, 1), :]
        grad_ref[0, pl.ds(start, kdim), :] = g0
        grad_ref[1, pl.ds(start, kdim), :] = g1
        hess_ref[0, pl.ds(b, 1), :] = h0
        hess_ref[1, pl.ds(b, 1), :] = h1
        return g0, g1, h0, h1

    zero_g = jnp.zeros((kdim, lanes), jnp.float32)
    zero_h = jnp.zeros((1, lanes), jnp.float32)
    ends = lax.fori_loop(0, levels, add_up, (zero_g, zero_g, zero_h, zero_h))
    for c in range(2):
        low = low_ref[c].astype(jnp.float32) / 1024.0
        high = high_ref[c].astype(jnp.float32) / 1024.0
        middle = 0.5 * (low + high)
        low_left = jnp.where(sign < 0, middle, low)
        high_left = jnp.where(sign > 0, middle, high)
        low_right = jnp.where(sign > 0, middle, low)
        high_right = jnp.where(sign < 0, middle, high)
        grad_before, _, grad_all = lane_prefix(ends[c], width)
        hess_rows = jnp.broadcast_to(ends[2 + c], (8, lanes))
        hess_before, _, hess_all = lane_prefix(hess_rows, width)
        hess_before, hess_all = hess_before[:1], hess_all[:1]

        def score(grad, hess, lower, upper):
            denom = jnp.maximum(hess, 0.0) + reg_lambda
            weight = jnp.clip(-grad / denom, lower, upper)
            return jnp.sum((2.0 * grad + denom * weight) * weight, axis=0, keepdims=True)

        def one_bin(b, carry):
            start = pl.multiple_of(b * kdim, kdim)
            grad_left = grad_ref[c, pl.ds(start, kdim), :] + grad_before
            hess_left = hess_ref[c, pl.ds(b, 1), :] + hess_before
            left = score(grad_left, hess_left, low_left, high_left)
            right = score(grad_all - grad_left, hess_all - hess_left, low_right, high_right)
            out_ref[c, pl.ds(b, 1), :] = (left + right) * (-1.0 / kdim)
            return carry

        lax.fori_loop(0, levels, one_bin, 0)


def gains_of(width, levels, lanes, kdim, last, right, left, par_grad, par_hess, sign, node_low, node_high):
    return pl.pallas_call(
        functools.partial(gain_kernel, width, levels, kdim),
        in_specs=[VMEM_SPEC] * 6 + [SMEM_SPEC] * 2,
        out_specs=VMEM_SPEC,
        out_shape=jax.ShapeDtypeStruct((2, levels, lanes), jnp.float32),
        scratch_shapes=[
            pltpu.VMEM((2, levels * kdim, lanes), jnp.float32),
            pltpu.VMEM((2, levels, lanes), jnp.float32),
        ],
        compiler_params=pltpu.CompilerParams(vmem_limit_bytes=24 * MIB),
        cost_estimate=pl.CostEstimate(flops=50 * levels * kdim * lanes, bytes_accessed=16 * levels * kdim * lanes, transcendentals=0),
        name="gains",
    )(last, right, left, par_grad, par_hess, sign, node_low, node_high)


def chosen(shift, got):
    value = got[0]
    for s in range(1, len(got)):
        value = jnp.where(shift == s, got[s], value)
    return value


def finish_kernel(width, *refs):
    out_ref = refs[-1]
    chunks = len(refs) - 1
    slab = width * chunks
    lanes = refs[0].shape[2]
    total = jnp.zeros((128, 128), jnp.float32)
    column = lax.broadcasted_iota(jnp.int32, (128, 128), 1)
    for child in range(2):
        for c in range(chunks):
            gain = refs[c][child]
            at = child * slab + c * width
            pieces = []
            for j in range(lanes // width):
                turn = (at - j * width) % lanes
                turned = pltpu.roll(gain, turn, 1) if turn else gain
                pieces.append(turned[:, :128])
            stack = jnp.concatenate(pieces, axis=0)
            total = jnp.where((column >= at) & (column < at + width), stack, total)
    turned = total.T
    for child in range(2):
        out_ref[:, child, :] = turned[child * slab : (child + 1) * slab]


def finish(width, nbins, parts):
    return pl.pallas_call(
        functools.partial(finish_kernel, width),
        in_specs=[VMEM_SPEC] * len(parts),
        out_specs=VMEM_SPEC,
        out_shape=jax.ShapeDtypeStruct((width * len(parts), 2, nbins), jnp.float32),
        name="finish",
    )(*parts)


def one_of(z, members):
    hit = z == members[0]
    for m in members[1:]:
        hit = hit | (z == m)
    return hit


def sum_line(line, chunks, units, unit, set_up):
    plan = plan_of(line)
    z = lax.axis_index("dp")
    from_left = [None] * chunks
    from_right = [None] * chunks
    arrived = []

    def pick(kind, step, c):
        where_at = {}
        for zz in range(line):
            for p, role in enumerate(plan[zz]):
                if role[:2] == (kind, step):
                    where_at.setdefault(p, []).append(zz)
        spots = sorted(where_at)
        value = units[spots[0], c]
        for p in spots[1:]:
            value = jnp.where(one_of(z, where_at[p]), units[p, c], value)
        return value

    def tie_of(step, c):
        at = min(step * chunks + c - 3, (line - 2) * chunks - 1)
        return (arrived[at],) if at >= 0 else (units[0, chunks - 1],)

    last = line - 1
    for step in range(last):
        for c in range(chunks):
            if step > 0:
                units[step, c] = unit(step, c, tie_of(step, c))
            to_right = pick("R", step, c)
            to_left = pick("L", step, c)
            if step > 0:
                to_right = to_right + from_left[c]
                to_left = to_left + from_right[c]
            from_left[c] = lax.ppermute(to_right, "dp", [(i, i + 1) for i in range(step + 1)])
            from_right[c] = lax.ppermute(to_left, "dp", [(line - 1 - i, line - 2 - i) for i in range(step + 1)])
            arrived.append(from_left[c])
    layout = set_up(tie_of(last, 0)[0])
    return [unit(last, c, tie_of(last, c)) for c in range(chunks)], from_left, from_right, layout


def sum_line_of_4(line, chunks, units, unit, set_up):
    inward, outer, middle = [(0, 1), (3, 2)], [(0, 1), (1, 0), (2, 3), (3, 2)], [(1, 2), (2, 1)]
    every = range(chunks)
    a0 = [lax.ppermute(units[0, c], "dp", inward) for c in every]
    a1, b1, a2, b2 = [None] * chunks, [None] * chunks, [None] * chunks, [None] * chunks
    for c in every:
        units[1, c] = unit(1, c, (a0[c - 1],) if c else (units[0, chunks - 1],))
        a1[c] = lax.ppermute(units[1, c], "dp", inward)
        b1[c] = lax.ppermute(units[0, c] + a0[c], "dp", middle)
    last = [None] * chunks
    last[0] = unit(3, 0, (a0[chunks - 1],))
    for c in every:
        units[2, c] = unit(2, c, (a1[0],))
        b2[c] = lax.ppermute(units[1, c] + a1[c], "dp", middle)
        a2[c] = lax.ppermute(units[2, c] + b1[c], "dp", outer)
    layout = set_up(a1[chunks - 1])
    for c in range(1, chunks):
        last[c] = unit(3, c, (a1[chunks - 1],))
    return last, a2, b2, layout


def per_device(bins, grads, hess, node_side, signs, child_owner, parent_owner, parent_grad, parent_hess, node_low, node_high):
    line = lax.axis_size("dp")
    kdim = grads.shape[1]
    nbins = parent_hess.shape[2]
    slab = parent_grad.shape[1]
    chunks = CHUNKS if slab >= 32 else 1
    width = slab // chunks
    lanes = min(256, width * nbins * kdim // 128)
    levels = nbins // (lanes // width)

    own, send, wt, wt_send = prep(line, slab, parent_owner, bins, grads, hess, node_side)
    swap = [(0, 1), (1, 0)]
    wt_other = lax.ppermute(wt_send, "sub", swap)
    other = lax.ppermute(send, "sub", swap)
    mine = (own, wt)
    theirs = (other, wt_other)

    def unit(p, c, pairs, init=None, tie=()):
        return hist(p * slab + c * width, width, levels, lanes, kdim, pairs, init, tie)

    def set_up(tie):
        return parent_layout(
            width, levels, lanes, kdim, chunks, line, child_owner, parent_owner, signs, parent_grad[0], parent_hess[0], tie
        )

    units = {}
    for c in range(chunks):
        units[0, c] = unit(0, c, [mine])
    for c in range(chunks):
        units[0, c] = unit(0, c, [theirs], units[0, c], (units[0, c - 1],) if c else ())
    collect = sum_line_of_4 if line == 4 else sum_line
    last, from_left, from_right, layout = collect(line, chunks, units, lambda p, c, tie: unit(p, c, [mine, theirs], tie=tie), set_up)
    par_grad, par_hess, sign, route = layout

    done = []
    for c in range(chunks):
        gain = gains_of(
            width, levels, lanes, kdim, last[c], from_left[c], from_right[c], par_grad[c], par_hess[c], sign[c], node_low, node_high
        )
        got = [gain] + [lax.ppermute(gain, "dp", [(i, (i + s) % line) for i in range(line)]) for s in range(1, line)]
        crossed = lax.ppermute(chosen(route[1, 0], got), "sub", swap)
        done.append(jnp.where(route[2, 0] == 1, chosen(route[0, 0], got), crossed))
    return finish(width, nbins, done)[None]


def solution(mesh):
    return jax.shard_map(
        per_device,
        mesh=mesh,
        in_specs=(
            P(("groups", "dp", "sub"), "feat"),
            P(("groups", "dp", "sub"), None),
            P(("groups", "dp", "sub")),
            P(("groups", "dp", "sub")),
            P("groups"),
            P("groups"),
            P("groups"),
            P(("groups", "dp", "sub"), "feat", None),
            P(("groups", "dp", "sub"), "feat", None),
            P("groups"),
            P("groups"),
        ),
        out_specs=P(("groups", "dp", "sub"), "feat", None, None),
        check_vma=False,
    )
```

```python
import functools

import jax
import jax.numpy as jnp
from jax import lax
from jax.experimental import pallas as pl
from jax.experimental.pallas import tpu as pltpu
from jax.sharding import PartitionSpec as P

reg_lambda = 1.0
CHUNKS = 2
TILE = 256
PACK = 128
FAST = 9
PREP_MIB = 56
MIB = 1024 * 1024
VMEM_SPEC = pl.BlockSpec(memory_space=pltpu.VMEM)
SMEM_SPEC = pl.BlockSpec(memory_space=pltpu.SMEM)


def plan_of(line):
    roles = []
    for z in range(line):
        mine = []
        for step in range(line - 1):
            now = []
            if z <= step:
                now.append(("R", step, line - 1 - step + z))
            if line - 1 - z <= step:
                now.append(("L", step, step - (line - 1 - z)))
            mine.extend(now if 2 * z < line else now[::-1])
        mine.append(("F", line - 1, z))
        roles.append(mine)
    return roles


def prep_kernel(line, slab, owner_ref, bins_ref, grads_ref, hess_ref, side_ref, own_ref, send_ref, wt_ref, wt_send_ref, buf_ref, sems, acc_ref, acc_w_ref):
    rows, f_dev = bins_ref.shape
    half = f_dev // 2
    kdim = grads_ref.shape[0]
    reach = TILE + PACK
    blocks = rows // TILE
    copies = []
    for i in range(blocks):
        part = pl.ds(i * TILE, TILE)
        copies.append(pltpu.make_async_copy(bins_ref.at[part, :], buf_ref.at[part, :], sems.at[i]))
        copies[-1].start()

    hess_row = hess_ref[...].astype(jnp.float32).reshape(1, rows)
    ones = [jnp.where(side_ref[:, i * TILE : (i + 1) * TILE] == 1, 1.0, 0.0) for i in range(blocks)]
    counts = [jnp.sum(x).astype(jnp.int32) for x in ones]
    bases = [jnp.int32(0)]
    for count in counts:
        bases.append(bases[-1] + count)
    starts = [pl.multiple_of((base // PACK) * PACK, PACK) for base in bases]
    marks = jnp.concatenate(ones, axis=0)
    before = lax.broadcasted_iota(jnp.int32, (TILE, TILE), 0) < lax.broadcasted_iota(jnp.int32, (TILE, TILE), 1)
    before = jnp.where(before, 1.0, 0.0).astype(jnp.bfloat16)
    ahead = jnp.dot(marks.astype(jnp.bfloat16), before, preferred_element_type=jnp.float32).astype(jnp.int32)
    slot = lax.broadcasted_iota(jnp.int32, (reach, TILE), 0)
    acc_ref[:PACK, :] = jnp.zeros((PACK, f_dev), jnp.bfloat16)
    acc_w_ref[:, :PACK] = jnp.zeros((acc_w_ref.shape[0], PACK), jnp.float32)

    z, core = lax.axis_index("dp"), lax.axis_index("sub")
    column = lax.broadcasted_iota(jnp.int32, (1, f_dev), 1)
    position = lax.rem(column, half) // slab
    table = plan_of(line)
    chip = jnp.zeros_like(column)
    for p in range(line):
        target = jnp.int32(0)
        for zz in range(line):
            target = jnp.where(z == zz, jnp.int32(table[zz][p][2]), target)
        chip = jnp.where(position == p, target, chip)
    owner = 2 * chip + jnp.where(column < half, core, 1 - core)
    source = jnp.zeros_like(column)
    for q in range(2 * line):
        source = jnp.where(owner == owner_ref[q], q, source)
    source = source * slab + lax.rem(column, slab)
    perm = jnp.where(lax.broadcasted_iota(jnp.int32, (f_dev, f_dev), 0) == source, 1.0, 0.0).astype(jnp.bfloat16)

    for i in range(blocks):
        part = slice(i * TILE, (i + 1) * TILE)
        goal = jnp.where(ones[i] > 0.5, ahead[i : i + 1] + (bases[i] - starts[i]), -1)
        pack = jnp.where(slot == goal, 1.0, 0.0).astype(jnp.bfloat16)
        hess = jnp.broadcast_to(hess_row[:, part], (16, TILE))
        first = lax.broadcasted_iota(jnp.int32, hess.shape, 0) == 0
        weights = jnp.concatenate([grads_ref[:, part].astype(jnp.float32), jnp.where(first, hess, 0.0)], axis=0)
        packed_w = lax.dot_general(weights.astype(jnp.bfloat16), pack, (((1,), (1,)), ((), ())), preferred_element_type=jnp.float32)
        acc_w_ref[:, pl.ds(starts[i], PACK)] += packed_w[:, :PACK]
        acc_w_ref[:, pl.ds(starts[i] + PACK, TILE)] = packed_w[:, PACK:]
        copies[i].wait()
        binned = buf_ref[part, :].astype(jnp.float32).astype(jnp.bfloat16)
        packed = jnp.dot(pack, binned, preferred_element_type=jnp.float32).astype(jnp.bfloat16)
        acc_ref[pl.ds(starts[i], PACK), :] += packed[:PACK]
        acc_ref[pl.ds(starts[i] + PACK, TILE), :] = packed[PACK:]

    def move(t, carry):
        part = pl.ds(pl.multiple_of(t * TILE, TILE), TILE)
        moved = jnp.dot(acc_ref[part, :], perm, preferred_element_type=jnp.float32)
        own_ref[part, :] = moved[:, :half].astype(jnp.bfloat16)
        send_ref[part, :] = moved[:, half:]
        return carry

    total = bases[blocks]
    lax.fori_loop(0, (total + TILE - 1) // TILE, move, 0)
    lane = lax.broadcasted_iota(jnp.int32, (acc_w_ref.shape[0], rows), 1)
    row = lax.broadcasted_iota(jnp.int32, lane.shape, 0)
    packed = jnp.where(lane < total, acc_w_ref[:, :rows], 0.0)
    packs = ((total + PACK - 1) // PACK).astype(jnp.float32)
    packed = jnp.where(row == kdim + 1, packs, packed)
    wt_ref[...] = packed.astype(jnp.bfloat16)
    wt_send_ref[...] = packed[: kdim + 8]


def prep(line, slab, owners, bins, grads, hess, side):
    rows, f_dev = bins.shape
    kdim = grads.shape[1]
    half = f_dev // 2
    return pl.pallas_call(
        functools.partial(prep_kernel, line, slab),
        in_specs=[SMEM_SPEC, pl.BlockSpec(memory_space=pl.ANY), VMEM_SPEC, VMEM_SPEC, VMEM_SPEC],
        out_specs=[VMEM_SPEC] * 4,
        out_shape=[
            jax.ShapeDtypeStruct((rows, half), jnp.bfloat16),
            jax.ShapeDtypeStruct((rows, half), jnp.float32),
            jax.ShapeDtypeStruct((kdim + 16, rows), jnp.bfloat16),
            jax.ShapeDtypeStruct((kdim + 8, rows), jnp.float32),
        ],
        scratch_shapes=[
            pltpu.VMEM((rows, f_dev), jnp.int32),
            pltpu.SemaphoreType.DMA((rows // TILE,)),
            pltpu.VMEM((rows + TILE + PACK, f_dev), jnp.bfloat16),
            pltpu.VMEM((kdim + 16, rows + TILE + PACK), jnp.float32),
        ],
        compiler_params=pltpu.CompilerParams(vmem_limit_bytes=PREP_MIB * MIB),
        cost_estimate=pl.CostEstimate(flops=4 * rows * f_dev * f_dev, bytes_accessed=8 * rows * f_dev, transcendentals=0),
        name="prep",
    )(owners, bins, grads.T, hess, side.reshape(1, rows))


def tiles_in(wt_ref, kdim):
    return jnp.max(wt_ref[:, :128].astype(jnp.float32)[kdim + 1 : kdim + 2]).astype(jnp.int32)


def hist_kernel(first_column, width, levels, parts, kdim, has_init, *refs):
    pairs = [refs[2 * i : 2 * i + 2] for i in range(parts)]
    init_ref = refs[2 * parts] if has_init else None
    out_ref, rel_ref, wt_ref = refs[-3:]
    lanes = out_ref.shape[1]
    rows, half = pairs[0][0].shape
    src = lax.broadcasted_iota(jnp.int32, (half, lanes), 0)
    dst = lax.broadcasted_iota(jnp.int32, (half, lanes), 1)
    spread = jnp.where(src == first_column + lax.rem(dst, width), 1.0, 0.0).astype(jnp.bfloat16)
    lane = lax.broadcasted_iota(jnp.int32, (1, lanes), 1)
    shift = ((lane // width) * levels).astype(jnp.float32)
    one = jnp.ones((TILE, lanes), jnp.bfloat16)
    zero = jnp.zeros((TILE, lanes), jnp.bfloat16)

    def place_rows(bins_ref, source, target, size):
        block = bins_ref[pl.ds(source, size), :].astype(jnp.bfloat16)
        moved = jnp.dot(block, spread, preferred_element_type=jnp.float32)
        rel_ref[pl.ds(target, size), :] = (moved - shift).astype(jnp.bfloat16)

    def place_weights(height):
        for i, (_, w_ref) in enumerate(pairs):
            weights = w_ref[:, :height]
            if w_ref.dtype != jnp.bfloat16:
                weights = jnp.concatenate([weights, jnp.zeros((8, height), jnp.float32)], axis=0).astype(jnp.bfloat16)
            wt_ref[:, i * height : (i + 1) * height] = weights

    def sums_of(b, tiles):
        value = jnp.full((TILE, lanes), b.astype(jnp.float32), jnp.float32).astype(jnp.bfloat16)
        total = jnp.zeros((wt_ref.shape[0], lanes), jnp.float32)
        for first, size in tiles:
            hit = rel_ref[pl.ds(first, size), :] == value[:size]
            onehot = jnp.where(hit, one[:size], zero[:size])
            total = total + jnp.dot(wt_ref[:, pl.ds(first, size)], onehot, preferred_element_type=jnp.float32)
        return total[:kdim], total[kdim : kdim + 1]

    def spots_of(b):
        return pl.ds(pl.multiple_of(b * kdim, kdim), kdim), pl.ds(levels * kdim + b, 1)

    def fast():
        height = FAST * PACK
        for i, (bins_ref, _) in enumerate(pairs):
            for r in range(0, height, 3 * PACK):
                place_rows(bins_ref, r, i * height + r, 3 * PACK)
        place_weights(height)
        tiles = [(r, min(TILE, parts * height - r)) for r in range(0, parts * height, TILE)]

        def level(b, carry):
            grad, hess = sums_of(b, tiles)
            grad_spot, hess_spot = spots_of(b)
            if has_init:
                grad, hess = grad + init_ref[grad_spot, :], hess + init_ref[hess_spot, :]
            out_ref[grad_spot, :] = grad
            out_ref[hess_spot, :] = hess
            return carry

        lax.fori_loop(0, levels, level, 0)

    def general():
        for i, (bins_ref, _) in enumerate(pairs):

            def one_pack(p, carry):
                r = pl.multiple_of(p * PACK, PACK)
                place_rows(bins_ref, r, i * rows + r, PACK)
                return carry

            lax.fori_loop(0, rows // PACK, one_pack, 0)
        place_weights(rows)
        out_ref[...] = init_ref[...] if has_init else jnp.zeros(out_ref.shape, jnp.float32)
        step = 2 * TILE

        def group(g, carry):
            first = pl.multiple_of(g * step, step)

            def level(b, carry):
                grad, hess = sums_of(b, [(first, TILE), (first + TILE, TILE)])
                grad_spot, hess_spot = spots_of(b)
                out_ref[grad_spot, :] += grad
                out_ref[hess_spot, :] += hess
                return carry

            return lax.fori_loop(0, levels, level, carry)

        lax.fori_loop(0, parts * rows // step, group, 0)

    needed = tiles_in(pairs[0][1], kdim)
    for _, w_ref in pairs[1:]:
        needed = jnp.maximum(needed, tiles_in(w_ref, kdim))
    if FAST * PACK < rows:
        pl.when(needed <= FAST)(fast)
        pl.when(needed > FAST)(general)
    else:
        general()


def hist(first_column, width, levels, lanes, kdim, pairs, init=None, tie=()):
    rows = pairs[0][0].shape[0]
    parts = len(pairs)
    operands = [x for pair in pairs for x in pair]
    if init is not None:
        operands.append(init)
    specs = [VMEM_SPEC] * len(operands) + [pl.BlockSpec(memory_space=pl.ANY)] * len(tie)
    height = levels * (kdim + 1)
    return pl.pallas_call(
        functools.partial(hist_kernel, first_column, width, levels, parts, kdim, init is not None),
        in_specs=specs,
        out_specs=VMEM_SPEC,
        out_shape=jax.ShapeDtypeStruct((height, lanes), jnp.float32),
        scratch_shapes=[
            pltpu.VMEM((parts * rows, lanes), jnp.bfloat16),
            pltpu.VMEM((kdim + 16, parts * rows), jnp.bfloat16),
        ],
        compiler_params=pltpu.CompilerParams(vmem_limit_bytes=20 * MIB),
        cost_estimate=pl.CostEstimate(
            flops=parts * rows * lanes, bytes_accessed=parts * rows * lanes, transcendentals=0
        ),
        name="hist",
    )(*operands, *tie)


def source_of(place, child_ref, parent_ref):
    source = jnp.int32(0)
    for q in range(child_ref.shape[0]):
        source = jnp.where(child_ref[q] == place, parent_ref[q], source)
    return source


def repeat_lanes(x, width, lanes):
    if lanes > x.shape[1]:
        x = jnp.concatenate([x] * (lanes // x.shape[1]), axis=1)
    x = jnp.where(lax.broadcasted_iota(jnp.int32, x.shape, 1) < width, x[:, :lanes], 0)
    reach = width
    while reach < lanes:
        x = x + pltpu.roll(x, reach, 1)
        reach *= 2
    return x


def layout_kernel(width, levels, kdim, chunks, line, child_ref, owner_ref, sign_ref, parent_ref, hess_ref, tie_ref, *out_refs):
    del tie_ref
    grad_refs, hess_refs, sign_refs = out_refs[:chunks], out_refs[chunks : 2 * chunks], out_refs[2 * chunks : 3 * chunks]
    lanes = grad_refs[0].shape[1]
    slab = width * chunks
    owners = owner_ref.shape[0]
    z, core = lax.axis_index("dp"), lax.axis_index("sub")
    place = 2 * z + core
    mine = source_of(place, child_ref, owner_ref)
    twin = source_of(2 * z + 1 - core, child_ref, owner_ref)
    row = lax.broadcasted_iota(jnp.int32, (8, 128), 0)
    route = jnp.where(row == 0, lax.rem(z - mine // 2 + line, line), lax.rem(z - twin // 2 + line, line))
    out_refs[-1][...] = jnp.where(row == 2, jnp.where(lax.rem(mine, 2) == core, 1, 0), route)
    slab_at = jnp.int32(0)
    for q in range(owners):
        slab_at = jnp.where(owner_ref[q] == place, q, slab_at)
    offset = lax.axis_index("feat") * (owners * slab) + slab_at * slab
    features = sign_ref.shape[1]
    signs = jnp.broadcast_to(sign_ref[...], (8, features))
    per_tile = 128 // width
    step = 128 // kdim
    for c in range(chunks):
        turned = pltpu.roll(signs, lax.rem(features - offset - c * width + features, features), 1)
        sign_refs[c][...] = repeat_lanes(turned[:, :128], width, lanes)
        rows = hess_ref[c * width : (c + 1) * width, :]
        turned = jnp.concatenate([rows] * (128 // width), axis=0).T
        total = jnp.zeros((levels, lanes), jnp.float32)
        for j in range(lanes // width):
            piece = turned[j * levels : (j + 1) * levels, :]
            piece = jnp.concatenate([piece] * (lanes // 128), axis=1)
            group = lax.broadcasted_iota(jnp.int32, piece.shape, 1) // width
            total = jnp.where(group == j, piece, total)
        hess_refs[c][...] = total
        for tile in range(lanes // 128):
            for b in range(0, levels, step):
                rows = []
                for jj in range(per_tile):
                    bin_at = (tile * per_tile + jj) * levels + b
                    rows.append(parent_ref[c * width : (c + 1) * width, bin_at * kdim : bin_at * kdim + 128])
                block = jnp.concatenate(rows, axis=0) if per_tile > 1 else rows[0]
                grad_refs[c][b * kdim : b * kdim + 128, tile * 128 : (tile + 1) * 128] = block.T


def parent_layout(width, levels, lanes, kdim, chunks, line, child_owner, owners, signs, parent, hess, tie):
    shapes = [jax.ShapeDtypeStruct((levels * kdim, lanes), jnp.float32)] * chunks
    shapes += [jax.ShapeDtypeStruct((levels, lanes), jnp.float32)] * chunks
    shapes += [jax.ShapeDtypeStruct((8, lanes), jnp.int32)] * chunks
    shapes += [jax.ShapeDtypeStruct((8, 128), jnp.int32)]
    out = pl.pallas_call(
        functools.partial(layout_kernel, width, levels, kdim, chunks, line),
        in_specs=[SMEM_SPEC] * 2 + [VMEM_SPEC] * 3 + [pl.BlockSpec(memory_space=pl.ANY)],
        out_specs=[VMEM_SPEC] * (3 * chunks + 1),
        out_shape=shapes,
        compiler_params=pltpu.CompilerParams(vmem_limit_bytes=16 * MIB),
        cost_estimate=pl.CostEstimate(flops=0, bytes_accessed=2 * parent.size * 4, transcendentals=0),
        name="parent_layout",
    )(child_owner, owners, signs.reshape(1, -1), parent, hess, tie)
    return out[:chunks], out[chunks : 2 * chunks], out[2 * chunks : 3 * chunks], out[-1]


def lane_prefix(total, width):
    lanes = total.shape[1]
    lane = lax.broadcasted_iota(jnp.int32, total.shape, 1)
    running = total
    reach = width
    while reach < lanes:
        running = running + jnp.where(lane >= reach, pltpu.roll(running, reach, 1), 0.0)
        reach *= 2
    whole = total
    reach = width
    while reach < lanes:
        whole = whole + pltpu.roll(whole, reach, 1)
        reach *= 2
    return running - total, running, whole


def gain_kernel(width, levels, kdim, last_ref, right_ref, left_ref, par_grad_ref, par_hess_ref, sign_ref, low_ref, high_ref, out_ref, grad_ref, hess_ref):
    hess_at = levels * kdim
    lanes = out_ref.shape[2]

    def small_at(start, size):
        return last_ref[pl.ds(start, size), :] + right_ref[pl.ds(start, size), :] + left_ref[pl.ds(start, size), :]

    sign = sign_ref[:1, :]
    small_hess = small_at(hess_at, levels)
    hess_ref[0] = small_hess
    hess_ref[1] = par_hess_ref[...] - small_hess

    def add_up(b, carry):
        g0, g1, h0, h1 = carry
        start = pl.multiple_of(b * kdim, kdim)
        small = small_at(start, kdim)
        g0 = g0 + small
        g1 = g1 + (par_grad_ref[pl.ds(start, kdim), :] - small)
        h0 = h0 + hess_ref[0, pl.ds(b, 1), :]
        h1 = h1 + hess_ref[1, pl.ds(b, 1), :]
        grad_ref[0, pl.ds(start, kdim), :] = g0
        grad_ref[1, pl.ds(start, kdim), :] = g1
        hess_ref[0, pl.ds(b, 1), :] = h0
        hess_ref[1, pl.ds(b, 1), :] = h1
        return g0, g1, h0, h1

    zero_g = jnp.zeros((kdim, lanes), jnp.float32)
    zero_h = jnp.zeros((1, lanes), jnp.float32)
    ends = lax.fori_loop(0, levels, add_up, (zero_g, zero_g, zero_h, zero_h))
    for c in range(2):
        low = low_ref[c].astype(jnp.float32) / 1024.0
        high = high_ref[c].astype(jnp.float32) / 1024.0
        middle = 0.5 * (low + high)
        low_left = jnp.where(sign < 0, middle, low)
        high_left = jnp.where(sign > 0, middle, high)
        low_right = jnp.where(sign > 0, middle, low)
        high_right = jnp.where(sign < 0, middle, high)
        grad_before, _, grad_all = lane_prefix(ends[c], width)
        hess_rows = jnp.broadcast_to(ends[2 + c], (8, lanes))
        hess_before, _, hess_all = lane_prefix(hess_rows, width)
        hess_before, hess_all = hess_before[:1], hess_all[:1]

        def score(grad, hess, lower, upper):
            denom = jnp.maximum(hess, 0.0) + reg_lambda
            weight = jnp.clip(-grad / denom, lower, upper)
            return jnp.sum((2.0 * grad + denom * weight) * weight, axis=0, keepdims=True)

        def one_bin(b, carry):
            start = pl.multiple_of(b * kdim, kdim)
            grad_left = grad_ref[c, pl.ds(start, kdim), :] + grad_before
            hess_left = hess_ref[c, pl.ds(b, 1), :] + hess_before
            left = score(grad_left, hess_left, low_left, high_left)
            right = score(grad_all - grad_left, hess_all - hess_left, low_right, high_right)
            out_ref[c, pl.ds(b, 1), :] = (left + right) * (-1.0 / kdim)
            return carry

        lax.fori_loop(0, levels, one_bin, 0)


def gains_of(width, levels, lanes, kdim, last, right, left, par_grad, par_hess, sign, node_low, node_high):
    return pl.pallas_call(
        functools.partial(gain_kernel, width, levels, kdim),
        in_specs=[VMEM_SPEC] * 6 + [SMEM_SPEC] * 2,
        out_specs=VMEM_SPEC,
        out_shape=jax.ShapeDtypeStruct((2, levels, lanes), jnp.float32),
        scratch_shapes=[
            pltpu.VMEM((2, levels * kdim, lanes), jnp.float32),
            pltpu.VMEM((2, levels, lanes), jnp.float32),
        ],
        compiler_params=pltpu.CompilerParams(vmem_limit_bytes=24 * MIB),
        cost_estimate=pl.CostEstimate(flops=50 * levels * kdim * lanes, bytes_accessed=16 * levels * kdim * lanes, transcendentals=0),
        name="gains",
    )(last, right, left, par_grad, par_hess, sign, node_low, node_high)


def chosen(shift, got):
    value = got[0]
    for s in range(1, len(got)):
        value = jnp.where(shift == s, got[s], value)
    return value


def finish_kernel(width, *refs):
    out_ref = refs[-1]
    chunks = len(refs) - 1
    slab = width * chunks
    lanes = refs[0].shape[2]
    total = jnp.zeros((128, 128), jnp.float32)
    column = lax.broadcasted_iota(jnp.int32, (128, 128), 1)
    for child in range(2):
        for c in range(chunks):
            gain = refs[c][child]
            at = child * slab + c * width
            pieces = []
            for j in range(lanes // width):
                turn = (at - j * width) % lanes
                turned = pltpu.roll(gain, turn, 1) if turn else gain
                pieces.append(turned[:, :128])
            stack = jnp.concatenate(pieces, axis=0)
            total = jnp.where((column >= at) & (column < at + width), stack, total)
    turned = total.T
    for child in range(2):
        out_ref[:, child, :] = turned[child * slab : (child + 1) * slab]


def finish(width, nbins, parts):
    return pl.pallas_call(
        functools.partial(finish_kernel, width),
        in_specs=[VMEM_SPEC] * len(parts),
        out_specs=VMEM_SPEC,
        out_shape=jax.ShapeDtypeStruct((width * len(parts), 2, nbins), jnp.float32),
        name="finish",
    )(*parts)


def one_of(z, members):
    hit = z == members[0]
    for m in members[1:]:
        hit = hit | (z == m)
    return hit


def sum_line(line, chunks, units, unit, set_up):
    plan = plan_of(line)
    z = lax.axis_index("dp")
    from_left = [None] * chunks
    from_right = [None] * chunks
    arrived = []

    def pick(kind, step, c):
        where_at = {}
        for zz in range(line):
            for p, role in enumerate(plan[zz]):
                if role[:2] == (kind, step):
                    where_at.setdefault(p, []).append(zz)
        spots = sorted(where_at)
        value = units[spots[0], c]
        for p in spots[1:]:
            value = jnp.where(one_of(z, where_at[p]), units[p, c], value)
        return value

    def tie_of(step, c):
        at = min(step * chunks + c - 3, (line - 2) * chunks - 1)
        return (arrived[at],) if at >= 0 else (units[0, chunks - 1],)

    last = line - 1
    for step in range(last):
        for c in range(chunks):
            if step > 0:
                units[step, c] = unit(step, c, tie_of(step, c))
            to_right = pick("R", step, c)
            to_left = pick("L", step, c)
            if step > 0:
                to_right = to_right + from_left[c]
                to_left = to_left + from_right[c]
            from_left[c] = lax.ppermute(to_right, "dp", [(i, i + 1) for i in range(step + 1)])
            from_right[c] = lax.ppermute(to_left, "dp", [(line - 1 - i, line - 2 - i) for i in range(step + 1)])
            arrived.append(from_left[c])
    layout = set_up(tie_of(last, 0)[0])
    return [unit(last, c, tie_of(last, c)) for c in range(chunks)], from_left, from_right, layout


def sum_line_of_4(line, chunks, units, unit, set_up):
    inward, outer, middle = [(0, 1), (3, 2)], [(0, 1), (1, 0), (2, 3), (3, 2)], [(1, 2), (2, 1)]
    a0, a1, a2, b1, b2, last = {}, {}, {}, {}, {}, {}
    for c in range(chunks):
        a0[c] = lax.ppermute(units[0, c], "dp", inward)
    for c in range(chunks):
        units[1, c] = unit(1, c, (a0[c], units[1, c - 1] if c else units[0, chunks - 1]))
        b1[c] = lax.ppermute(units[0, c] + a0[c], "dp", middle)
        a1[c] = lax.ppermute(units[1, c], "dp", inward)
    for c in range(chunks):
        units[2, c] = unit(2, c, (a1[c], last[c - 1] if c else units[1, chunks - 1]))
        b2[c] = lax.ppermute(units[1, c] + a1[c], "dp", middle)
        a2[c] = lax.ppermute(units[2, c] + b1[c], "dp", outer)
        last[c] = unit(3, c, (units[2, c],))
    return last, a2, b2, set_up(units[2, chunks - 1])


def per_device(bins, grads, hess, node_side, signs, child_owner, parent_owner, parent_grad, parent_hess, node_low, node_high):
    line = lax.axis_size("dp")
    kdim = grads.shape[1]
    nbins = parent_hess.shape[2]
    slab = parent_grad.shape[1]
    chunks = CHUNKS if slab >= 32 else 1
    width = slab // chunks
    lanes = min(256, width * nbins * kdim // 128)
    levels = nbins // (lanes // width)

    own, send, wt, wt_send = prep(line, slab, parent_owner, bins, grads, hess, node_side)
    swap = [(0, 1), (1, 0)]
    wt_other = lax.ppermute(wt_send, "sub", swap)
    other = lax.ppermute(send, "sub", swap)
    mine = (own, wt)
    theirs = (other, wt_other)

    def unit(p, c, pairs, init=None, tie=()):
        return hist(p * slab + c * width, width, levels, lanes, kdim, pairs, init, tie)

    def set_up(tie):
        return parent_layout(
            width, levels, lanes, kdim, chunks, line, child_owner, parent_owner, signs, parent_grad[0], parent_hess[0], tie
        )

    units = {}
    units[0, 0] = unit(0, 0, [theirs], unit(0, 0, [mine]))
    for c in range(1, chunks):
        units[0, c] = unit(0, c, [mine, theirs], tie=(units[0, c - 1],))
    collect = sum_line_of_4 if line == 4 else sum_line
    last, from_left, from_right, layout = collect(line, chunks, units, lambda p, c, tie: unit(p, c, [mine, theirs], tie=tie), set_up)
    par_grad, par_hess, sign, route = layout

    done = []
    for c in range(chunks):
        gain = gains_of(
            width, levels, lanes, kdim, last[c], from_left[c], from_right[c], par_grad[c], par_hess[c], sign[c], node_low, node_high
        )
        got = [gain] + [lax.ppermute(gain, "dp", [(i, (i + s) % line) for i in range(line)]) for s in range(1, line)]
        crossed = lax.ppermute(chosen(route[1, 0], got), "sub", swap)
        done.append(jnp.where(route[2, 0] == 1, chosen(route[0, 0], got), crossed))
    return finish(width, nbins, done)[None]


def solution(mesh):
    return jax.shard_map(
        per_device,
        mesh=mesh,
        in_specs=(
            P(("groups", "dp", "sub"), "feat"),
            P(("groups", "dp", "sub"), None),
            P(("groups", "dp", "sub")),
            P(("groups", "dp", "sub")),
            P("groups"),
            P("groups"),
            P("groups"),
            P(("groups", "dp", "sub"), "feat", None),
            P(("groups", "dp", "sub"), "feat", None),
            P("groups"),
            P("groups"),
        ),
        out_specs=P(("groups", "dp", "sub"), "feat", None, None),
        check_vma=False,
    )
```

```python
import functools

import jax
import jax.numpy as jnp
from jax import lax
from jax.experimental import pallas as pl
from jax.experimental.pallas import tpu as pltpu
from jax.sharding import PartitionSpec as P

reg_lambda = 1.0
CHUNKS = 2
TILE = 256
PACK = 128
FAST = 9
PREP_MIB = 56
MIB = 1024 * 1024
VMEM_SPEC = pl.BlockSpec(memory_space=pltpu.VMEM)
SMEM_SPEC = pl.BlockSpec(memory_space=pltpu.SMEM)


def plan_of(line):
    roles = []
    for z in range(line):
        mine = []
        for step in range(line - 1):
            now = []
            if z <= step:
                now.append(("R", step, line - 1 - step + z))
            if line - 1 - z <= step:
                now.append(("L", step, step - (line - 1 - z)))
            mine.extend(now if 2 * z < line else now[::-1])
        mine.append(("F", line - 1, z))
        roles.append(mine)
    return roles


def prep_kernel(line, slab, owner_ref, bins_ref, grads_ref, hess_ref, side_ref, own_ref, send_ref, wt_ref, wt_send_ref, buf_ref, sems, acc_ref, acc_w_ref):
    rows, f_dev = bins_ref.shape
    half = f_dev // 2
    kdim = grads_ref.shape[0]
    reach = TILE + PACK
    blocks = rows // TILE
    copies = []
    for i in range(blocks):
        part = pl.ds(i * TILE, TILE)
        copies.append(pltpu.make_async_copy(bins_ref.at[part, :], buf_ref.at[part, :], sems.at[i]))
        copies[-1].start()

    hess_row = hess_ref[...].astype(jnp.float32).reshape(1, rows)
    ones = [jnp.where(side_ref[:, i * TILE : (i + 1) * TILE] == 1, 1.0, 0.0) for i in range(blocks)]
    counts = [jnp.sum(x).astype(jnp.int32) for x in ones]
    bases = [jnp.int32(0)]
    for count in counts:
        bases.append(bases[-1] + count)
    starts = [pl.multiple_of((base // PACK) * PACK, PACK) for base in bases]
    marks = jnp.concatenate(ones, axis=0)
    before = lax.broadcasted_iota(jnp.int32, (TILE, TILE), 0) < lax.broadcasted_iota(jnp.int32, (TILE, TILE), 1)
    before = jnp.where(before, 1.0, 0.0).astype(jnp.bfloat16)
    ahead = jnp.dot(marks.astype(jnp.bfloat16), before, preferred_element_type=jnp.float32).astype(jnp.int32)
    slot = lax.broadcasted_iota(jnp.int32, (reach, TILE), 0)
    acc_ref[:PACK, :] = jnp.zeros((PACK, f_dev), jnp.bfloat16)
    acc_w_ref[:, :PACK] = jnp.zeros((acc_w_ref.shape[0], PACK), jnp.float32)

    z, core = lax.axis_index("dp"), lax.axis_index("sub")
    column = lax.broadcasted_iota(jnp.int32, (1, f_dev), 1)
    position = lax.rem(column, half) // slab
    table = plan_of(line)
    chip = jnp.zeros_like(column)
    for p in range(line):
        target = jnp.int32(0)
        for zz in range(line):
            target = jnp.where(z == zz, jnp.int32(table[zz][p][2]), target)
        chip = jnp.where(position == p, target, chip)
    owner = 2 * chip + jnp.where(column < half, core, 1 - core)
    source = jnp.zeros_like(column)
    for q in range(2 * line):
        source = jnp.where(owner == owner_ref[q], q, source)
    source = source * slab + lax.rem(column, slab)
    perm = jnp.where(lax.broadcasted_iota(jnp.int32, (f_dev, f_dev), 0) == source, 1.0, 0.0).astype(jnp.bfloat16)

    for i in range(blocks):
        part = slice(i * TILE, (i + 1) * TILE)
        goal = jnp.where(ones[i] > 0.5, ahead[i : i + 1] + (bases[i] - starts[i]), -1)
        pack = jnp.where(slot == goal, 1.0, 0.0).astype(jnp.bfloat16)
        hess = jnp.broadcast_to(hess_row[:, part], (16, TILE))
        first = lax.broadcasted_iota(jnp.int32, hess.shape, 0) == 0
        weights = jnp.concatenate([grads_ref[:, part].astype(jnp.float32), jnp.where(first, hess, 0.0)], axis=0)
        packed_w = lax.dot_general(weights.astype(jnp.bfloat16), pack, (((1,), (1,)), ((), ())), preferred_element_type=jnp.float32)
        acc_w_ref[:, pl.ds(starts[i], PACK)] += packed_w[:, :PACK]
        acc_w_ref[:, pl.ds(starts[i] + PACK, TILE)] = packed_w[:, PACK:]
        copies[i].wait()
        binned = buf_ref[part, :].astype(jnp.float32).astype(jnp.bfloat16)
        packed = jnp.dot(pack, binned, preferred_element_type=jnp.float32).astype(jnp.bfloat16)
        acc_ref[pl.ds(starts[i], PACK), :] += packed[:PACK]
        acc_ref[pl.ds(starts[i] + PACK, TILE), :] = packed[PACK:]

    def move(t, carry):
        part = pl.ds(pl.multiple_of(t * TILE, TILE), TILE)
        moved = jnp.dot(acc_ref[part, :], perm, preferred_element_type=jnp.float32)
        own_ref[part, :] = moved[:, :half].astype(jnp.bfloat16)
        send_ref[part, :] = moved[:, half:]
        return carry

    total = bases[blocks]
    lax.fori_loop(0, (total + TILE - 1) // TILE, move, 0)
    lane = lax.broadcasted_iota(jnp.int32, (acc_w_ref.shape[0], rows), 1)
    row = lax.broadcasted_iota(jnp.int32, lane.shape, 0)
    packed = jnp.where(lane < total, acc_w_ref[:, :rows], 0.0)
    packs = ((total + PACK - 1) // PACK).astype(jnp.float32)
    packed = jnp.where(row == kdim + 1, packs, packed)
    wt_ref[...] = packed.astype(jnp.bfloat16)
    wt_send_ref[...] = packed[: kdim + 8]


def prep(line, slab, owners, bins, grads, hess, side):
    rows, f_dev = bins.shape
    kdim = grads.shape[1]
    half = f_dev // 2
    return pl.pallas_call(
        functools.partial(prep_kernel, line, slab),
        in_specs=[SMEM_SPEC, pl.BlockSpec(memory_space=pl.ANY), VMEM_SPEC, VMEM_SPEC, VMEM_SPEC],
        out_specs=[VMEM_SPEC] * 4,
        out_shape=[
            jax.ShapeDtypeStruct((rows, half), jnp.bfloat16),
            jax.ShapeDtypeStruct((rows, half), jnp.float32),
            jax.ShapeDtypeStruct((kdim + 16, rows), jnp.bfloat16),
            jax.ShapeDtypeStruct((kdim + 8, rows), jnp.float32),
        ],
        scratch_shapes=[
            pltpu.VMEM((rows, f_dev), jnp.int32),
            pltpu.SemaphoreType.DMA((rows // TILE,)),
            pltpu.VMEM((rows + TILE + PACK, f_dev), jnp.bfloat16),
            pltpu.VMEM((kdim + 16, rows + TILE + PACK), jnp.float32),
        ],
        compiler_params=pltpu.CompilerParams(vmem_limit_bytes=PREP_MIB * MIB),
        cost_estimate=pl.CostEstimate(flops=4 * rows * f_dev * f_dev, bytes_accessed=8 * rows * f_dev, transcendentals=0),
        name="prep",
    )(owners, bins, grads.T, hess, side.reshape(1, rows))


def tiles_in(wt_ref, kdim):
    return jnp.max(wt_ref[:, :128].astype(jnp.float32)[kdim + 1 : kdim + 2]).astype(jnp.int32)


def hist_kernel(first_column, width, levels, parts, kdim, has_init, *refs):
    pairs = [refs[2 * i : 2 * i + 2] for i in range(parts)]
    init_ref = refs[2 * parts] if has_init else None
    out_ref, rel_ref, wt_ref = refs[-3:]
    lanes = out_ref.shape[1]
    rows, half = pairs[0][0].shape
    src = lax.broadcasted_iota(jnp.int32, (half, lanes), 0)
    dst = lax.broadcasted_iota(jnp.int32, (half, lanes), 1)
    spread = jnp.where(src == first_column + lax.rem(dst, width), 1.0, 0.0).astype(jnp.bfloat16)
    lane = lax.broadcasted_iota(jnp.int32, (1, lanes), 1)
    shift = ((lane // width) * levels).astype(jnp.float32)
    one = jnp.ones((TILE, lanes), jnp.bfloat16)
    zero = jnp.zeros((TILE, lanes), jnp.bfloat16)

    def place_rows(bins_ref, source, target, size):
        block = bins_ref[pl.ds(source, size), :].astype(jnp.bfloat16)
        moved = jnp.dot(block, spread, preferred_element_type=jnp.float32)
        rel_ref[pl.ds(target, size), :] = (moved - shift).astype(jnp.bfloat16)

    def place_weights(height):
        for i, (_, w_ref) in enumerate(pairs):
            weights = w_ref[:, :height]
            if w_ref.dtype != jnp.bfloat16:
                weights = jnp.concatenate([weights, jnp.zeros((8, height), jnp.float32)], axis=0).astype(jnp.bfloat16)
            wt_ref[:, i * height : (i + 1) * height] = weights

    def sums_of(b, tiles):
        value = jnp.full((TILE, lanes), b.astype(jnp.float32), jnp.float32).astype(jnp.bfloat16)
        total = jnp.zeros((wt_ref.shape[0], lanes), jnp.float32)
        for first, size in tiles:
            hit = rel_ref[pl.ds(first, size), :] == value[:size]
            onehot = jnp.where(hit, one[:size], zero[:size])
            total = total + jnp.dot(wt_ref[:, pl.ds(first, size)], onehot, preferred_element_type=jnp.float32)
        return total[:kdim], total[kdim : kdim + 1]

    def spots_of(b):
        return pl.ds(pl.multiple_of(b * kdim, kdim), kdim), pl.ds(levels * kdim + b, 1)

    def fast():
        height = FAST * PACK
        for i, (bins_ref, _) in enumerate(pairs):
            for r in range(0, height, 3 * PACK):
                place_rows(bins_ref, r, i * height + r, 3 * PACK)
        place_weights(height)
        tiles = [(r, min(TILE, parts * height - r)) for r in range(0, parts * height, TILE)]

        def level(b, carry):
            grad, hess = sums_of(b, tiles)
            grad_spot, hess_spot = spots_of(b)
            if has_init:
                grad, hess = grad + init_ref[grad_spot, :], hess + init_ref[hess_spot, :]
            out_ref[grad_spot, :] = grad
            out_ref[hess_spot, :] = hess
            return carry

        lax.fori_loop(0, levels, level, 0)

    def general():
        for i, (bins_ref, _) in enumerate(pairs):

            def one_pack(p, carry):
                r = pl.multiple_of(p * PACK, PACK)
                place_rows(bins_ref, r, i * rows + r, PACK)
                return carry

            lax.fori_loop(0, rows // PACK, one_pack, 0)
        place_weights(rows)
        out_ref[...] = init_ref[...] if has_init else jnp.zeros(out_ref.shape, jnp.float32)
        step = 2 * TILE

        def group(g, carry):
            first = pl.multiple_of(g * step, step)

            def level(b, carry):
                grad, hess = sums_of(b, [(first, TILE), (first + TILE, TILE)])
                grad_spot, hess_spot = spots_of(b)
                out_ref[grad_spot, :] += grad
                out_ref[hess_spot, :] += hess
                return carry

            return lax.fori_loop(0, levels, level, carry)

        lax.fori_loop(0, parts * rows // step, group, 0)

    needed = tiles_in(pairs[0][1], kdim)
    for _, w_ref in pairs[1:]:
        needed = jnp.maximum(needed, tiles_in(w_ref, kdim))
    if FAST * PACK < rows:
        pl.when(needed <= FAST)(fast)
        pl.when(needed > FAST)(general)
    else:
        general()


def hist(first_column, width, levels, lanes, kdim, pairs, init=None, tie=()):
    rows = pairs[0][0].shape[0]
    parts = len(pairs)
    operands = [x for pair in pairs for x in pair]
    if init is not None:
        operands.append(init)
    specs = [VMEM_SPEC] * len(operands) + [pl.BlockSpec(memory_space=pl.ANY)] * len(tie)
    height = levels * (kdim + 1)
    return pl.pallas_call(
        functools.partial(hist_kernel, first_column, width, levels, parts, kdim, init is not None),
        in_specs=specs,
        out_specs=VMEM_SPEC,
        out_shape=jax.ShapeDtypeStruct((height, lanes), jnp.float32),
        scratch_shapes=[
            pltpu.VMEM((parts * rows, lanes), jnp.bfloat16),
            pltpu.VMEM((kdim + 16, parts * rows), jnp.bfloat16),
        ],
        compiler_params=pltpu.CompilerParams(vmem_limit_bytes=20 * MIB),
        cost_estimate=pl.CostEstimate(
            flops=parts * rows * lanes, bytes_accessed=parts * rows * lanes, transcendentals=0
        ),
        name="hist",
    )(*operands, *tie)


def source_of(place, child_ref, parent_ref):
    source = jnp.int32(0)
    for q in range(child_ref.shape[0]):
        source = jnp.where(child_ref[q] == place, parent_ref[q], source)
    return source


def repeat_lanes(x, width, lanes):
    if lanes > x.shape[1]:
        x = jnp.concatenate([x] * (lanes // x.shape[1]), axis=1)
    x = jnp.where(lax.broadcasted_iota(jnp.int32, x.shape, 1) < width, x[:, :lanes], 0)
    reach = width
    while reach < lanes:
        x = x + pltpu.roll(x, reach, 1)
        reach *= 2
    return x


def layout_kernel(width, levels, kdim, chunks, line, child_ref, owner_ref, low_ref, high_ref, sign_ref, parent_ref, hess_ref, tie_ref, *out_refs):
    del tie_ref
    grad_refs, hess_refs, bound_refs = out_refs[:chunks], out_refs[chunks : 2 * chunks], out_refs[2 * chunks : 3 * chunks]
    lanes = grad_refs[0].shape[1]
    slab = width * chunks
    owners = owner_ref.shape[0]
    z, core = lax.axis_index("dp"), lax.axis_index("sub")
    place = 2 * z + core
    mine = source_of(place, child_ref, owner_ref)
    twin = source_of(2 * z + 1 - core, child_ref, owner_ref)
    row = lax.broadcasted_iota(jnp.int32, (8, lanes), 0)
    route = jnp.where(row == 0, lax.rem(z - mine // 2 + line, line), lax.rem(z - twin // 2 + line, line))
    out_refs[-1][...] = jnp.where(row == 2, jnp.where(lax.rem(mine, 2) == core, 1, 0), route)
    slab_at = jnp.int32(0)
    for q in range(owners):
        slab_at = jnp.where(owner_ref[q] == place, q, slab_at)
    offset = lax.axis_index("feat") * (owners * slab) + slab_at * slab
    features = sign_ref.shape[1]
    signs = jnp.broadcast_to(sign_ref[...], (8, features))
    per_tile = 128 // width
    step = 128 // kdim
    for c in range(chunks):
        turned = pltpu.roll(signs, lax.rem(features - offset - c * width + features, features), 1)
        sign = repeat_lanes(turned[:, :128], width, lanes)[:1]
        bounds = []
        for child in range(2):
            low = low_ref[child].astype(jnp.float32) / 1024.0
            high = high_ref[child].astype(jnp.float32) / 1024.0
            middle = 0.5 * (low + high)
            bounds.append(jnp.where(sign < 0, middle, low))
            bounds.append(jnp.where(sign > 0, middle, high))
            bounds.append(jnp.where(sign > 0, middle, low))
            bounds.append(jnp.where(sign < 0, middle, high))
        bound_refs[c][...] = jnp.concatenate(bounds, axis=0)
        rows = hess_ref[c * width : (c + 1) * width, :]
        turned = jnp.concatenate([rows] * (128 // width), axis=0).T
        total = jnp.zeros((levels, lanes), jnp.float32)
        for j in range(lanes // width):
            piece = turned[j * levels : (j + 1) * levels, :]
            piece = jnp.concatenate([piece] * (lanes // 128), axis=1)
            group = lax.broadcasted_iota(jnp.int32, piece.shape, 1) // width
            total = jnp.where(group == j, piece, total)
        hess_refs[c][...] = total
        for tile in range(lanes // 128):
            for b in range(0, levels, step):
                rows = []
                for jj in range(per_tile):
                    bin_at = (tile * per_tile + jj) * levels + b
                    rows.append(parent_ref[c * width : (c + 1) * width, bin_at * kdim : bin_at * kdim + 128])
                block = jnp.concatenate(rows, axis=0) if per_tile > 1 else rows[0]
                grad_refs[c][b * kdim : b * kdim + 128, tile * 128 : (tile + 1) * 128] = block.T


def parent_layout(width, levels, lanes, kdim, chunks, line, child_owner, owners, low, high, signs, parent, hess, tie):
    shapes = [jax.ShapeDtypeStruct((levels * kdim, lanes), jnp.float32)] * chunks
    shapes += [jax.ShapeDtypeStruct((levels, lanes), jnp.float32)] * chunks
    shapes += [jax.ShapeDtypeStruct((8, lanes), jnp.float32)] * chunks
    shapes += [jax.ShapeDtypeStruct((8, lanes), jnp.int32)]
    out = pl.pallas_call(
        functools.partial(layout_kernel, width, levels, kdim, chunks, line),
        in_specs=[SMEM_SPEC] * 4 + [VMEM_SPEC] * 3 + [pl.BlockSpec(memory_space=pl.ANY)],
        out_specs=[VMEM_SPEC] * (3 * chunks + 1),
        out_shape=shapes,
        compiler_params=pltpu.CompilerParams(vmem_limit_bytes=16 * MIB),
        cost_estimate=pl.CostEstimate(flops=0, bytes_accessed=2 * parent.size * 4, transcendentals=0),
        name="parent_layout",
    )(child_owner, owners, low, high, signs.reshape(1, -1), parent, hess, tie)
    return out[:chunks], out[chunks : 2 * chunks], out[2 * chunks : 3 * chunks], out[-1]


def lane_prefix(total, width):
    lanes = total.shape[1]
    lane = lax.broadcasted_iota(jnp.int32, total.shape, 1)
    running = total
    reach = width
    while reach < lanes:
        running = running + jnp.where(lane >= reach, pltpu.roll(running, reach, 1), 0.0)
        reach *= 2
    whole = total
    reach = width
    while reach < lanes:
        whole = whole + pltpu.roll(whole, reach, 1)
        reach *= 2
    return running - total, running, whole


def gain_kernel(width, levels, kdim, last_ref, right_ref, left_ref, par_grad_ref, par_hess_ref, bound_ref, tie_ref, out_ref, grad_ref, hess_ref):
    del tie_ref
    hess_at = levels * kdim
    lanes = out_ref.shape[2]

    def small_at(start, size):
        return last_ref[pl.ds(start, size), :] + right_ref[pl.ds(start, size), :] + left_ref[pl.ds(start, size), :]

    small_hess = small_at(hess_at, levels)
    hess_ref[0] = small_hess
    hess_ref[1] = par_hess_ref[...] - small_hess

    def add_up(b, carry):
        g0, g1, h0, h1 = carry
        start = pl.multiple_of(b * kdim, kdim)
        small = small_at(start, kdim)
        g0 = g0 + small
        g1 = g1 + (par_grad_ref[pl.ds(start, kdim), :] - small)
        h0 = h0 + hess_ref[0, pl.ds(b, 1), :]
        h1 = h1 + hess_ref[1, pl.ds(b, 1), :]
        grad_ref[0, pl.ds(start, kdim), :] = g0
        grad_ref[1, pl.ds(start, kdim), :] = g1
        hess_ref[0, pl.ds(b, 1), :] = h0
        hess_ref[1, pl.ds(b, 1), :] = h1
        return g0, g1, h0, h1

    zero_g = jnp.zeros((kdim, lanes), jnp.float32)
    zero_h = jnp.zeros((1, lanes), jnp.float32)
    ends = lax.fori_loop(0, levels, add_up, (zero_g, zero_g, zero_h, zero_h), unroll=4)
    for c in range(2):
        low_left, high_left, low_right, high_right = [bound_ref[4 * c + i : 4 * c + i + 1, :] for i in range(4)]
        grad_before, _, grad_all = lane_prefix(ends[c], width)
        hess_rows = jnp.broadcast_to(ends[2 + c], (8, lanes))
        hess_before, _, hess_all = lane_prefix(hess_rows, width)
        hess_before, hess_all = hess_before[:1], hess_all[:1]

        def score(grad, hess, lower, upper):
            denom = jnp.maximum(hess, 0.0) + reg_lambda
            weight = jnp.clip(-grad / denom, lower, upper)
            return jnp.sum((2.0 * grad + denom * weight) * weight, axis=0, keepdims=True)

        def one_bin(b, carry):
            start = pl.multiple_of(b * kdim, kdim)
            grad_left = grad_ref[c, pl.ds(start, kdim), :] + grad_before
            hess_left = hess_ref[c, pl.ds(b, 1), :] + hess_before
            left = score(grad_left, hess_left, low_left, high_left)
            right = score(grad_all - grad_left, hess_all - hess_left, low_right, high_right)
            out_ref[c, pl.ds(b, 1), :] = (left + right) * (-1.0 / kdim)
            return carry

        lax.fori_loop(0, levels, one_bin, 0, unroll=4)


def gains_of(width, levels, lanes, kdim, last, right, left, par_grad, par_hess, bounds, tie):
    return pl.pallas_call(
        functools.partial(gain_kernel, width, levels, kdim),
        in_specs=[VMEM_SPEC] * 6 + [pl.BlockSpec(memory_space=pl.ANY)],
        out_specs=VMEM_SPEC,
        out_shape=jax.ShapeDtypeStruct((2, levels, lanes), jnp.float32),
        scratch_shapes=[
            pltpu.VMEM((2, levels * kdim, lanes), jnp.float32),
            pltpu.VMEM((2, levels, lanes), jnp.float32),
        ],
        compiler_params=pltpu.CompilerParams(vmem_limit_bytes=24 * MIB),
        cost_estimate=pl.CostEstimate(flops=50 * levels * kdim * lanes, bytes_accessed=16 * levels * kdim * lanes, transcendentals=0),
        name="gains",
    )(last, right, left, par_grad, par_hess, bounds, tie)


def chosen(shift, got):
    value = got[0]
    for s in range(1, len(got)):
        value = jnp.where(shift == s, got[s], value)
    return value


def finish_kernel(width, line, route_ref, *refs):
    out_ref = refs[-1]
    chunks = (len(refs) - 1) // (line + 1)
    slab = width * chunks
    lanes = route_ref.shape[1]
    shift, same = route_ref[:1, :], route_ref[2:3, :]
    total = jnp.zeros((128, 128), jnp.float32)
    column = lax.broadcasted_iota(jnp.int32, (128, 128), 1)
    for child in range(2):
        for c in range(chunks):
            got = [ref[child] for ref in refs[c * (line + 1) : (c + 1) * (line + 1)]]
            gain = jnp.where(same == 1, chosen(shift, got[:line]), got[line])
            at = child * slab + c * width
            pieces = []
            for j in range(lanes // width):
                turn = (at - j * width) % lanes
                turned = pltpu.roll(gain, turn, 1) if turn else gain
                pieces.append(turned[:, :128])
            stack = jnp.concatenate(pieces, axis=0)
            total = jnp.where((column >= at) & (column < at + width), stack, total)
    turned = total.T
    for child in range(2):
        out_ref[:, child, :] = turned[child * slab : (child + 1) * slab]


def finish(width, nbins, line, route, parts):
    flat = [x for part in parts for x in part]
    return pl.pallas_call(
        functools.partial(finish_kernel, width, line),
        in_specs=[VMEM_SPEC] * (1 + len(flat)),
        out_specs=VMEM_SPEC,
        out_shape=jax.ShapeDtypeStruct((width * len(parts), 2, nbins), jnp.float32),
        name="finish",
    )(route, *flat)


def one_of(z, members):
    hit = z == members[0]
    for m in members[1:]:
        hit = hit | (z == m)
    return hit


def sum_line(line, chunks, units, unit, set_up):
    plan = plan_of(line)
    z = lax.axis_index("dp")
    from_left = [None] * chunks
    from_right = [None] * chunks
    arrived = []

    def pick(kind, step, c):
        where_at = {}
        for zz in range(line):
            for p, role in enumerate(plan[zz]):
                if role[:2] == (kind, step):
                    where_at.setdefault(p, []).append(zz)
        spots = sorted(where_at)
        value = units[spots[0], c]
        for p in spots[1:]:
            value = jnp.where(one_of(z, where_at[p]), units[p, c], value)
        return value

    def tie_of(step, c):
        at = min(step * chunks + c - 3, (line - 2) * chunks - 1)
        return (arrived[at],) if at >= 0 else (units[0, chunks - 1],)

    last = line - 1
    for step in range(last):
        for c in range(chunks):
            if step > 0:
                units[step, c] = unit(step, c, tie_of(step, c))
            to_right = pick("R", step, c)
            to_left = pick("L", step, c)
            if step > 0:
                to_right = to_right + from_left[c]
                to_left = to_left + from_right[c]
            from_left[c] = lax.ppermute(to_right, "dp", [(i, i + 1) for i in range(step + 1)])
            from_right[c] = lax.ppermute(to_left, "dp", [(line - 1 - i, line - 2 - i) for i in range(step + 1)])
            arrived.append(from_left[c])
    layout = set_up(tie_of(last, 0)[0])
    return [unit(last, c, tie_of(last, c)) for c in range(chunks)], from_left, from_right, layout


def sum_line_of_4(line, chunks, units, unit, set_up):
    inward, outer, middle = [(0, 1), (3, 2)], [(0, 1), (1, 0), (2, 3), (3, 2)], [(1, 2), (2, 1)]
    a0, a1, a2, b1, b2, last = {}, {}, {}, {}, {}, {}
    for c in range(chunks):
        a0[c] = lax.ppermute(units[0, c], "dp", inward)
    last[0] = unit(3, 0, (units[0, chunks - 1],))
    for c in range(chunks):
        units[1, c] = unit(1, c, (a0[c], units[1, c - 1] if c else last[0]))
        b1[c] = lax.ppermute(units[0, c] + a0[c], "dp", middle)
        a1[c] = lax.ppermute(units[1, c], "dp", inward)
    for c in range(chunks):
        units[2, c] = unit(2, c, (a1[c], units[2, c - 1] if c else units[1, chunks - 1]))
        b2[c] = lax.ppermute(units[1, c] + a1[c], "dp", middle)
        a2[c] = lax.ppermute(units[2, c] + b1[c], "dp", outer)
    layout = set_up(units[2, 0])
    for c in range(1, chunks):
        last[c] = unit(3, c, (units[2, chunks - 1],))
    return last, a2, b2, layout


def per_device(bins, grads, hess, node_side, signs, child_owner, parent_owner, parent_grad, parent_hess, node_low, node_high):
    line = lax.axis_size("dp")
    kdim = grads.shape[1]
    nbins = parent_hess.shape[2]
    slab = parent_grad.shape[1]
    chunks = CHUNKS if slab >= 32 else 1
    width = slab // chunks
    lanes = min(256, width * nbins * kdim // 128)
    levels = nbins // (lanes // width)

    own, send, wt, wt_send = prep(line, slab, parent_owner, bins, grads, hess, node_side)
    swap = [(0, 1), (1, 0)]
    wt_other = lax.ppermute(wt_send, "sub", swap)
    other = lax.ppermute(send, "sub", swap)
    mine = (own, wt)
    theirs = (other, wt_other)

    def unit(p, c, pairs, init=None, tie=()):
        return hist(p * slab + c * width, width, levels, lanes, kdim, pairs, init, tie)

    def set_up(tie):
        return parent_layout(
            width, levels, lanes, kdim, chunks, line, child_owner, parent_owner, node_low, node_high, signs, parent_grad[0], parent_hess[0], tie
        )

    units = {}
    units[0, 0] = unit(0, 0, [theirs], unit(0, 0, [mine]))
    for c in range(1, chunks):
        units[0, c] = unit(0, c, [mine, theirs], tie=(units[0, c - 1],))
    collect = sum_line_of_4 if line == 4 else sum_line
    last, from_left, from_right, layout = collect(line, chunks, units, lambda p, c, tie: unit(p, c, [mine, theirs], tie=tie), set_up)
    par_grad, par_hess, bounds, route = layout

    done = []
    for c in range(chunks):
        gain = gains_of(
            width, levels, lanes, kdim, last[c], from_left[c], from_right[c], par_grad[c], par_hess[c], bounds[c], last[chunks - 1]
        )
        got = [gain] + [lax.ppermute(gain, "dp", [(i, (i + s) % line) for i in range(line)]) for s in range(1, line)]
        crossed = lax.ppermute(chosen(route[1, 0], got), "sub", swap)
        done.append([*got, crossed])
    return finish(width, nbins, line, route, done)[None]


def solution(mesh):
    return jax.shard_map(
        per_device,
        mesh=mesh,
        in_specs=(
            P(("groups", "dp", "sub"), "feat"),
            P(("groups", "dp", "sub"), None),
            P(("groups", "dp", "sub")),
            P(("groups", "dp", "sub")),
            P("groups"),
            P("groups"),
            P("groups"),
            P(("groups", "dp", "sub"), "feat", None),
            P(("groups", "dp", "sub"), "feat", None),
            P("groups"),
            P("groups"),
        ),
        out_specs=P(("groups", "dp", "sub"), "feat", None, None),
        check_vma=False,
    )
```

```python
import functools

import jax
import jax.numpy as jnp
from jax import lax
from jax.experimental import pallas as pl
from jax.experimental.pallas import tpu as pltpu
from jax.sharding import PartitionSpec as P

reg_lambda = 1.0
CHUNKS = 2
TILE = 256
PACK = 128
FAST = 9
PREP_MIB = 56
MIB = 1024 * 1024
VMEM_SPEC = pl.BlockSpec(memory_space=pltpu.VMEM)
SMEM_SPEC = pl.BlockSpec(memory_space=pltpu.SMEM)


def plan_of(line):
    roles = []
    for z in range(line):
        mine = []
        for step in range(line - 1):
            now = []
            if z <= step:
                now.append(("R", step, line - 1 - step + z))
            if line - 1 - z <= step:
                now.append(("L", step, step - (line - 1 - z)))
            mine.extend(now if 2 * z < line else now[::-1])
        mine.append(("F", line - 1, z))
        roles.append(mine)
    return roles


def prep_kernel(line, slab, owner_ref, bins_ref, grads_ref, hess_ref, side_ref, own_ref, send_ref, wt_ref, wt_send_ref, buf_ref, sems, acc_ref, acc_w_ref, own_buf, send_buf, out_sems):
    rows, f_dev = bins_ref.shape
    half = f_dev // 2
    kdim = grads_ref.shape[0]
    reach = TILE + PACK
    blocks = rows // TILE
    copies = []
    for i in range(blocks):
        part = pl.ds(i * TILE, TILE)
        copies.append(pltpu.make_async_copy(bins_ref.at[part, :], buf_ref.at[part, :], sems.at[i]))
        copies[-1].start()

    hess_row = hess_ref[...].astype(jnp.float32).reshape(1, rows)
    ones = [jnp.where(side_ref[:, i * TILE : (i + 1) * TILE] == 1, 1.0, 0.0) for i in range(blocks)]
    counts = [jnp.sum(x).astype(jnp.int32) for x in ones]
    bases = [jnp.int32(0)]
    for count in counts:
        bases.append(bases[-1] + count)
    starts = [pl.multiple_of((base // PACK) * PACK, PACK) for base in bases]
    marks = jnp.concatenate(ones, axis=0)
    before = lax.broadcasted_iota(jnp.int32, (TILE, TILE), 0) < lax.broadcasted_iota(jnp.int32, (TILE, TILE), 1)
    before = jnp.where(before, 1.0, 0.0).astype(jnp.bfloat16)
    ahead = jnp.dot(marks.astype(jnp.bfloat16), before, preferred_element_type=jnp.float32).astype(jnp.int32)
    slot = lax.broadcasted_iota(jnp.int32, (reach, TILE), 0)
    acc_ref[:PACK, :] = jnp.zeros((PACK, f_dev), jnp.bfloat16)
    acc_w_ref[:, :PACK] = jnp.zeros((acc_w_ref.shape[0], PACK), jnp.float32)

    z, core = lax.axis_index("dp"), lax.axis_index("sub")
    column = lax.broadcasted_iota(jnp.int32, (1, f_dev), 1)
    position = lax.rem(column, half) // slab
    table = plan_of(line)
    chip = jnp.zeros_like(column)
    for p in range(line):
        target = jnp.int32(0)
        for zz in range(line):
            target = jnp.where(z == zz, jnp.int32(table[zz][p][2]), target)
        chip = jnp.where(position == p, target, chip)
    owner = 2 * chip + jnp.where(column < half, core, 1 - core)
    source = jnp.zeros_like(column)
    for q in range(2 * line):
        source = jnp.where(owner == owner_ref[q], q, source)
    source = source * slab + lax.rem(column, slab)
    perm = jnp.where(lax.broadcasted_iota(jnp.int32, (f_dev, f_dev), 0) == source, 1.0, 0.0).astype(jnp.bfloat16)

    for i in range(blocks):
        part = slice(i * TILE, (i + 1) * TILE)
        goal = jnp.where(ones[i] > 0.5, ahead[i : i + 1] + (bases[i] - starts[i]), -1)
        pack = jnp.where(slot == goal, 1.0, 0.0).astype(jnp.bfloat16)
        hess = jnp.broadcast_to(hess_row[:, part], (16, TILE))
        first = lax.broadcasted_iota(jnp.int32, hess.shape, 0) == 0
        weights = jnp.concatenate([grads_ref[:, part].astype(jnp.float32), jnp.where(first, hess, 0.0)], axis=0)
        packed_w = lax.dot_general(weights.astype(jnp.bfloat16), pack, (((1,), (1,)), ((), ())), preferred_element_type=jnp.float32)
        acc_w_ref[:, pl.ds(starts[i], PACK)] += packed_w[:, :PACK]
        acc_w_ref[:, pl.ds(starts[i] + PACK, TILE)] = packed_w[:, PACK:]
        copies[i].wait()
        binned = buf_ref[part, :].astype(jnp.float32).astype(jnp.bfloat16)
        packed = jnp.dot(pack, binned, preferred_element_type=jnp.float32).astype(jnp.bfloat16)
        acc_ref[pl.ds(starts[i], PACK), :] += packed[:PACK]
        acc_ref[pl.ds(starts[i] + PACK, TILE), :] = packed[PACK:]

    def move(t, carry):
        part = pl.ds(pl.multiple_of(t * TILE, TILE), TILE)
        moved = jnp.dot(acc_ref[part, :], perm, preferred_element_type=jnp.float32)
        own_buf[part, :] = moved[:, :half].astype(jnp.bfloat16)
        send_buf[part, :] = moved[:, half:]
        pltpu.make_async_copy(own_buf.at[part, :], own_ref.at[part, :], out_sems.at[t, 0]).start()
        pltpu.make_async_copy(send_buf.at[part, :], send_ref.at[part, :], out_sems.at[t, 1]).start()
        return carry

    def moved_out(t, carry):
        part = pl.ds(pl.multiple_of(t * TILE, TILE), TILE)
        pltpu.make_async_copy(own_buf.at[part, :], own_ref.at[part, :], out_sems.at[t, 0]).wait()
        pltpu.make_async_copy(send_buf.at[part, :], send_ref.at[part, :], out_sems.at[t, 1]).wait()
        return carry

    total = bases[blocks]
    used = (total + TILE - 1) // TILE
    lax.fori_loop(0, used, move, 0)
    lane = lax.broadcasted_iota(jnp.int32, (acc_w_ref.shape[0], rows), 1)
    row = lax.broadcasted_iota(jnp.int32, lane.shape, 0)
    packed = jnp.where(lane < total, acc_w_ref[:, :rows], 0.0)
    packs = ((total + PACK - 1) // PACK).astype(jnp.float32)
    packed = jnp.where(row == kdim + 1, packs, packed)
    wt_ref[...] = packed.astype(jnp.bfloat16)
    wt_send_ref[...] = packed[: kdim + 8]
    lax.fori_loop(0, used, moved_out, 0)


def prep(line, slab, owners, bins, grads, hess, side):
    rows, f_dev = bins.shape
    kdim = grads.shape[1]
    half = f_dev // 2
    return pl.pallas_call(
        functools.partial(prep_kernel, line, slab),
        in_specs=[SMEM_SPEC, pl.BlockSpec(memory_space=pl.ANY), VMEM_SPEC, VMEM_SPEC, VMEM_SPEC],
        out_specs=[pl.BlockSpec(memory_space=pl.ANY)] * 2 + [VMEM_SPEC] * 2,
        out_shape=[
            jax.ShapeDtypeStruct((rows, half), jnp.bfloat16),
            jax.ShapeDtypeStruct((rows, half), jnp.float32),
            jax.ShapeDtypeStruct((kdim + 16, rows), jnp.bfloat16),
            jax.ShapeDtypeStruct((kdim + 8, rows), jnp.float32),
        ],
        scratch_shapes=[
            pltpu.VMEM((rows, f_dev), jnp.int32),
            pltpu.SemaphoreType.DMA((rows // TILE,)),
            pltpu.VMEM((rows + TILE + PACK, f_dev), jnp.bfloat16),
            pltpu.VMEM((kdim + 16, rows + TILE + PACK), jnp.float32),
            pltpu.VMEM((rows, half), jnp.bfloat16),
            pltpu.VMEM((rows, half), jnp.float32),
            pltpu.SemaphoreType.DMA((rows // TILE, 2)),
        ],
        compiler_params=pltpu.CompilerParams(vmem_limit_bytes=PREP_MIB * MIB),
        cost_estimate=pl.CostEstimate(flops=4 * rows * f_dev * f_dev, bytes_accessed=8 * rows * f_dev, transcendentals=0),
        name="prep",
    )(owners, bins, grads.T, hess, side.reshape(1, rows))


def tiles_in(wt_ref, kdim):
    return jnp.max(wt_ref[:, :128].astype(jnp.float32)[kdim + 1 : kdim + 2]).astype(jnp.int32)


def hist_kernel(first_column, width, levels, parts, kdim, has_init, *refs):
    pairs = [refs[2 * i : 2 * i + 2] for i in range(parts)]
    init_ref = refs[2 * parts] if has_init else None
    out_ref, rel_ref, wt_ref = refs[-3:]
    lanes = out_ref.shape[1]
    rows, half = pairs[0][0].shape
    src = lax.broadcasted_iota(jnp.int32, (half, lanes), 0)
    dst = lax.broadcasted_iota(jnp.int32, (half, lanes), 1)
    spread = jnp.where(src == first_column + lax.rem(dst, width), 1.0, 0.0).astype(jnp.bfloat16)
    lane = lax.broadcasted_iota(jnp.int32, (1, lanes), 1)
    shift = ((lane // width) * levels).astype(jnp.float32)
    one = jnp.ones((TILE, lanes), jnp.bfloat16)
    zero = jnp.zeros((TILE, lanes), jnp.bfloat16)

    def place_rows(bins_ref, source, target, size):
        block = bins_ref[pl.ds(source, size), :].astype(jnp.bfloat16)
        moved = jnp.dot(block, spread, preferred_element_type=jnp.float32)
        rel_ref[pl.ds(target, size), :] = (moved - shift).astype(jnp.bfloat16)

    def place_weights(height):
        for i, (_, w_ref) in enumerate(pairs):
            weights = w_ref[:, :height]
            if w_ref.dtype != jnp.bfloat16:
                weights = jnp.concatenate([weights, jnp.zeros((8, height), jnp.float32)], axis=0).astype(jnp.bfloat16)
            wt_ref[:, i * height : (i + 1) * height] = weights

    def sums_of(some, tiles):
        values = [jnp.full((TILE, lanes), b.astype(jnp.float32), jnp.float32).astype(jnp.bfloat16) for b in some]
        totals = [jnp.zeros((wt_ref.shape[0], lanes), jnp.float32) for _ in some]
        for first, size in tiles:
            found = rel_ref[pl.ds(first, size), :]
            weights = wt_ref[:, pl.ds(first, size)]
            for i, value in enumerate(values):
                onehot = jnp.where(found == value[:size], one[:size], zero[:size])
                totals[i] = totals[i] + jnp.dot(weights, onehot, preferred_element_type=jnp.float32)
        return [(total[:kdim], total[kdim : kdim + 1]) for total in totals]

    def spots_of(b):
        return pl.ds(pl.multiple_of(b * kdim, kdim), kdim), pl.ds(levels * kdim + b, 1)

    def fast():
        height = FAST * PACK
        for i, (bins_ref, _) in enumerate(pairs):
            for r in range(0, height, 3 * PACK):
                place_rows(bins_ref, r, i * height + r, 3 * PACK)
        place_weights(height)
        tiles = [(r, min(TILE, parts * height - r)) for r in range(0, parts * height, TILE)]

        def two_levels(step, carry):
            some = [2 * step, 2 * step + 1]
            for b, (grad, hess) in zip(some, sums_of(some, tiles)):
                grad_spot, hess_spot = spots_of(b)
                if has_init:
                    grad, hess = grad + init_ref[grad_spot, :], hess + init_ref[hess_spot, :]
                out_ref[grad_spot, :] = grad
                out_ref[hess_spot, :] = hess
            return carry

        lax.fori_loop(0, levels // 2, two_levels, 0)

    def general():
        for i, (bins_ref, _) in enumerate(pairs):

            def one_pack(p, carry):
                r = pl.multiple_of(p * PACK, PACK)
                place_rows(bins_ref, r, i * rows + r, PACK)
                return carry

            lax.fori_loop(0, rows // PACK, one_pack, 0)
        place_weights(rows)
        out_ref[...] = init_ref[...] if has_init else jnp.zeros(out_ref.shape, jnp.float32)
        step = 2 * TILE

        def group(g, carry):
            first = pl.multiple_of(g * step, step)

            def level(b, carry):
                ((grad, hess),) = sums_of([b], [(first, TILE), (first + TILE, TILE)])
                grad_spot, hess_spot = spots_of(b)
                out_ref[grad_spot, :] += grad
                out_ref[hess_spot, :] += hess
                return carry

            return lax.fori_loop(0, levels, level, carry)

        lax.fori_loop(0, parts * rows // step, group, 0)

    needed = tiles_in(pairs[0][1], kdim)
    for _, w_ref in pairs[1:]:
        needed = jnp.maximum(needed, tiles_in(w_ref, kdim))
    if FAST * PACK < rows:
        pl.when(needed <= FAST)(fast)
        pl.when(needed > FAST)(general)
    else:
        general()


def hist(first_column, width, levels, lanes, kdim, pairs, init=None, tie=()):
    rows = pairs[0][0].shape[0]
    parts = len(pairs)
    operands = [x for pair in pairs for x in pair]
    if init is not None:
        operands.append(init)
    specs = [VMEM_SPEC] * len(operands) + [pl.BlockSpec(memory_space=pl.ANY)] * len(tie)
    height = levels * (kdim + 1)
    return pl.pallas_call(
        functools.partial(hist_kernel, first_column, width, levels, parts, kdim, init is not None),
        in_specs=specs,
        out_specs=VMEM_SPEC,
        out_shape=jax.ShapeDtypeStruct((height, lanes), jnp.float32),
        scratch_shapes=[
            pltpu.VMEM((parts * rows, lanes), jnp.bfloat16),
            pltpu.VMEM((kdim + 16, parts * rows), jnp.bfloat16),
        ],
        compiler_params=pltpu.CompilerParams(vmem_limit_bytes=20 * MIB),
        cost_estimate=pl.CostEstimate(
            flops=parts * rows * lanes, bytes_accessed=parts * rows * lanes, transcendentals=0
        ),
        name="hist",
    )(*operands, *tie)


def source_of(place, child_ref, parent_ref):
    source = jnp.int32(0)
    for q in range(child_ref.shape[0]):
        source = jnp.where(child_ref[q] == place, parent_ref[q], source)
    return source


def repeat_lanes(x, width, lanes):
    if lanes > x.shape[1]:
        x = jnp.concatenate([x] * (lanes // x.shape[1]), axis=1)
    x = jnp.where(lax.broadcasted_iota(jnp.int32, x.shape, 1) < width, x[:, :lanes], 0)
    reach = width
    while reach < lanes:
        x = x + pltpu.roll(x, reach, 1)
        reach *= 2
    return x


def layout_kernel(width, levels, kdim, chunks, child_ref, owner_ref, low_ref, high_ref, sign_ref, parent_ref, hess_ref, tie_ref, *out_refs):
    del tie_ref
    grad_refs, hess_refs, bound_refs = out_refs[:chunks], out_refs[chunks : 2 * chunks], out_refs[2 * chunks : 3 * chunks]
    lanes = grad_refs[0].shape[1]
    slab = width * chunks
    owners = owner_ref.shape[0]
    z, core = lax.axis_index("dp"), lax.axis_index("sub")
    place = 2 * z + core
    route_ref = out_refs[-1]
    route_ref[...] = jnp.full(route_ref.shape, source_of(place, child_ref, owner_ref), jnp.int32)
    slab_at = jnp.int32(0)
    for q in range(owners):
        slab_at = jnp.where(owner_ref[q] == place, q, slab_at)
    offset = lax.axis_index("feat") * (owners * slab) + slab_at * slab
    features = sign_ref.shape[1]
    signs = jnp.broadcast_to(sign_ref[...], (8, features))
    per_tile = 128 // width
    step = 128 // kdim
    for c in range(chunks):
        turned = pltpu.roll(signs, lax.rem(features - offset - c * width + features, features), 1)
        sign = repeat_lanes(turned[:, :128], width, lanes)[:1]
        bounds = []
        for child in range(2):
            low = low_ref[child].astype(jnp.float32) / 1024.0
            high = high_ref[child].astype(jnp.float32) / 1024.0
            middle = 0.5 * (low + high)
            bounds.append(jnp.where(sign < 0, middle, low))
            bounds.append(jnp.where(sign > 0, middle, high))
            bounds.append(jnp.where(sign > 0, middle, low))
            bounds.append(jnp.where(sign < 0, middle, high))
        bound_refs[c][...] = jnp.concatenate(bounds, axis=0)
        rows = hess_ref[c * width : (c + 1) * width, :]
        turned = jnp.concatenate([rows] * (128 // width), axis=0).T
        total = jnp.zeros((levels, lanes), jnp.float32)
        for j in range(lanes // width):
            piece = turned[j * levels : (j + 1) * levels, :]
            piece = jnp.concatenate([piece] * (lanes // 128), axis=1)
            group = lax.broadcasted_iota(jnp.int32, piece.shape, 1) // width
            total = jnp.where(group == j, piece, total)
        hess_refs[c][...] = total
        for tile in range(lanes // 128):
            for b in range(0, levels, step):
                rows = []
                for jj in range(per_tile):
                    bin_at = (tile * per_tile + jj) * levels + b
                    rows.append(parent_ref[c * width : (c + 1) * width, bin_at * kdim : bin_at * kdim + 128])
                block = jnp.concatenate(rows, axis=0) if per_tile > 1 else rows[0]
                grad_refs[c][b * kdim : b * kdim + 128, tile * 128 : (tile + 1) * 128] = block.T


def parent_layout(width, levels, lanes, kdim, chunks, child_owner, owners, low, high, signs, parent, hess, tie):
    shapes = [jax.ShapeDtypeStruct((levels * kdim, lanes), jnp.float32)] * chunks
    shapes += [jax.ShapeDtypeStruct((levels, lanes), jnp.float32)] * chunks
    shapes += [jax.ShapeDtypeStruct((8, lanes), jnp.float32)] * chunks
    shapes += [jax.ShapeDtypeStruct((8, lanes), jnp.int32)]
    out = pl.pallas_call(
        functools.partial(layout_kernel, width, levels, kdim, chunks),
        in_specs=[SMEM_SPEC] * 4 + [VMEM_SPEC] * 3 + [pl.BlockSpec(memory_space=pl.ANY)],
        out_specs=[VMEM_SPEC] * (3 * chunks + 1),
        out_shape=shapes,
        compiler_params=pltpu.CompilerParams(vmem_limit_bytes=16 * MIB),
        cost_estimate=pl.CostEstimate(flops=0, bytes_accessed=2 * parent.size * 4, transcendentals=0),
        name="parent_layout",
    )(child_owner, owners, low, high, signs.reshape(1, -1), parent, hess, tie)
    return out[:chunks], out[chunks : 2 * chunks], out[2 * chunks : 3 * chunks], out[-1]


def lane_prefix(total, width):
    lanes = total.shape[1]
    lane = lax.broadcasted_iota(jnp.int32, total.shape, 1)
    running = total
    reach = width
    while reach < lanes:
        running = running + jnp.where(lane >= reach, pltpu.roll(running, reach, 1), 0.0)
        reach *= 2
    whole = total
    reach = width
    while reach < lanes:
        whole = whole + pltpu.roll(whole, reach, 1)
        reach *= 2
    return running - total, running, whole


def gain_kernel(width, levels, kdim, last_ref, right_ref, left_ref, par_grad_ref, par_hess_ref, bound_ref, tie_ref, out_ref, grad_ref, hess_ref):
    del tie_ref
    hess_at = levels * kdim
    lanes = out_ref.shape[2]

    def small_at(start, size):
        return last_ref[pl.ds(start, size), :] + right_ref[pl.ds(start, size), :] + left_ref[pl.ds(start, size), :]

    small_hess = small_at(hess_at, levels)
    hess_ref[0] = small_hess
    hess_ref[1] = par_hess_ref[...] - small_hess

    def add_up(b, carry):
        g0, g1, h0, h1 = carry
        start = pl.multiple_of(b * kdim, kdim)
        small = small_at(start, kdim)
        g0 = g0 + small
        g1 = g1 + (par_grad_ref[pl.ds(start, kdim), :] - small)
        h0 = h0 + hess_ref[0, pl.ds(b, 1), :]
        h1 = h1 + hess_ref[1, pl.ds(b, 1), :]
        grad_ref[0, pl.ds(start, kdim), :] = g0
        grad_ref[1, pl.ds(start, kdim), :] = g1
        hess_ref[0, pl.ds(b, 1), :] = h0
        hess_ref[1, pl.ds(b, 1), :] = h1
        return g0, g1, h0, h1

    zero_g = jnp.zeros((kdim, lanes), jnp.float32)
    zero_h = jnp.zeros((1, lanes), jnp.float32)
    ends = lax.fori_loop(0, levels, add_up, (zero_g, zero_g, zero_h, zero_h), unroll=4)
    for c in range(2):
        low_left, high_left, low_right, high_right = [bound_ref[4 * c + i : 4 * c + i + 1, :] for i in range(4)]
        grad_before, _, grad_all = lane_prefix(ends[c], width)
        hess_rows = jnp.broadcast_to(ends[2 + c], (8, lanes))
        hess_before, _, hess_all = lane_prefix(hess_rows, width)
        hess_before, hess_all = hess_before[:1], hess_all[:1]

        def score(grad, hess, lower, upper):
            denom = jnp.maximum(hess, 0.0) + reg_lambda
            weight = jnp.clip(-grad / denom, lower, upper)
            return jnp.sum((2.0 * grad + denom * weight) * weight, axis=0, keepdims=True)

        def one_bin(b, carry):
            start = pl.multiple_of(b * kdim, kdim)
            grad_left = grad_ref[c, pl.ds(start, kdim), :] + grad_before
            hess_left = hess_ref[c, pl.ds(b, 1), :] + hess_before
            left = score(grad_left, hess_left, low_left, high_left)
            right = score(grad_all - grad_left, hess_all - hess_left, low_right, high_right)
            out_ref[c, pl.ds(b, 1), :] = (left + right) * (-1.0 / kdim)
            return carry

        lax.fori_loop(0, levels, one_bin, 0, unroll=4)


def gains_of(width, levels, lanes, kdim, last, right, left, par_grad, par_hess, bounds, tie):
    return pl.pallas_call(
        functools.partial(gain_kernel, width, levels, kdim),
        in_specs=[VMEM_SPEC] * 6 + [pl.BlockSpec(memory_space=pl.ANY)],
        out_specs=VMEM_SPEC,
        out_shape=jax.ShapeDtypeStruct((2, levels, lanes), jnp.float32),
        scratch_shapes=[
            pltpu.VMEM((2, levels * kdim, lanes), jnp.float32),
            pltpu.VMEM((2, levels, lanes), jnp.float32),
        ],
        compiler_params=pltpu.CompilerParams(vmem_limit_bytes=24 * MIB),
        cost_estimate=pl.CostEstimate(flops=50 * levels * kdim * lanes, bytes_accessed=16 * levels * kdim * lanes, transcendentals=0),
        name="gains",
    )(last, right, left, par_grad, par_hess, bounds, tie)


def finish_kernel(width, route_ref, *refs):
    out_ref = refs[-1]
    chunks = len(refs) - 1
    slab = width * chunks
    lanes = route_ref.shape[1]
    source = route_ref[:1, :]
    total = jnp.zeros((128, 128), jnp.float32)
    column = lax.broadcasted_iota(jnp.int32, (128, 128), 1)
    for child in range(2):
        for c in range(chunks):
            gain = refs[c][0, child]
            for s in range(1, refs[c].shape[0]):
                gain = jnp.where(source == s, refs[c][s, child], gain)
            at = child * slab + c * width
            pieces = []
            for j in range(lanes // width):
                turn = (at - j * width) % lanes
                turned = pltpu.roll(gain, turn, 1) if turn else gain
                pieces.append(turned[:, :128])
            stack = jnp.concatenate(pieces, axis=0)
            total = jnp.where((column >= at) & (column < at + width), stack, total)
    turned = total.T
    for child in range(2):
        out_ref[:, child, :] = turned[child * slab : (child + 1) * slab]


def finish(width, nbins, route, parts):
    return pl.pallas_call(
        functools.partial(finish_kernel, width),
        in_specs=[VMEM_SPEC] * (1 + len(parts)),
        out_specs=VMEM_SPEC,
        out_shape=jax.ShapeDtypeStruct((width * len(parts), 2, nbins), jnp.float32),
        name="finish",
    )(route, *parts)


def one_of(z, members):
    hit = z == members[0]
    for m in members[1:]:
        hit = hit | (z == m)
    return hit


def sum_line(line, chunks, units, unit, set_up):
    plan = plan_of(line)
    z = lax.axis_index("dp")
    from_left = [None] * chunks
    from_right = [None] * chunks
    arrived = []

    def pick(kind, step, c):
        where_at = {}
        for zz in range(line):
            for p, role in enumerate(plan[zz]):
                if role[:2] == (kind, step):
                    where_at.setdefault(p, []).append(zz)
        spots = sorted(where_at)
        value = units[spots[0], c]
        for p in spots[1:]:
            value = jnp.where(one_of(z, where_at[p]), units[p, c], value)
        return value

    def tie_of(step, c):
        at = min(step * chunks + c - 3, (line - 2) * chunks - 1)
        return (arrived[at],) if at >= 0 else (units[0, chunks - 1],)

    last = line - 1
    for step in range(last):
        for c in range(chunks):
            if step > 0:
                units[step, c] = unit(step, c, tie_of(step, c))
            to_right = pick("R", step, c)
            to_left = pick("L", step, c)
            if step > 0:
                to_right = to_right + from_left[c]
                to_left = to_left + from_right[c]
            from_left[c] = lax.ppermute(to_right, "dp", [(i, i + 1) for i in range(step + 1)])
            from_right[c] = lax.ppermute(to_left, "dp", [(line - 1 - i, line - 2 - i) for i in range(step + 1)])
            arrived.append(from_left[c])
    layout = set_up(tie_of(last, 0)[0])
    return [unit(last, c, tie_of(last, c)) for c in range(chunks)], from_left, from_right, layout


def sum_line_of_4(line, chunks, units, unit, set_up):
    inward, outer, middle = [(0, 1), (3, 2)], [(0, 1), (1, 0), (2, 3), (3, 2)], [(1, 2), (2, 1)]
    a0, a1, a2, b1, b2, last = {}, {}, {}, {}, {}, {}
    for c in range(chunks):
        a0[c] = lax.ppermute(units[0, c], "dp", inward)
    last[0] = unit(3, 0, (units[0, chunks - 1],))
    for c in range(chunks):
        units[1, c] = unit(1, c, (a0[c], units[1, c - 1] if c else last[0]))
        b1[c] = lax.ppermute(units[0, c] + a0[c], "dp", middle)
        a1[c] = lax.ppermute(units[1, c], "dp", inward)
    for c in range(chunks):
        units[2, c] = unit(2, c, (a1[c], units[2, c - 1] if c else units[1, chunks - 1]))
        b2[c] = lax.ppermute(units[1, c] + a1[c], "dp", middle)
        a2[c] = lax.ppermute(units[2, c] + b1[c], "dp", outer)
    layout = set_up(units[2, 0])
    for c in range(1, chunks):
        last[c] = unit(3, c, (units[2, chunks - 1],))
    return last, a2, b2, layout


def per_device(bins, grads, hess, node_side, signs, child_owner, parent_owner, parent_grad, parent_hess, node_low, node_high):
    line = lax.axis_size("dp")
    kdim = grads.shape[1]
    nbins = parent_hess.shape[2]
    slab = parent_grad.shape[1]
    chunks = CHUNKS if slab >= 32 else 1
    width = slab // chunks
    lanes = min(256, width * nbins * kdim // 128)
    levels = nbins // (lanes // width)

    own, send, wt, wt_send = prep(line, slab, parent_owner, bins, grads, hess, node_side)
    swap = [(0, 1), (1, 0)]
    wt_other = lax.ppermute(wt_send, "sub", swap)
    other = lax.ppermute(send, "sub", swap)
    mine = (own, wt)
    theirs = (other, wt_other)

    def unit(p, c, pairs, init=None, tie=()):
        return hist(p * slab + c * width, width, levels, lanes, kdim, pairs, init, tie)

    def set_up(tie):
        return parent_layout(
            width, levels, lanes, kdim, chunks, child_owner, parent_owner, node_low, node_high, signs, parent_grad[0], parent_hess[0], tie
        )

    units = {}
    units[0, 0] = unit(0, 0, [theirs], unit(0, 0, [mine]))
    for c in range(1, chunks):
        units[0, c] = unit(0, c, [mine, theirs], tie=(units[0, c - 1],))
    collect = sum_line_of_4 if line == 4 else sum_line
    last, from_left, from_right, layout = collect(line, chunks, units, lambda p, c, tie: unit(p, c, [mine, theirs], tie=tie), set_up)
    par_grad, par_hess, bounds, route = layout

    done = []
    for c in range(chunks):
        gain = gains_of(
            width, levels, lanes, kdim, last[c], from_left[c], from_right[c], par_grad[c], par_hess[c], bounds[c], last[chunks - 1]
        )
        everyone = jnp.broadcast_to(gain[None], (2 * line, *gain.shape))
        done.append(lax.all_to_all(everyone, ("dp", "sub"), 0, 0))
    return finish(width, nbins, route, done)[None]


def solution(mesh):
    return jax.shard_map(
        per_device,
        mesh=mesh,
        in_specs=(
            P(("groups", "dp", "sub"), "feat"),
            P(("groups", "dp", "sub"), None),
            P(("groups", "dp", "sub")),
            P(("groups", "dp", "sub")),
            P("groups"),
            P("groups"),
            P("groups"),
            P(("groups", "dp", "sub"), "feat", None),
            P(("groups", "dp", "sub"), "feat", None),
            P("groups"),
            P("groups"),
        ),
        out_specs=P(("groups", "dp", "sub"), "feat", None, None),
        check_vma=False,
    )
```

```python
import functools

import jax
import jax.numpy as jnp
from jax import lax
from jax.experimental import pallas as pl
from jax.experimental.pallas import tpu as pltpu
from jax.sharding import PartitionSpec as P

reg_lambda = 1.0
CHUNKS = 2
TILE = 256
PACK = 128
FAST = 9
PREP_MIB = 56
MIB = 1024 * 1024
VMEM_SPEC = pl.BlockSpec(memory_space=pltpu.VMEM)
SMEM_SPEC = pl.BlockSpec(memory_space=pltpu.SMEM)


def sum_after_kernel(x_ref, y_ref, tie_ref, out_ref):
    del tie_ref
    out_ref[...] = x_ref[...] + y_ref[...]


def sum_after(x, y, tie):
    return pl.pallas_call(
        sum_after_kernel,
        in_specs=[VMEM_SPEC] * 2 + [pl.BlockSpec(memory_space=pl.ANY)],
        out_specs=VMEM_SPEC,
        out_shape=jax.ShapeDtypeStruct(x.shape, jnp.float32),
        compiler_params=pltpu.CompilerParams(vmem_limit_bytes=16 * MIB),
        cost_estimate=pl.CostEstimate(flops=x.size, bytes_accessed=12 * x.size, transcendentals=0),
        name="sum_after",
    )(x, y, tie)


def plan_of(line):
    roles = []
    for z in range(line):
        mine = []
        for step in range(line - 1):
            now = []
            if z <= step:
                now.append(("R", step, line - 1 - step + z))
            if line - 1 - z <= step:
                now.append(("L", step, step - (line - 1 - z)))
            mine.extend(now if 2 * z < line else now[::-1])
        mine.append(("F", line - 1, z))
        roles.append(mine)
    return roles


def prep_kernel(line, slab, owner_ref, bins_ref, grads_ref, hess_ref, side_ref, own_ref, send_ref, wt_ref, wt_send_ref, buf_ref, sems, acc_ref, acc_w_ref, own_buf, send_buf, out_sems):
    rows, f_dev = bins_ref.shape
    half = f_dev // 2
    kdim = grads_ref.shape[0]
    reach = TILE + PACK
    blocks = rows // TILE
    copies = []
    for i in range(blocks):
        part = pl.ds(i * TILE, TILE)
        copies.append(pltpu.make_async_copy(bins_ref.at[part, :], buf_ref.at[part, :], sems.at[i]))
        copies[-1].start()

    hess_row = hess_ref[...].astype(jnp.float32).reshape(1, rows)
    ones = [jnp.where(side_ref[:, i * TILE : (i + 1) * TILE] == 1, 1.0, 0.0) for i in range(blocks)]
    counts = [jnp.sum(x).astype(jnp.int32) for x in ones]
    bases = [jnp.int32(0)]
    for count in counts:
        bases.append(bases[-1] + count)
    starts = [pl.multiple_of((base // PACK) * PACK, PACK) for base in bases]
    marks = jnp.concatenate(ones, axis=0)
    before = lax.broadcasted_iota(jnp.int32, (TILE, TILE), 0) < lax.broadcasted_iota(jnp.int32, (TILE, TILE), 1)
    before = jnp.where(before, 1.0, 0.0).astype(jnp.bfloat16)
    ahead = jnp.dot(marks.astype(jnp.bfloat16), before, preferred_element_type=jnp.float32).astype(jnp.int32)
    slot = lax.broadcasted_iota(jnp.int32, (reach, TILE), 0)
    acc_ref[:PACK, :] = jnp.zeros((PACK, f_dev), jnp.bfloat16)
    acc_w_ref[:, :PACK] = jnp.zeros((acc_w_ref.shape[0], PACK), jnp.float32)

    z, core = lax.axis_index("dp"), lax.axis_index("sub")
    column = lax.broadcasted_iota(jnp.int32, (1, f_dev), 1)
    position = lax.rem(column, half) // slab
    table = plan_of(line)
    chip = jnp.zeros_like(column)
    for p in range(line):
        target = jnp.int32(0)
        for zz in range(line):
            target = jnp.where(z == zz, jnp.int32(table[zz][p][2]), target)
        chip = jnp.where(position == p, target, chip)
    owner = 2 * chip + jnp.where(column < half, core, 1 - core)
    source = jnp.zeros_like(column)
    for q in range(2 * line):
        source = jnp.where(owner == owner_ref[q], q, source)
    source = source * slab + lax.rem(column, slab)
    perm = jnp.where(lax.broadcasted_iota(jnp.int32, (f_dev, f_dev), 0) == source, 1.0, 0.0).astype(jnp.bfloat16)

    for copy in copies:
        copy.wait()
    for i in range(blocks):
        part = slice(i * TILE, (i + 1) * TILE)
        goal = jnp.where(ones[i] > 0.5, ahead[i : i + 1] + (bases[i] - starts[i]), -1)
        pack = jnp.where(slot == goal, 1.0, 0.0).astype(jnp.bfloat16)
        hess = jnp.broadcast_to(hess_row[:, part], (16, TILE))
        first = lax.broadcasted_iota(jnp.int32, hess.shape, 0) == 0
        weights = jnp.concatenate([grads_ref[:, part].astype(jnp.float32), jnp.where(first, hess, 0.0)], axis=0)
        packed_w = lax.dot_general(weights.astype(jnp.bfloat16), pack, (((1,), (1,)), ((), ())), preferred_element_type=jnp.float32)
        acc_w_ref[:, pl.ds(starts[i], PACK)] += packed_w[:, :PACK]
        acc_w_ref[:, pl.ds(starts[i] + PACK, TILE)] = packed_w[:, PACK:]
        binned = buf_ref[part, :].astype(jnp.float32).astype(jnp.bfloat16)
        packed = jnp.dot(pack, binned, preferred_element_type=jnp.float32).astype(jnp.bfloat16)
        acc_ref[pl.ds(starts[i], PACK), :] += packed[:PACK]
        acc_ref[pl.ds(starts[i] + PACK, TILE), :] = packed[PACK:]

    def move(t, carry):
        part = pl.ds(pl.multiple_of(t * TILE, TILE), TILE)
        moved = jnp.dot(acc_ref[part, :], perm, preferred_element_type=jnp.float32)
        own_buf[part, :] = moved[:, :half].astype(jnp.bfloat16)
        send_buf[part, :] = moved[:, half:]
        pltpu.make_async_copy(own_buf.at[part, :], own_ref.at[part, :], out_sems.at[t, 0]).start()
        pltpu.make_async_copy(send_buf.at[part, :], send_ref.at[part, :], out_sems.at[t, 1]).start()
        return carry

    def moved_out(t, carry):
        part = pl.ds(pl.multiple_of(t * TILE, TILE), TILE)
        pltpu.make_async_copy(own_buf.at[part, :], own_ref.at[part, :], out_sems.at[t, 0]).wait()
        pltpu.make_async_copy(send_buf.at[part, :], send_ref.at[part, :], out_sems.at[t, 1]).wait()
        return carry

    total = bases[blocks]
    used = (total + TILE - 1) // TILE
    lax.fori_loop(0, used, move, 0)
    lane = lax.broadcasted_iota(jnp.int32, (acc_w_ref.shape[0], rows), 1)
    row = lax.broadcasted_iota(jnp.int32, lane.shape, 0)
    packed = jnp.where(lane < total, acc_w_ref[:, :rows], 0.0)
    packs = ((total + PACK - 1) // PACK).astype(jnp.float32)
    packed = jnp.where(row == kdim + 1, packs, packed)
    wt_ref[...] = packed.astype(jnp.bfloat16)
    wt_send_ref[...] = packed[: kdim + 8]
    lax.fori_loop(0, used, moved_out, 0)


def prep(line, slab, owners, bins, grads, hess, side):
    rows, f_dev = bins.shape
    kdim = grads.shape[1]
    half = f_dev // 2
    return pl.pallas_call(
        functools.partial(prep_kernel, line, slab),
        in_specs=[SMEM_SPEC, pl.BlockSpec(memory_space=pl.ANY), VMEM_SPEC, VMEM_SPEC, VMEM_SPEC],
        out_specs=[pl.BlockSpec(memory_space=pl.ANY)] * 2 + [VMEM_SPEC] * 2,
        out_shape=[
            jax.ShapeDtypeStruct((rows, half), jnp.bfloat16),
            jax.ShapeDtypeStruct((rows, half), jnp.float32),
            jax.ShapeDtypeStruct((kdim + 16, rows), jnp.bfloat16),
            jax.ShapeDtypeStruct((kdim + 8, rows), jnp.float32),
        ],
        scratch_shapes=[
            pltpu.VMEM((rows, f_dev), jnp.int32),
            pltpu.SemaphoreType.DMA((rows // TILE,)),
            pltpu.VMEM((rows + TILE + PACK, f_dev), jnp.bfloat16),
            pltpu.VMEM((kdim + 16, rows + TILE + PACK), jnp.float32),
            pltpu.VMEM((rows, half), jnp.bfloat16),
            pltpu.VMEM((rows, half), jnp.float32),
            pltpu.SemaphoreType.DMA((rows // TILE, 2)),
        ],
        compiler_params=pltpu.CompilerParams(vmem_limit_bytes=PREP_MIB * MIB),
        cost_estimate=pl.CostEstimate(flops=4 * rows * f_dev * f_dev, bytes_accessed=8 * rows * f_dev, transcendentals=0),
        name="prep",
    )(owners, bins, grads.T, hess, side.reshape(1, rows))


def tiles_in(wt_ref, kdim):
    return jnp.max(wt_ref[:, :128].astype(jnp.float32)[kdim + 1 : kdim + 2]).astype(jnp.int32)


def hist_kernel(first_column, width, levels, parts, kdim, has_init, *refs):
    pairs = [refs[2 * i : 2 * i + 2] for i in range(parts)]
    init_ref = refs[2 * parts] if has_init else None
    out_ref, rel_ref, wt_ref = refs[-3:]
    lanes = out_ref.shape[1]
    rows, half = pairs[0][0].shape
    src = lax.broadcasted_iota(jnp.int32, (half, lanes), 0)
    dst = lax.broadcasted_iota(jnp.int32, (half, lanes), 1)
    spread = jnp.where(src == first_column + lax.rem(dst, width), 1.0, 0.0).astype(jnp.bfloat16)
    lane = lax.broadcasted_iota(jnp.int32, (1, lanes), 1)
    shift = ((lane // width) * levels).astype(jnp.float32)
    one = jnp.ones((TILE, lanes), jnp.bfloat16)
    zero = jnp.zeros((TILE, lanes), jnp.bfloat16)

    def place_rows(bins_ref, source, target, size):
        block = bins_ref[pl.ds(source, size), :].astype(jnp.bfloat16)
        moved = jnp.dot(block, spread, preferred_element_type=jnp.float32)
        rel_ref[pl.ds(target, size), :] = (moved - shift).astype(jnp.bfloat16)

    def place_weights(height):
        for i, (_, w_ref) in enumerate(pairs):
            weights = w_ref[:, :height]
            if w_ref.dtype != jnp.bfloat16:
                weights = jnp.concatenate([weights, jnp.zeros((8, height), jnp.float32)], axis=0).astype(jnp.bfloat16)
            wt_ref[:, i * height : (i + 1) * height] = weights

    def sums_of(some, tiles):
        values = [jnp.full((TILE, lanes), b.astype(jnp.float32), jnp.float32).astype(jnp.bfloat16) for b in some]
        totals = [jnp.zeros((wt_ref.shape[0], lanes), jnp.float32) for _ in some]
        for first, size in tiles:
            found = rel_ref[pl.ds(first, size), :]
            weights = wt_ref[:, pl.ds(first, size)]
            for i, value in enumerate(values):
                onehot = jnp.where(found == value[:size], one[:size], zero[:size])
                totals[i] = totals[i] + jnp.dot(weights, onehot, preferred_element_type=jnp.float32)
        return [(total[:kdim], total[kdim : kdim + 1]) for total in totals]

    def spots_of(b):
        return pl.ds(pl.multiple_of(b * kdim, kdim), kdim), pl.ds(levels * kdim + b, 1)

    def fast():
        height = FAST * PACK
        for i, (bins_ref, _) in enumerate(pairs):
            for r in range(0, height, 3 * PACK):
                place_rows(bins_ref, r, i * height + r, 3 * PACK)
        place_weights(height)
        tiles = [(r, min(TILE, parts * height - r)) for r in range(0, parts * height, TILE)]

        def two_levels(step, carry):
            some = [2 * step, 2 * step + 1]
            for b, (grad, hess) in zip(some, sums_of(some, tiles)):
                grad_spot, hess_spot = spots_of(b)
                if has_init:
                    grad, hess = grad + init_ref[grad_spot, :], hess + init_ref[hess_spot, :]
                out_ref[grad_spot, :] = grad
                out_ref[hess_spot, :] = hess
            return carry

        lax.fori_loop(0, levels // 2, two_levels, 0)

    def general():
        for i, (bins_ref, _) in enumerate(pairs):

            def one_pack(p, carry):
                r = pl.multiple_of(p * PACK, PACK)
                place_rows(bins_ref, r, i * rows + r, PACK)
                return carry

            lax.fori_loop(0, rows // PACK, one_pack, 0)
        place_weights(rows)
        out_ref[...] = init_ref[...] if has_init else jnp.zeros(out_ref.shape, jnp.float32)
        step = 2 * TILE

        def group(g, carry):
            first = pl.multiple_of(g * step, step)

            def level(b, carry):
                ((grad, hess),) = sums_of([b], [(first, TILE), (first + TILE, TILE)])
                grad_spot, hess_spot = spots_of(b)
                out_ref[grad_spot, :] += grad
                out_ref[hess_spot, :] += hess
                return carry

            return lax.fori_loop(0, levels, level, carry)

        lax.fori_loop(0, parts * rows // step, group, 0)

    needed = tiles_in(pairs[0][1], kdim)
    for _, w_ref in pairs[1:]:
        needed = jnp.maximum(needed, tiles_in(w_ref, kdim))
    if FAST * PACK < rows:
        pl.when(needed <= FAST)(fast)
        pl.when(needed > FAST)(general)
    else:
        general()


def hist(first_column, width, levels, lanes, kdim, pairs, init=None, tie=()):
    rows = pairs[0][0].shape[0]
    parts = len(pairs)
    operands = [x for pair in pairs for x in pair]
    if init is not None:
        operands.append(init)
    specs = [VMEM_SPEC] * len(operands) + [pl.BlockSpec(memory_space=pl.ANY)] * len(tie)
    height = levels * (kdim + 1)
    return pl.pallas_call(
        functools.partial(hist_kernel, first_column, width, levels, parts, kdim, init is not None),
        in_specs=specs,
        out_specs=VMEM_SPEC,
        out_shape=jax.ShapeDtypeStruct((height, lanes), jnp.float32),
        scratch_shapes=[
            pltpu.VMEM((parts * rows, lanes), jnp.bfloat16),
            pltpu.VMEM((kdim + 16, parts * rows), jnp.bfloat16),
        ],
        compiler_params=pltpu.CompilerParams(vmem_limit_bytes=20 * MIB),
        cost_estimate=pl.CostEstimate(
            flops=parts * rows * lanes, bytes_accessed=parts * rows * lanes, transcendentals=0
        ),
        name="hist",
    )(*operands, *tie)


def source_of(place, child_ref, parent_ref):
    source = jnp.int32(0)
    for q in range(child_ref.shape[0]):
        source = jnp.where(child_ref[q] == place, parent_ref[q], source)
    return source


def repeat_lanes(x, width, lanes):
    if lanes > x.shape[1]:
        x = jnp.concatenate([x] * (lanes // x.shape[1]), axis=1)
    x = jnp.where(lax.broadcasted_iota(jnp.int32, x.shape, 1) < width, x[:, :lanes], 0)
    reach = width
    while reach < lanes:
        x = x + pltpu.roll(x, reach, 1)
        reach *= 2
    return x


def layout_kernel(width, levels, kdim, chunks, child_ref, owner_ref, low_ref, high_ref, sign_ref, parent_ref, hess_ref, tie_ref, *out_refs):
    del tie_ref
    grad_refs, hess_refs, bound_refs = out_refs[:chunks], out_refs[chunks : 2 * chunks], out_refs[2 * chunks : 3 * chunks]
    lanes = grad_refs[0].shape[1]
    slab = width * chunks
    owners = owner_ref.shape[0]
    z, core = lax.axis_index("dp"), lax.axis_index("sub")
    place = 2 * z + core
    mine = source_of(place, child_ref, owner_ref)
    twin = source_of(2 * z + 1 - core, child_ref, owner_ref)
    row = lax.broadcasted_iota(jnp.int32, (8, lanes), 0)
    route = jnp.where(row == 0, (mine // 2) ^ z, (twin // 2) ^ z)
    out_refs[-1][...] = jnp.where(row == 2, jnp.where(lax.rem(mine, 2) == core, 1, 0), route)
    slab_at = jnp.int32(0)
    for q in range(owners):
        slab_at = jnp.where(owner_ref[q] == place, q, slab_at)
    offset = lax.axis_index("feat") * (owners * slab) + slab_at * slab
    features = sign_ref.shape[1]
    signs = jnp.broadcast_to(sign_ref[...], (8, features))
    per_tile = 128 // width
    step = 128 // kdim
    for c in range(chunks):
        turned = pltpu.roll(signs, lax.rem(features - offset - c * width + features, features), 1)
        sign = repeat_lanes(turned[:, :128], width, lanes)[:1]
        bounds = []
        for child in range(2):
            low = low_ref[child].astype(jnp.float32) / 1024.0
            high = high_ref[child].astype(jnp.float32) / 1024.0
            middle = 0.5 * (low + high)
            bounds.append(jnp.where(sign < 0, middle, low))
            bounds.append(jnp.where(sign > 0, middle, high))
            bounds.append(jnp.where(sign > 0, middle, low))
            bounds.append(jnp.where(sign < 0, middle, high))
        bound_refs[c][...] = jnp.concatenate(bounds, axis=0)
        rows = hess_ref[c * width : (c + 1) * width, :]
        turned = jnp.concatenate([rows] * (128 // width), axis=0).T
        total = jnp.zeros((levels, lanes), jnp.float32)
        for j in range(lanes // width):
            piece = turned[j * levels : (j + 1) * levels, :]
            piece = jnp.concatenate([piece] * (lanes // 128), axis=1)
            group = lax.broadcasted_iota(jnp.int32, piece.shape, 1) // width
            total = jnp.where(group == j, piece, total)
        hess_refs[c][...] = total
        for tile in range(lanes // 128):
            for b in range(0, levels, step):
                rows = []
                for jj in range(per_tile):
                    bin_at = (tile * per_tile + jj) * levels + b
                    rows.append(parent_ref[c * width : (c + 1) * width, bin_at * kdim : bin_at * kdim + 128])
                block = jnp.concatenate(rows, axis=0) if per_tile > 1 else rows[0]
                grad_refs[c][b * kdim : b * kdim + 128, tile * 128 : (tile + 1) * 128] = block.T


def parent_layout(width, levels, lanes, kdim, chunks, child_owner, owners, low, high, signs, parent, hess, tie):
    shapes = [jax.ShapeDtypeStruct((levels * kdim, lanes), jnp.float32)] * chunks
    shapes += [jax.ShapeDtypeStruct((levels, lanes), jnp.float32)] * chunks
    shapes += [jax.ShapeDtypeStruct((8, lanes), jnp.float32)] * chunks
    shapes += [jax.ShapeDtypeStruct((8, lanes), jnp.int32)]
    out = pl.pallas_call(
        functools.partial(layout_kernel, width, levels, kdim, chunks),
        in_specs=[SMEM_SPEC] * 4 + [VMEM_SPEC] * 3 + [pl.BlockSpec(memory_space=pl.ANY)],
        out_specs=[VMEM_SPEC] * (3 * chunks + 1),
        out_shape=shapes,
        compiler_params=pltpu.CompilerParams(vmem_limit_bytes=16 * MIB),
        cost_estimate=pl.CostEstimate(flops=0, bytes_accessed=2 * parent.size * 4, transcendentals=0),
        name="parent_layout",
    )(child_owner, owners, low, high, signs.reshape(1, -1), parent, hess, tie)
    return out[:chunks], out[chunks : 2 * chunks], out[2 * chunks : 3 * chunks], out[-1]


def lane_prefix(total, width):
    lanes = total.shape[1]
    lane = lax.broadcasted_iota(jnp.int32, total.shape, 1)
    running = total
    reach = width
    while reach < lanes:
        running = running + jnp.where(lane >= reach, pltpu.roll(running, reach, 1), 0.0)
        reach *= 2
    whole = total
    reach = width
    while reach < lanes:
        whole = whole + pltpu.roll(whole, reach, 1)
        reach *= 2
    return running - total, running, whole


def gain_kernel(width, levels, kdim, last_ref, right_ref, left_ref, par_grad_ref, par_hess_ref, bound_ref, tie_ref, out_ref, grad_ref, hess_ref):
    del tie_ref
    hess_at = levels * kdim
    lanes = out_ref.shape[2]

    def small_at(start, size):
        return last_ref[pl.ds(start, size), :] + right_ref[pl.ds(start, size), :] + left_ref[pl.ds(start, size), :]

    small_hess = small_at(hess_at, levels)
    hess_ref[0] = small_hess
    hess_ref[1] = par_hess_ref[...] - small_hess

    def add_up(b, carry):
        g0, g1, h0, h1 = carry
        start = pl.multiple_of(b * kdim, kdim)
        small = small_at(start, kdim)
        g0 = g0 + small
        g1 = g1 + (par_grad_ref[pl.ds(start, kdim), :] - small)
        h0 = h0 + hess_ref[0, pl.ds(b, 1), :]
        h1 = h1 + hess_ref[1, pl.ds(b, 1), :]
        grad_ref[0, pl.ds(start, kdim), :] = g0
        grad_ref[1, pl.ds(start, kdim), :] = g1
        hess_ref[0, pl.ds(b, 1), :] = h0
        hess_ref[1, pl.ds(b, 1), :] = h1
        return g0, g1, h0, h1

    zero_g = jnp.zeros((kdim, lanes), jnp.float32)
    zero_h = jnp.zeros((1, lanes), jnp.float32)
    ends = lax.fori_loop(0, levels, add_up, (zero_g, zero_g, zero_h, zero_h), unroll=4)
    for c in range(2):
        low_left, high_left, low_right, high_right = [bound_ref[4 * c + i : 4 * c + i + 1, :] for i in range(4)]
        grad_before, _, grad_all = lane_prefix(ends[c], width)
        hess_rows = jnp.broadcast_to(ends[2 + c], (8, lanes))
        hess_before, _, hess_all = lane_prefix(hess_rows, width)
        hess_before, hess_all = hess_before[:1], hess_all[:1]

        def score(grad, hess, lower, upper):
            denom = jnp.maximum(hess, 0.0) + reg_lambda
            weight = jnp.clip(-grad / denom, lower, upper)
            return jnp.sum((2.0 * grad + denom * weight) * weight, axis=0, keepdims=True)

        def one_bin(b, carry):
            start = pl.multiple_of(b * kdim, kdim)
            grad_left = grad_ref[c, pl.ds(start, kdim), :] + grad_before
            hess_left = hess_ref[c, pl.ds(b, 1), :] + hess_before
            left = score(grad_left, hess_left, low_left, high_left)
            right = score(grad_all - grad_left, hess_all - hess_left, low_right, high_right)
            out_ref[c, pl.ds(b, 1), :] = (left + right) * (-1.0 / kdim)
            return carry

        lax.fori_loop(0, levels, one_bin, 0, unroll=4)


def gains_of(width, levels, lanes, kdim, last, right, left, par_grad, par_hess, bounds, tie):
    return pl.pallas_call(
        functools.partial(gain_kernel, width, levels, kdim),
        in_specs=[VMEM_SPEC] * 6 + [pl.BlockSpec(memory_space=pl.ANY)],
        out_specs=VMEM_SPEC,
        out_shape=jax.ShapeDtypeStruct((2, levels, lanes), jnp.float32),
        scratch_shapes=[
            pltpu.VMEM((2, levels * kdim, lanes), jnp.float32),
            pltpu.VMEM((2, levels, lanes), jnp.float32),
        ],
        compiler_params=pltpu.CompilerParams(vmem_limit_bytes=24 * MIB),
        cost_estimate=pl.CostEstimate(flops=50 * levels * kdim * lanes, bytes_accessed=16 * levels * kdim * lanes, transcendentals=0),
        name="gains",
    )(last, right, left, par_grad, par_hess, bounds, tie)


def chosen(shift, got):
    value = got[0]
    for s in range(1, len(got)):
        value = jnp.where(shift == s, got[s], value)
    return value


def finish_kernel(width, line, route_ref, *refs):
    out_ref = refs[-1]
    chunks = (len(refs) - 1) // (line + 1)
    slab = width * chunks
    lanes = route_ref.shape[1]
    shift, same = route_ref[:1, :], route_ref[2:3, :]
    total = jnp.zeros((128, 128), jnp.float32)
    column = lax.broadcasted_iota(jnp.int32, (128, 128), 1)
    for child in range(2):
        for c in range(chunks):
            got = [ref[child] for ref in refs[c * (line + 1) : (c + 1) * (line + 1)]]
            gain = jnp.where(same == 1, chosen(shift, got[:line]), got[line])
            at = child * slab + c * width
            pieces = []
            for j in range(lanes // width):
                turn = (at - j * width) % lanes
                turned = pltpu.roll(gain, turn, 1) if turn else gain
                pieces.append(turned[:, :128])
            stack = jnp.concatenate(pieces, axis=0)
            total = jnp.where((column >= at) & (column < at + width), stack, total)
    turned = total.T
    for child in range(2):
        out_ref[:, child, :] = turned[child * slab : (child + 1) * slab]


def finish(width, nbins, line, route, parts):
    flat = [x for part in parts for x in part]
    return pl.pallas_call(
        functools.partial(finish_kernel, width, line),
        in_specs=[VMEM_SPEC] * (1 + len(flat)),
        out_specs=VMEM_SPEC,
        out_shape=jax.ShapeDtypeStruct((width * len(parts), 2, nbins), jnp.float32),
        name="finish",
    )(route, *flat)


def one_of(z, members):
    hit = z == members[0]
    for m in members[1:]:
        hit = hit | (z == m)
    return hit


def sum_line(line, chunks, units, unit, set_up):
    plan = plan_of(line)
    z = lax.axis_index("dp")
    from_left = [None] * chunks
    from_right = [None] * chunks
    arrived = []

    def pick(kind, step, c):
        where_at = {}
        for zz in range(line):
            for p, role in enumerate(plan[zz]):
                if role[:2] == (kind, step):
                    where_at.setdefault(p, []).append(zz)
        spots = sorted(where_at)
        value = units[spots[0], c]
        for p in spots[1:]:
            value = jnp.where(one_of(z, where_at[p]), units[p, c], value)
        return value

    def tie_of(step, c):
        at = min(step * chunks + c - 3, (line - 2) * chunks - 1)
        return (arrived[at],) if at >= 0 else (units[0, chunks - 1],)

    last = line - 1
    for step in range(last):
        for c in range(chunks):
            if step > 0:
                units[step, c] = unit(step, c, tie_of(step, c))
            to_right = pick("R", step, c)
            to_left = pick("L", step, c)
            if step > 0:
                to_right = to_right + from_left[c]
                to_left = to_left + from_right[c]
            from_left[c] = lax.ppermute(to_right, "dp", [(i, i + 1) for i in range(step + 1)])
            from_right[c] = lax.ppermute(to_left, "dp", [(line - 1 - i, line - 2 - i) for i in range(step + 1)])
            arrived.append(from_left[c])
    layout = set_up(tie_of(last, 0)[0])
    return [unit(last, c, tie_of(last, c)) for c in range(chunks)], from_left, from_right, layout


def sum_line_of_4(line, chunks, units, unit, set_up):
    inward, outer, middle = [(0, 1), (3, 2)], [(0, 1), (1, 0), (2, 3), (3, 2)], [(1, 2), (2, 1)]
    a0, a1, a2, b1, b2, last = {}, {}, {}, {}, {}, {}
    final = chunks - 1
    for c in range(chunks):
        a0[c] = lax.ppermute(units[0, c], "dp", inward)
    for c in range(chunks):
        units[1, c] = unit(1, c, (units[1, c - 1] if c else units[0, final],))
        a1[c] = lax.ppermute(units[1, c], "dp", inward)
        b1[c] = lax.ppermute(sum_after(units[0, c], a0[c], units[1, c]), "dp", middle)
    for c in range(chunks):
        units[2, c] = unit(2, c, (units[2, c - 1], b1[c - 1], a1[c - 1]) if c else (units[1, final], a0[final]))
        a2[c] = lax.ppermute(units[2, c] + b1[c], "dp", outer)
    for c in range(chunks):
        last[c] = unit(3, c, (last[c - 1], a1[c]) if c else (units[2, final], b1[final]))
    for c in range(chunks):
        b2[c] = lax.ppermute(sum_after(units[1, c], a1[c], last[c - 1] if c else units[2, c]), "dp", middle)
    return last, a2, b2, set_up(last[final])


def per_device(bins, grads, hess, node_side, signs, child_owner, parent_owner, parent_grad, parent_hess, node_low, node_high):
    line = lax.axis_size("dp")
    kdim = grads.shape[1]
    nbins = parent_hess.shape[2]
    slab = parent_grad.shape[1]
    chunks = CHUNKS if slab >= 32 else 1
    width = slab // chunks
    lanes = min(256, width * nbins * kdim // 128)
    levels = nbins // (lanes // width)

    own, send, wt, wt_send = prep(line, slab, parent_owner, bins, grads, hess, node_side)
    swap = [(0, 1), (1, 0)]
    wt_other = lax.ppermute(wt_send, "sub", swap)
    other = lax.ppermute(send, "sub", swap)
    mine = (own, wt)
    theirs = (other, wt_other)

    def unit(p, c, pairs, init=None, tie=()):
        return hist(p * slab + c * width, width, levels, lanes, kdim, pairs, init, tie)

    def set_up(tie):
        return parent_layout(
            width, levels, lanes, kdim, chunks, child_owner, parent_owner, node_low, node_high, signs, parent_grad[0], parent_hess[0], tie
        )

    units = {}
    units[0, 0] = unit(0, 0, [theirs], unit(0, 0, [mine]))
    for c in range(1, chunks):
        units[0, c] = unit(0, c, [mine, theirs], tie=(units[0, c - 1],))
    collect = sum_line_of_4 if line == 4 else sum_line
    last, from_left, from_right, layout = collect(line, chunks, units, lambda p, c, tie: unit(p, c, [mine, theirs], tie=tie), set_up)
    par_grad, par_hess, bounds, route = layout

    done = []
    for c in range(chunks):
        gain = gains_of(
            width, levels, lanes, kdim, last[c], from_left[c], from_right[c], par_grad[c], par_hess[c], bounds[c], last[chunks - 1]
        )
        got = [gain] + [lax.ppermute(gain, "dp", [(i, i ^ s) for i in range(line)]) for s in range(1, line)]
        crossed = lax.ppermute(chosen(route[1, 0], got), "sub", swap)
        done.append([*got, crossed])
    return finish(width, nbins, line, route, done)[None]


def solution(mesh):
    return jax.shard_map(
        per_device,
        mesh=mesh,
        in_specs=(
            P(("groups", "dp", "sub"), "feat"),
            P(("groups", "dp", "sub"), None),
            P(("groups", "dp", "sub")),
            P(("groups", "dp", "sub")),
            P("groups"),
            P("groups"),
            P("groups"),
            P(("groups", "dp", "sub"), "feat", None),
            P(("groups", "dp", "sub"), "feat", None),
            P("groups"),
            P("groups"),
        ),
        out_specs=P(("groups", "dp", "sub"), "feat", None, None),
        check_vma=False,
    )
```

```python
import functools

import jax
import jax.numpy as jnp
from jax import lax
from jax.experimental import pallas as pl
from jax.experimental.pallas import tpu as pltpu
from jax.sharding import PartitionSpec as P

reg_lambda = 1.0
CHUNKS = 2
TILE = 256
PACK = 128
FAST = 9
HEAD = 5
PREP_MIB = 56
MIB = 1024 * 1024
VMEM_SPEC = pl.BlockSpec(memory_space=pltpu.VMEM)
SMEM_SPEC = pl.BlockSpec(memory_space=pltpu.SMEM)


def sum_after_kernel(x_ref, y_ref, tie_ref, out_ref):
    del tie_ref
    out_ref[...] = x_ref[...] + y_ref[...]


def sum_after(x, y, tie):
    return pl.pallas_call(
        sum_after_kernel,
        in_specs=[VMEM_SPEC] * 2 + [pl.BlockSpec(memory_space=pl.ANY)],
        out_specs=VMEM_SPEC,
        out_shape=jax.ShapeDtypeStruct(x.shape, jnp.float32),
        compiler_params=pltpu.CompilerParams(vmem_limit_bytes=16 * MIB),
        cost_estimate=pl.CostEstimate(flops=x.size, bytes_accessed=12 * x.size, transcendentals=0),
        name="sum_after",
    )(x, y, tie)


def plan_of(line):
    roles = []
    for z in range(line):
        mine = []
        for step in range(line - 1):
            now = []
            if z <= step:
                now.append(("R", step, line - 1 - step + z))
            if line - 1 - z <= step:
                now.append(("L", step, step - (line - 1 - z)))
            mine.extend(now if 2 * z < line else now[::-1])
        mine.append(("F", line - 1, z))
        roles.append(mine)
    return roles


def prep_kernel(line, slab, owner_ref, bins_ref, grads_ref, hess_ref, side_ref, own_ref, send_ref, wt_ref, wt_send_ref, buf_ref, sems, acc_ref, acc_w_ref, own_buf, send_buf, out_sems):
    rows, f_dev = bins_ref.shape
    half = f_dev // 2
    kdim = grads_ref.shape[0]
    reach = TILE + PACK
    blocks = rows // TILE
    copies = []
    for i in range(blocks):
        part = pl.ds(i * TILE, TILE)
        copies.append(pltpu.make_async_copy(bins_ref.at[part, :], buf_ref.at[part, :], sems.at[i]))
        copies[-1].start()

    hess_row = hess_ref[...].astype(jnp.float32).reshape(1, rows)
    ones = [jnp.where(side_ref[:, i * TILE : (i + 1) * TILE] == 1, 1.0, 0.0) for i in range(blocks)]
    counts = [jnp.sum(x).astype(jnp.int32) for x in ones]
    bases = [jnp.int32(0)]
    for count in counts:
        bases.append(bases[-1] + count)
    starts = [pl.multiple_of((base // PACK) * PACK, PACK) for base in bases]
    marks = jnp.concatenate(ones, axis=0)
    before = lax.broadcasted_iota(jnp.int32, (TILE, TILE), 0) < lax.broadcasted_iota(jnp.int32, (TILE, TILE), 1)
    before = jnp.where(before, 1.0, 0.0).astype(jnp.bfloat16)
    ahead = jnp.dot(marks.astype(jnp.bfloat16), before, preferred_element_type=jnp.float32).astype(jnp.int32)
    slot = lax.broadcasted_iota(jnp.int32, (reach, TILE), 0)
    acc_ref[:PACK, :] = jnp.zeros((PACK, f_dev), jnp.bfloat16)
    acc_w_ref[:, :PACK] = jnp.zeros((acc_w_ref.shape[0], PACK), jnp.float32)

    z, core = lax.axis_index("dp"), lax.axis_index("sub")
    column = lax.broadcasted_iota(jnp.int32, (1, f_dev), 1)
    position = lax.rem(column, half) // slab
    table = plan_of(line)
    chip = jnp.zeros_like(column)
    for p in range(line):
        target = jnp.int32(0)
        for zz in range(line):
            target = jnp.where(z == zz, jnp.int32(table[zz][p][2]), target)
        chip = jnp.where(position == p, target, chip)
    owner = 2 * chip + jnp.where(column < half, core, 1 - core)
    source = jnp.zeros_like(column)
    for q in range(2 * line):
        source = jnp.where(owner == owner_ref[q], q, source)
    source = source * slab + lax.rem(column, slab)
    perm = jnp.where(lax.broadcasted_iota(jnp.int32, (f_dev, f_dev), 0) == source, 1.0, 0.0).astype(jnp.bfloat16)

    for copy in copies:
        copy.wait()
    for i in range(blocks):
        part = slice(i * TILE, (i + 1) * TILE)
        goal = jnp.where(ones[i] > 0.5, ahead[i : i + 1] + (bases[i] - starts[i]), -1)
        pack = jnp.where(slot == goal, 1.0, 0.0).astype(jnp.bfloat16)
        hess = jnp.broadcast_to(hess_row[:, part], (16, TILE))
        first = lax.broadcasted_iota(jnp.int32, hess.shape, 0) == 0
        weights = jnp.concatenate([grads_ref[:, part].astype(jnp.float32), jnp.where(first, hess, 0.0)], axis=0)
        packed_w = lax.dot_general(weights.astype(jnp.bfloat16), pack, (((1,), (1,)), ((), ())), preferred_element_type=jnp.float32)
        acc_w_ref[:, pl.ds(starts[i], PACK)] += packed_w[:, :PACK]
        acc_w_ref[:, pl.ds(starts[i] + PACK, TILE)] = packed_w[:, PACK:]
        binned = buf_ref[part, :].astype(jnp.float32).astype(jnp.bfloat16)
        packed = jnp.dot(pack, binned, preferred_element_type=jnp.float32).astype(jnp.bfloat16)
        acc_ref[pl.ds(starts[i], PACK), :] += packed[:PACK]
        acc_ref[pl.ds(starts[i] + PACK, TILE), :] = packed[PACK:]

    def move(t, carry):
        part = pl.ds(pl.multiple_of(t * TILE, TILE), TILE)
        moved = jnp.dot(acc_ref[part, :], perm, preferred_element_type=jnp.float32)
        own_buf[part, :] = moved[:, :half].astype(jnp.bfloat16)
        send_buf[part, :] = moved[:, half:]
        pltpu.make_async_copy(own_buf.at[part, :], own_ref.at[part, :], out_sems.at[t, 0]).start()
        pltpu.make_async_copy(send_buf.at[part, :], send_ref.at[part, :], out_sems.at[t, 1]).start()
        return carry

    def moved_out(t, carry):
        part = pl.ds(pl.multiple_of(t * TILE, TILE), TILE)
        pltpu.make_async_copy(own_buf.at[part, :], own_ref.at[part, :], out_sems.at[t, 0]).wait()
        pltpu.make_async_copy(send_buf.at[part, :], send_ref.at[part, :], out_sems.at[t, 1]).wait()
        return carry

    total = bases[blocks]
    used = jnp.maximum((total + TILE - 1) // TILE, HEAD)
    head = pl.ds(0, HEAD * TILE)
    send_buf[head, :] = jnp.dot(acc_ref[head, :], perm[:, half:], preferred_element_type=jnp.float32)
    send_head = pltpu.make_async_copy(send_buf.at[head, :], send_ref.at[head, :], out_sems.at[0, 1])
    send_head.start()
    own_buf[head, :] = jnp.dot(acc_ref[head, :], perm[:, :half], preferred_element_type=jnp.float32).astype(jnp.bfloat16)
    own_head = pltpu.make_async_copy(own_buf.at[head, :], own_ref.at[head, :], out_sems.at[0, 0])
    own_head.start()
    lax.fori_loop(HEAD, used, move, 0)
    lane = lax.broadcasted_iota(jnp.int32, (acc_w_ref.shape[0], rows), 1)
    row = lax.broadcasted_iota(jnp.int32, lane.shape, 0)
    packed = jnp.where(lane < total, acc_w_ref[:, :rows], 0.0)
    packs = ((total + PACK - 1) // PACK).astype(jnp.float32)
    packed = jnp.where(row == kdim + 1, packs, packed)
    wt_ref[...] = packed.astype(jnp.bfloat16)
    wt_send_ref[...] = packed[: kdim + 8]
    send_head.wait()
    own_head.wait()
    lax.fori_loop(HEAD, used, moved_out, 0)


def prep(line, slab, owners, bins, grads, hess, side):
    rows, f_dev = bins.shape
    kdim = grads.shape[1]
    half = f_dev // 2
    return pl.pallas_call(
        functools.partial(prep_kernel, line, slab),
        in_specs=[SMEM_SPEC, pl.BlockSpec(memory_space=pl.ANY), VMEM_SPEC, VMEM_SPEC, VMEM_SPEC],
        out_specs=[pl.BlockSpec(memory_space=pl.ANY)] * 2 + [VMEM_SPEC] * 2,
        out_shape=[
            jax.ShapeDtypeStruct((rows, half), jnp.bfloat16),
            jax.ShapeDtypeStruct((rows, half), jnp.float32),
            jax.ShapeDtypeStruct((kdim + 16, rows), jnp.bfloat16),
            jax.ShapeDtypeStruct((kdim + 8, rows), jnp.float32),
        ],
        scratch_shapes=[
            pltpu.VMEM((rows, f_dev), jnp.int32),
            pltpu.SemaphoreType.DMA((rows // TILE,)),
            pltpu.VMEM((rows + TILE + PACK, f_dev), jnp.bfloat16),
            pltpu.VMEM((kdim + 16, rows + TILE + PACK), jnp.float32),
            pltpu.VMEM((rows, half), jnp.bfloat16),
            pltpu.VMEM((rows, half), jnp.float32),
            pltpu.SemaphoreType.DMA((rows // TILE, 2)),
        ],
        compiler_params=pltpu.CompilerParams(vmem_limit_bytes=PREP_MIB * MIB),
        cost_estimate=pl.CostEstimate(flops=4 * rows * f_dev * f_dev, bytes_accessed=8 * rows * f_dev, transcendentals=0),
        name="prep",
    )(owners, bins, grads.T, hess, side.reshape(1, rows))


def tiles_in(wt_ref, kdim):
    return jnp.max(wt_ref[:, :128].astype(jnp.float32)[kdim + 1 : kdim + 2]).astype(jnp.int32)


def hist_kernel(first_column, width, levels, parts, kdim, has_init, *refs):
    pairs = [refs[2 * i : 2 * i + 2] for i in range(parts)]
    init_ref = refs[2 * parts] if has_init else None
    out_ref, rel_ref, wt_ref = refs[-3:]
    lanes = out_ref.shape[1]
    rows, half = pairs[0][0].shape
    src = lax.broadcasted_iota(jnp.int32, (half, lanes), 0)
    dst = lax.broadcasted_iota(jnp.int32, (half, lanes), 1)
    spread = jnp.where(src == first_column + lax.rem(dst, width), 1.0, 0.0).astype(jnp.bfloat16)
    lane = lax.broadcasted_iota(jnp.int32, (1, lanes), 1)
    shift = ((lane // width) * levels).astype(jnp.float32)
    one = jnp.ones((TILE, lanes), jnp.bfloat16)
    zero = jnp.zeros((TILE, lanes), jnp.bfloat16)

    def place_rows(bins_ref, source, target, size):
        block = bins_ref[pl.ds(source, size), :].astype(jnp.bfloat16)
        moved = jnp.dot(block, spread, preferred_element_type=jnp.float32)
        rel_ref[pl.ds(target, size), :] = (moved - shift).astype(jnp.bfloat16)

    def place_weights(height):
        for i, (_, w_ref) in enumerate(pairs):
            weights = w_ref[:, :height]
            if w_ref.dtype != jnp.bfloat16:
                weights = jnp.concatenate([weights, jnp.zeros((8, height), jnp.float32)], axis=0).astype(jnp.bfloat16)
            wt_ref[:, i * height : (i + 1) * height] = weights

    def sums_of(some, tiles):
        values = [jnp.full((TILE, lanes), b.astype(jnp.float32), jnp.float32).astype(jnp.bfloat16) for b in some]
        totals = [jnp.zeros((wt_ref.shape[0], lanes), jnp.float32) for _ in some]
        for first, size in tiles:
            found = rel_ref[pl.ds(first, size), :]
            weights = wt_ref[:, pl.ds(first, size)]
            for i, value in enumerate(values):
                onehot = jnp.where(found == value[:size], one[:size], zero[:size])
                totals[i] = totals[i] + jnp.dot(weights, onehot, preferred_element_type=jnp.float32)
        return [(total[:kdim], total[kdim : kdim + 1]) for total in totals]

    def spots_of(b):
        return pl.ds(pl.multiple_of(b * kdim, kdim), kdim), pl.ds(levels * kdim + b, 1)

    def fast():
        height = FAST * PACK
        for i, (bins_ref, _) in enumerate(pairs):
            for r in range(0, height, 3 * PACK):
                place_rows(bins_ref, r, i * height + r, 3 * PACK)
        place_weights(height)
        tiles = [(r, min(TILE, parts * height - r)) for r in range(0, parts * height, TILE)]

        together = 4 if parts == 1 and levels % 4 == 0 else 2

        def some_levels(step, carry):
            some = [together * step + i for i in range(together)]
            for b, (grad, hess) in zip(some, sums_of(some, tiles)):
                grad_spot, hess_spot = spots_of(b)
                if has_init:
                    grad, hess = grad + init_ref[grad_spot, :], hess + init_ref[hess_spot, :]
                out_ref[grad_spot, :] = grad
                out_ref[hess_spot, :] = hess
            return carry

        lax.fori_loop(0, levels // together, some_levels, 0)

    def general():
        for i, (bins_ref, _) in enumerate(pairs):

            def one_pack(p, carry):
                r = pl.multiple_of(p * PACK, PACK)
                place_rows(bins_ref, r, i * rows + r, PACK)
                return carry

            lax.fori_loop(0, rows // PACK, one_pack, 0)
        place_weights(rows)
        out_ref[...] = init_ref[...] if has_init else jnp.zeros(out_ref.shape, jnp.float32)
        step = 2 * TILE

        def group(g, carry):
            first = pl.multiple_of(g * step, step)

            def level(b, carry):
                ((grad, hess),) = sums_of([b], [(first, TILE), (first + TILE, TILE)])
                grad_spot, hess_spot = spots_of(b)
                out_ref[grad_spot, :] += grad
                out_ref[hess_spot, :] += hess
                return carry

            return lax.fori_loop(0, levels, level, carry)

        lax.fori_loop(0, parts * rows // step, group, 0)

    needed = tiles_in(pairs[0][1], kdim)
    for _, w_ref in pairs[1:]:
        needed = jnp.maximum(needed, tiles_in(w_ref, kdim))
    if FAST * PACK < rows:
        pl.when(needed <= FAST)(fast)
        pl.when(needed > FAST)(general)
    else:
        general()


def hist(first_column, width, levels, lanes, kdim, pairs, init=None, tie=()):
    rows = pairs[0][0].shape[0]
    parts = len(pairs)
    operands = [x for pair in pairs for x in pair]
    if init is not None:
        operands.append(init)
    specs = [VMEM_SPEC] * len(operands) + [pl.BlockSpec(memory_space=pl.ANY)] * len(tie)
    height = levels * (kdim + 1)
    return pl.pallas_call(
        functools.partial(hist_kernel, first_column, width, levels, parts, kdim, init is not None),
        in_specs=specs,
        out_specs=VMEM_SPEC,
        out_shape=jax.ShapeDtypeStruct((height, lanes), jnp.float32),
        scratch_shapes=[
            pltpu.VMEM((parts * rows, lanes), jnp.bfloat16),
            pltpu.VMEM((kdim + 16, parts * rows), jnp.bfloat16),
        ],
        compiler_params=pltpu.CompilerParams(vmem_limit_bytes=20 * MIB),
        cost_estimate=pl.CostEstimate(
            flops=parts * rows * lanes, bytes_accessed=parts * rows * lanes, transcendentals=0
        ),
        name="hist",
    )(*operands, *tie)


def source_of(place, child_ref, parent_ref):
    source = jnp.int32(0)
    for q in range(child_ref.shape[0]):
        source = jnp.where(child_ref[q] == place, parent_ref[q], source)
    return source


def repeat_lanes(x, width, lanes):
    if lanes > x.shape[1]:
        x = jnp.concatenate([x] * (lanes // x.shape[1]), axis=1)
    x = jnp.where(lax.broadcasted_iota(jnp.int32, x.shape, 1) < width, x[:, :lanes], 0)
    reach = width
    while reach < lanes:
        x = x + pltpu.roll(x, reach, 1)
        reach *= 2
    return x


def layout_kernel(width, levels, kdim, chunks, child_ref, owner_ref, low_ref, high_ref, sign_ref, parent_ref, hess_ref, tie_ref, *out_refs):
    del tie_ref
    grad_refs, hess_refs, bound_refs = out_refs[:chunks], out_refs[chunks : 2 * chunks], out_refs[2 * chunks : 3 * chunks]
    lanes = grad_refs[0].shape[1]
    slab = width * chunks
    owners = owner_ref.shape[0]
    z, core = lax.axis_index("dp"), lax.axis_index("sub")
    place = 2 * z + core
    mine = source_of(place, child_ref, owner_ref)
    twin = source_of(2 * z + 1 - core, child_ref, owner_ref)
    row = lax.broadcasted_iota(jnp.int32, (8, lanes), 0)
    route = jnp.where(row == 0, (mine // 2) ^ z, (twin // 2) ^ z)
    out_refs[-1][...] = jnp.where(row == 2, jnp.where(lax.rem(mine, 2) == core, 1, 0), route)
    slab_at = jnp.int32(0)
    for q in range(owners):
        slab_at = jnp.where(owner_ref[q] == place, q, slab_at)
    offset = lax.axis_index("feat") * (owners * slab) + slab_at * slab
    features = sign_ref.shape[1]
    signs = jnp.broadcast_to(sign_ref[...], (8, features))
    per_tile = 128 // width
    step = 128 // kdim
    for c in range(chunks):
        turned = pltpu.roll(signs, lax.rem(features - offset - c * width + features, features), 1)
        sign = repeat_lanes(turned[:, :128], width, lanes)[:1]
        bounds = []
        for child in range(2):
            low = low_ref[child].astype(jnp.float32) / 1024.0
            high = high_ref[child].astype(jnp.float32) / 1024.0
            middle = 0.5 * (low + high)
            bounds.append(jnp.where(sign < 0, middle, low))
            bounds.append(jnp.where(sign > 0, middle, high))
            bounds.append(jnp.where(sign > 0, middle, low))
            bounds.append(jnp.where(sign < 0, middle, high))
        bound_refs[c][...] = jnp.concatenate(bounds, axis=0)
        rows = hess_ref[c * width : (c + 1) * width, :]
        turned = jnp.concatenate([rows] * (128 // width), axis=0).T
        total = jnp.zeros((levels, lanes), jnp.float32)
        for j in range(lanes // width):
            piece = turned[j * levels : (j + 1) * levels, :]
            piece = jnp.concatenate([piece] * (lanes // 128), axis=1)
            group = lax.broadcasted_iota(jnp.int32, piece.shape, 1) // width
            total = jnp.where(group == j, piece, total)
        hess_refs[c][...] = total
        for tile in range(lanes // 128):
            for b in range(0, levels, step):
                rows = []
                for jj in range(per_tile):
                    bin_at = (tile * per_tile + jj) * levels + b
                    rows.append(parent_ref[c * width : (c + 1) * width, bin_at * kdim : bin_at * kdim + 128])
                block = jnp.concatenate(rows, axis=0) if per_tile > 1 else rows[0]
                grad_refs[c][b * kdim : b * kdim + 128, tile * 128 : (tile + 1) * 128] = block.T


def parent_layout(width, levels, lanes, kdim, chunks, child_owner, owners, low, high, signs, parent, hess, tie):
    shapes = [jax.ShapeDtypeStruct((levels * kdim, lanes), jnp.float32)] * chunks
    shapes += [jax.ShapeDtypeStruct((levels, lanes), jnp.float32)] * chunks
    shapes += [jax.ShapeDtypeStruct((8, lanes), jnp.float32)] * chunks
    shapes += [jax.ShapeDtypeStruct((8, lanes), jnp.int32)]
    out = pl.pallas_call(
        functools.partial(layout_kernel, width, levels, kdim, chunks),
        in_specs=[SMEM_SPEC] * 4 + [VMEM_SPEC] * 3 + [pl.BlockSpec(memory_space=pl.ANY)],
        out_specs=[VMEM_SPEC] * (3 * chunks + 1),
        out_shape=shapes,
        compiler_params=pltpu.CompilerParams(vmem_limit_bytes=16 * MIB),
        cost_estimate=pl.CostEstimate(flops=0, bytes_accessed=2 * parent.size * 4, transcendentals=0),
        name="parent_layout",
    )(child_owner, owners, low, high, signs.reshape(1, -1), parent, hess, tie)
    return out[:chunks], out[chunks : 2 * chunks], out[2 * chunks : 3 * chunks], out[-1]


def lane_prefix(total, width):
    lanes = total.shape[1]
    lane = lax.broadcasted_iota(jnp.int32, total.shape, 1)
    running = total
    reach = width
    while reach < lanes:
        running = running + jnp.where(lane >= reach, pltpu.roll(running, reach, 1), 0.0)
        reach *= 2
    whole = total
    reach = width
    while reach < lanes:
        whole = whole + pltpu.roll(whole, reach, 1)
        reach *= 2
    return running - total, running, whole


def gain_kernel(width, levels, kdim, last_ref, right_ref, left_ref, par_grad_ref, par_hess_ref, bound_ref, tie_ref, out_ref, grad_ref, hess_ref):
    del tie_ref
    hess_at = levels * kdim
    lanes = out_ref.shape[2]

    def small_at(start, size):
        return last_ref[pl.ds(start, size), :] + right_ref[pl.ds(start, size), :] + left_ref[pl.ds(start, size), :]

    small_hess = small_at(hess_at, levels)
    hess_ref[0] = small_hess
    hess_ref[1] = par_hess_ref[...] - small_hess

    def add_up(b, carry):
        g0, g1, h0, h1 = carry
        start = pl.multiple_of(b * kdim, kdim)
        small = small_at(start, kdim)
        g0 = g0 + small
        g1 = g1 + (par_grad_ref[pl.ds(start, kdim), :] - small)
        h0 = h0 + hess_ref[0, pl.ds(b, 1), :]
        h1 = h1 + hess_ref[1, pl.ds(b, 1), :]
        grad_ref[0, pl.ds(start, kdim), :] = g0
        grad_ref[1, pl.ds(start, kdim), :] = g1
        hess_ref[0, pl.ds(b, 1), :] = h0
        hess_ref[1, pl.ds(b, 1), :] = h1
        return g0, g1, h0, h1

    zero_g = jnp.zeros((kdim, lanes), jnp.float32)
    zero_h = jnp.zeros((1, lanes), jnp.float32)
    ends = lax.fori_loop(0, levels, add_up, (zero_g, zero_g, zero_h, zero_h), unroll=4)
    for c in range(2):
        low_left, high_left, low_right, high_right = [bound_ref[4 * c + i : 4 * c + i + 1, :] for i in range(4)]
        grad_before, _, grad_all = lane_prefix(ends[c], width)
        hess_rows = jnp.broadcast_to(ends[2 + c], (8, lanes))
        hess_before, _, hess_all = lane_prefix(hess_rows, width)
        hess_before, hess_all = hess_before[:1], hess_all[:1]

        def score(grad, hess, lower, upper):
            denom = jnp.maximum(hess, 0.0) + reg_lambda
            weight = jnp.clip(-grad / denom, lower, upper)
            return jnp.sum((2.0 * grad + denom * weight) * weight, axis=0, keepdims=True)

        def one_bin(b, carry):
            start = pl.multiple_of(b * kdim, kdim)
            grad_left = grad_ref[c, pl.ds(start, kdim), :] + grad_before
            hess_left = hess_ref[c, pl.ds(b, 1), :] + hess_before
            left = score(grad_left, hess_left, low_left, high_left)
            right = score(grad_all - grad_left, hess_all - hess_left, low_right, high_right)
            out_ref[c, pl.ds(b, 1), :] = (left + right) * (-1.0 / kdim)
            return carry

        lax.fori_loop(0, levels, one_bin, 0, unroll=4)


def gains_of(width, levels, lanes, kdim, last, right, left, par_grad, par_hess, bounds, tie):
    return pl.pallas_call(
        functools.partial(gain_kernel, width, levels, kdim),
        in_specs=[VMEM_SPEC] * 6 + [pl.BlockSpec(memory_space=pl.ANY)],
        out_specs=VMEM_SPEC,
        out_shape=jax.ShapeDtypeStruct((2, levels, lanes), jnp.float32),
        scratch_shapes=[
            pltpu.VMEM((2, levels * kdim, lanes), jnp.float32),
            pltpu.VMEM((2, levels, lanes), jnp.float32),
        ],
        compiler_params=pltpu.CompilerParams(vmem_limit_bytes=24 * MIB),
        cost_estimate=pl.CostEstimate(flops=50 * levels * kdim * lanes, bytes_accessed=16 * levels * kdim * lanes, transcendentals=0),
        name="gains",
    )(last, right, left, par_grad, par_hess, bounds, tie)


def chosen(shift, got):
    value = got[0]
    for s in range(1, len(got)):
        value = jnp.where(shift == s, got[s], value)
    return value


def finish_kernel(width, line, route_ref, *refs):
    out_ref = refs[-1]
    chunks = (len(refs) - 1) // (line + 1)
    slab = width * chunks
    lanes = route_ref.shape[1]
    shift, same = route_ref[:1, :], route_ref[2:3, :]
    total = jnp.zeros((128, 128), jnp.float32)
    column = lax.broadcasted_iota(jnp.int32, (128, 128), 1)
    for child in range(2):
        for c in range(chunks):
            got = [ref[child] for ref in refs[c * (line + 1) : (c + 1) * (line + 1)]]
            gain = jnp.where(same == 1, chosen(shift, got[:line]), got[line])
            at = child * slab + c * width
            pieces = []
            for j in range(lanes // width):
                turn = (at - j * width) % lanes
                turned = pltpu.roll(gain, turn, 1) if turn else gain
                pieces.append(turned[:, :128])
            stack = jnp.concatenate(pieces, axis=0)
            total = jnp.where((column >= at) & (column < at + width), stack, total)
    turned = total.T
    for child in range(2):
        out_ref[:, child, :] = turned[child * slab : (child + 1) * slab]


def finish(width, nbins, line, route, parts):
    flat = [x for part in parts for x in part]
    return pl.pallas_call(
        functools.partial(finish_kernel, width, line),
        in_specs=[VMEM_SPEC] * (1 + len(flat)),
        out_specs=VMEM_SPEC,
        out_shape=jax.ShapeDtypeStruct((width * len(parts), 2, nbins), jnp.float32),
        compiler_params=pltpu.CompilerParams(vmem_limit_bytes=16 * MIB),
        name="finish",
    )(route, *flat)


def one_of(z, members):
    hit = z == members[0]
    for m in members[1:]:
        hit = hit | (z == m)
    return hit


def sum_line(line, chunks, units, unit, set_up):
    plan = plan_of(line)
    z = lax.axis_index("dp")
    from_left = [None] * chunks
    from_right = [None] * chunks
    arrived = []

    def pick(kind, step, c):
        where_at = {}
        for zz in range(line):
            for p, role in enumerate(plan[zz]):
                if role[:2] == (kind, step):
                    where_at.setdefault(p, []).append(zz)
        spots = sorted(where_at)
        value = units[spots[0], c]
        for p in spots[1:]:
            value = jnp.where(one_of(z, where_at[p]), units[p, c], value)
        return value

    def tie_of(step, c):
        at = min(step * chunks + c - 3, (line - 2) * chunks - 1)
        return (arrived[at],) if at >= 0 else (units[0, chunks - 1],)

    last = line - 1
    for step in range(last):
        for c in range(chunks):
            if step > 0:
                units[step, c] = unit(step, c, tie_of(step, c))
            to_right = pick("R", step, c)
            to_left = pick("L", step, c)
            if step > 0:
                to_right = to_right + from_left[c]
                to_left = to_left + from_right[c]
            from_left[c] = lax.ppermute(to_right, "dp", [(i, i + 1) for i in range(step + 1)])
            from_right[c] = lax.ppermute(to_left, "dp", [(line - 1 - i, line - 2 - i) for i in range(step + 1)])
            arrived.append(from_left[c])
    layout = set_up(tie_of(last, 0)[0])
    return [unit(last, c, tie_of(last, c)) for c in range(chunks)], from_left, from_right, layout


def sum_line_of_4(line, chunks, units, unit, set_up):
    inward, outer, middle = [(0, 1), (3, 2)], [(0, 1), (1, 0), (2, 3), (3, 2)], [(1, 2), (2, 1)]
    a0, a1, a2, b1, b2, last = {}, {}, {}, {}, {}, {}
    final = chunks - 1
    for c in range(chunks):
        a0[c] = lax.ppermute(units[0, c], "dp", inward)
    for c in range(chunks):
        units[1, c] = unit(1, c, (units[1, c - 1] if c else units[0, final],))
        a1[c] = lax.ppermute(units[1, c], "dp", inward)
        b1[c] = lax.ppermute(sum_after(units[0, c], a0[c], units[1, c]), "dp", middle)
    for c in range(chunks):
        units[2, c] = unit(2, c, (units[2, c - 1], b1[c - 1], a1[c - 1]) if c else (units[1, final], a0[final]))
        a2[c] = lax.ppermute(units[2, c] + b1[c], "dp", outer)
    for c in range(chunks):
        last[c] = unit(3, c, (last[c - 1], a1[c]) if c else (units[2, final], b1[final]))
    for c in range(chunks):
        b2[c] = lax.ppermute(sum_after(units[1, c], a1[c], last[c - 1] if c else units[2, c]), "dp", middle)
    return last, a2, b2, set_up(last[final])


def per_device(bins, grads, hess, node_side, signs, child_owner, parent_owner, parent_grad, parent_hess, node_low, node_high):
    line = lax.axis_size("dp")
    kdim = grads.shape[1]
    nbins = parent_hess.shape[2]
    slab = parent_grad.shape[1]
    chunks = CHUNKS if slab >= 32 else 1
    width = slab // chunks
    lanes = min(256, width * nbins * kdim // 128)
    levels = nbins // (lanes // width)

    own, send, wt, wt_send = prep(line, slab, parent_owner, bins, grads, hess, node_side)
    swap = [(0, 1), (1, 0)]
    wt_other = lax.ppermute(wt_send, "sub", swap)
    other = lax.ppermute(send, "sub", swap)
    mine = (own, wt)
    theirs = (other, wt_other)

    def unit(p, c, pairs, init=None, tie=()):
        return hist(p * slab + c * width, width, levels, lanes, kdim, pairs, init, tie)

    def set_up(tie):
        return parent_layout(
            width, levels, lanes, kdim, chunks, child_owner, parent_owner, node_low, node_high, signs, parent_grad[0], parent_hess[0], tie
        )

    units = {}
    units[0, 0] = unit(0, 0, [theirs], unit(0, 0, [mine]))
    for c in range(1, chunks):
        units[0, c] = unit(0, c, [mine, theirs], tie=(units[0, c - 1],))
    collect = sum_line_of_4 if line == 4 else sum_line
    last, from_left, from_right, layout = collect(line, chunks, units, lambda p, c, tie: unit(p, c, [mine, theirs], tie=tie), set_up)
    par_grad, par_hess, bounds, route = layout

    done = []
    for c in range(chunks):
        gain = gains_of(
            width, levels, lanes, kdim, last[c], from_left[c], from_right[c], par_grad[c], par_hess[c], bounds[c], last[chunks - 1]
        )
        got = [gain] + [lax.ppermute(gain, "dp", [(i, i ^ s) for i in range(line)]) for s in range(1, line)]
        crossed = lax.ppermute(chosen(route[1, 0], got), "sub", swap)
        done.append([*got, crossed])
    return finish(width, nbins, line, route, done)[None]


def solution(mesh):
    return jax.shard_map(
        per_device,
        mesh=mesh,
        in_specs=(
            P(("groups", "dp", "sub"), "feat"),
            P(("groups", "dp", "sub"), None),
            P(("groups", "dp", "sub")),
            P(("groups", "dp", "sub")),
            P("groups"),
            P("groups"),
            P("groups"),
            P(("groups", "dp", "sub"), "feat", None),
            P(("groups", "dp", "sub"), "feat", None),
            P("groups"),
            P("groups"),
        ),
        out_specs=P(("groups", "dp", "sub"), "feat", None, None),
        check_vma=False,
    )
```

```python
import functools

import jax
import jax.numpy as jnp
from jax import lax
from jax.experimental import pallas as pl
from jax.experimental.pallas import tpu as pltpu
from jax.sharding import PartitionSpec as P

reg_lambda = 1.0
CHUNKS = 2
TILE = 256
PACK = 128
FAST = 9
HEAD = 5
PREP_MIB = 56
MIB = 1024 * 1024
VMEM_SPEC = pl.BlockSpec(memory_space=pltpu.VMEM)
SMEM_SPEC = pl.BlockSpec(memory_space=pltpu.SMEM)


def sum_after_kernel(x_ref, y_ref, tie_ref, out_ref):
    del tie_ref
    out_ref[...] = x_ref[...] + y_ref[...]


def sum_after(x, y, tie):
    return pl.pallas_call(
        sum_after_kernel,
        in_specs=[VMEM_SPEC] * 2 + [pl.BlockSpec(memory_space=pl.ANY)],
        out_specs=VMEM_SPEC,
        out_shape=jax.ShapeDtypeStruct(x.shape, jnp.float32),
        compiler_params=pltpu.CompilerParams(vmem_limit_bytes=16 * MIB),
        cost_estimate=pl.CostEstimate(flops=x.size, bytes_accessed=12 * x.size, transcendentals=0),
        name="sum_after",
    )(x, y, tie)


def plan_of(line):
    roles = []
    for z in range(line):
        mine = []
        for step in range(line - 1):
            now = []
            if z <= step:
                now.append(("R", step, line - 1 - step + z))
            if line - 1 - z <= step:
                now.append(("L", step, step - (line - 1 - z)))
            mine.extend(now if 2 * z < line else now[::-1])
        mine.append(("F", line - 1, z))
        roles.append(mine)
    return roles


def prep_kernel(line, slab, owner_ref, bins_ref, grads_ref, hess_ref, side_ref, own_ref, send_ref, buf_ref, sems, acc_ref, acc_w_ref, own_buf, send_buf, out_sems):
    rows, f_dev = bins_ref.shape
    half = f_dev // 2
    kdim = grads_ref.shape[0]
    reach = TILE + PACK
    blocks = rows // TILE
    copies = []
    for i in range(blocks):
        part = pl.ds(i * TILE, TILE)
        copies.append(pltpu.make_async_copy(bins_ref.at[part, :], buf_ref.at[part, :], sems.at[i]))
        copies[-1].start()

    hess_row = hess_ref[...].astype(jnp.float32).reshape(1, rows)
    ones = [jnp.where(side_ref[:, i * TILE : (i + 1) * TILE] == 1, 1.0, 0.0) for i in range(blocks)]
    counts = [jnp.sum(x).astype(jnp.int32) for x in ones]
    bases = [jnp.int32(0)]
    for count in counts:
        bases.append(bases[-1] + count)
    starts = [pl.multiple_of((base // PACK) * PACK, PACK) for base in bases]
    marks = jnp.concatenate(ones, axis=0)
    before = lax.broadcasted_iota(jnp.int32, (TILE, TILE), 0) < lax.broadcasted_iota(jnp.int32, (TILE, TILE), 1)
    before = jnp.where(before, 1.0, 0.0).astype(jnp.bfloat16)
    ahead = jnp.dot(marks.astype(jnp.bfloat16), before, preferred_element_type=jnp.float32).astype(jnp.int32)
    slot = lax.broadcasted_iota(jnp.int32, (reach, TILE), 0)
    acc_ref[:PACK, :] = jnp.zeros((PACK, f_dev), jnp.bfloat16)
    acc_w_ref[:, :PACK] = jnp.zeros((acc_w_ref.shape[0], PACK), jnp.float32)

    z, core = lax.axis_index("dp"), lax.axis_index("sub")
    column = lax.broadcasted_iota(jnp.int32, (1, f_dev), 1)
    position = lax.rem(column, half) // slab
    table = plan_of(line)
    chip = jnp.zeros_like(column)
    for p in range(line):
        target = jnp.int32(0)
        for zz in range(line):
            target = jnp.where(z == zz, jnp.int32(table[zz][p][2]), target)
        chip = jnp.where(position == p, target, chip)
    owner = 2 * chip + jnp.where(column < half, core, 1 - core)
    source = jnp.zeros_like(column)
    for q in range(2 * line):
        source = jnp.where(owner == owner_ref[q], q, source)
    source = source * slab + lax.rem(column, slab)
    perm = jnp.where(lax.broadcasted_iota(jnp.int32, (f_dev, f_dev), 0) == source, 1.0, 0.0).astype(jnp.bfloat16)

    for copy in copies:
        copy.wait()
    for i in range(blocks):
        part = slice(i * TILE, (i + 1) * TILE)
        goal = jnp.where(ones[i] > 0.5, ahead[i : i + 1] + (bases[i] - starts[i]), -1)
        pack = jnp.where(slot == goal, 1.0, 0.0).astype(jnp.bfloat16)
        hess = jnp.broadcast_to(hess_row[:, part], (16, TILE))
        first = lax.broadcasted_iota(jnp.int32, hess.shape, 0) == 0
        weights = jnp.concatenate([grads_ref[:, part].astype(jnp.float32), jnp.where(first, hess, 0.0)], axis=0)
        packed_w = lax.dot_general(weights.astype(jnp.bfloat16), pack, (((1,), (1,)), ((), ())), preferred_element_type=jnp.float32)
        acc_w_ref[:, pl.ds(starts[i], PACK)] += packed_w[:, :PACK]
        acc_w_ref[:, pl.ds(starts[i] + PACK, TILE)] = packed_w[:, PACK:]
        binned = buf_ref[part, :].astype(jnp.float32).astype(jnp.bfloat16)
        packed = jnp.dot(pack, binned, preferred_element_type=jnp.float32).astype(jnp.bfloat16)
        acc_ref[pl.ds(starts[i], PACK), :] += packed[:PACK]
        acc_ref[pl.ds(starts[i] + PACK, TILE), :] = packed[PACK:]

    def move(t, carry):
        part = pl.ds(pl.multiple_of(t * TILE, TILE), TILE)
        moved = jnp.dot(acc_ref[part, :], perm, preferred_element_type=jnp.float32)
        own_buf[part, :] = moved[:, :half].astype(jnp.bfloat16)
        send_buf[part, :] = moved[:, half:]
        pltpu.make_async_copy(own_buf.at[part, :], own_ref.at[part, :], out_sems.at[t, 0]).start()
        pltpu.make_async_copy(send_buf.at[part, :], send_ref.at[part, :], out_sems.at[t, 1]).start()
        return carry

    def moved_out(t, carry):
        part = pl.ds(pl.multiple_of(t * TILE, TILE), TILE)
        pltpu.make_async_copy(own_buf.at[part, :], own_ref.at[part, :], out_sems.at[t, 0]).wait()
        pltpu.make_async_copy(send_buf.at[part, :], send_ref.at[part, :], out_sems.at[t, 1]).wait()
        return carry

    total = bases[blocks]
    used = jnp.maximum((total + TILE - 1) // TILE, HEAD)
    head = pl.ds(0, HEAD * TILE)
    send_buf[head, :] = jnp.dot(acc_ref[head, :], perm[:, half:], preferred_element_type=jnp.float32)
    send_head = pltpu.make_async_copy(send_buf.at[head, :], send_ref.at[head, :], out_sems.at[0, 1])
    send_head.start()
    own_buf[head, :] = jnp.dot(acc_ref[head, :], perm[:, :half], preferred_element_type=jnp.float32).astype(jnp.bfloat16)
    own_head = pltpu.make_async_copy(own_buf.at[head, :], own_ref.at[head, :], out_sems.at[0, 0])
    own_head.start()
    lax.fori_loop(HEAD, used, move, 0)
    lane = lax.broadcasted_iota(jnp.int32, (acc_w_ref.shape[0], rows), 1)
    row = lax.broadcasted_iota(jnp.int32, lane.shape, 0)
    packed = jnp.where(lane < total, acc_w_ref[:, :rows], 0.0)
    packs = ((total + PACK - 1) // PACK).astype(jnp.float32)
    packed = jnp.where(row == kdim + 1, packs, packed)
    for i in range(rows // half):
        part = packed[:, i * half : (i + 1) * half]
        own_buf[rows + i * (kdim + 16) : rows + (i + 1) * (kdim + 16), :] = part.astype(jnp.bfloat16)
        send_buf[rows + i * (kdim + 16) : rows + (i + 1) * (kdim + 16), :] = part
    below = pl.ds(rows, own_ref.shape[0] - rows)
    own_tail = pltpu.make_async_copy(own_buf.at[below, :], own_ref.at[below, :], out_sems.at[blocks, 0])
    own_tail.start()
    send_tail = pltpu.make_async_copy(send_buf.at[below, :], send_ref.at[below, :], out_sems.at[blocks, 1])
    send_tail.start()
    own_tail.wait()
    send_tail.wait()
    send_head.wait()
    own_head.wait()
    lax.fori_loop(HEAD, used, moved_out, 0)


def prep(line, slab, owners, bins, grads, hess, side):
    rows, f_dev = bins.shape
    kdim = grads.shape[1]
    half = f_dev // 2
    height = rows + (kdim + 16) * (rows // half)
    return pl.pallas_call(
        functools.partial(prep_kernel, line, slab),
        in_specs=[SMEM_SPEC, pl.BlockSpec(memory_space=pl.ANY), VMEM_SPEC, VMEM_SPEC, VMEM_SPEC],
        out_specs=[pl.BlockSpec(memory_space=pl.ANY)] * 2,
        out_shape=[
            jax.ShapeDtypeStruct((height, half), jnp.bfloat16),
            jax.ShapeDtypeStruct((height, half), jnp.float32),
        ],
        scratch_shapes=[
            pltpu.VMEM((rows, f_dev), jnp.int32),
            pltpu.SemaphoreType.DMA((rows // TILE,)),
            pltpu.VMEM((rows + TILE + PACK, f_dev), jnp.bfloat16),
            pltpu.VMEM((kdim + 16, rows + TILE + PACK), jnp.float32),
            pltpu.VMEM((height, half), jnp.bfloat16),
            pltpu.VMEM((height, half), jnp.float32),
            pltpu.SemaphoreType.DMA((rows // TILE + 1, 2)),
        ],
        compiler_params=pltpu.CompilerParams(vmem_limit_bytes=PREP_MIB * MIB),
        cost_estimate=pl.CostEstimate(flops=4 * rows * f_dev * f_dev, bytes_accessed=8 * rows * f_dev, transcendentals=0),
        name="prep",
    )(owners, bins, grads.T, hess, side.reshape(1, rows))


def tiles_in(rows_ref, rows, kdim):
    first = rows_ref[rows : rows + kdim + 16, :].astype(jnp.float32)
    return jnp.max(first[kdim + 1 : kdim + 2]).astype(jnp.int32)


def hist_kernel(first_column, width, levels, rows, parts, kdim, has_init, *refs):
    sources = refs[:parts]
    init_ref = refs[parts] if has_init else None
    out_ref, rel_ref, wt_ref = refs[-3:]
    lanes = out_ref.shape[1]
    half = sources[0].shape[1]
    src = lax.broadcasted_iota(jnp.int32, (half, lanes), 0)
    dst = lax.broadcasted_iota(jnp.int32, (half, lanes), 1)
    spread = jnp.where(src == first_column + lax.rem(dst, width), 1.0, 0.0).astype(jnp.bfloat16)
    lane = lax.broadcasted_iota(jnp.int32, (1, lanes), 1)
    shift = ((lane // width) * levels).astype(jnp.float32)
    one = jnp.ones((TILE, lanes), jnp.bfloat16)
    zero = jnp.zeros((TILE, lanes), jnp.bfloat16)

    def place_rows(bins_ref, source, target, size):
        block = bins_ref[pl.ds(source, size), :].astype(jnp.bfloat16)
        moved = jnp.dot(block, spread, preferred_element_type=jnp.float32)
        rel_ref[pl.ds(target, size), :] = (moved - shift).astype(jnp.bfloat16)

    def place_weights(height):
        for i, rows_ref in enumerate(sources):
            for j in range(0, height, half):
                size = min(half, height - j)
                at = rows + (j // half) * (kdim + 16)
                weights = rows_ref[at : at + kdim + 16, :].astype(jnp.bfloat16)
                wt_ref[:, i * height + j : i * height + j + size] = weights[:, :size]

    def sums_of(some, tiles):
        values = [jnp.full((TILE, lanes), b.astype(jnp.float32), jnp.float32).astype(jnp.bfloat16) for b in some]
        totals = [jnp.zeros((wt_ref.shape[0], lanes), jnp.float32) for _ in some]
        for first, size in tiles:
            found = rel_ref[pl.ds(first, size), :]
            weights = wt_ref[:, pl.ds(first, size)]
            for i, value in enumerate(values):
                onehot = jnp.where(found == value[:size], one[:size], zero[:size])
                totals[i] = totals[i] + jnp.dot(weights, onehot, preferred_element_type=jnp.float32)
        return [(total[:kdim], total[kdim : kdim + 1]) for total in totals]

    def spots_of(b):
        return pl.ds(pl.multiple_of(b * kdim, kdim), kdim), pl.ds(levels * kdim + b, 1)

    def fast():
        height = FAST * PACK
        for i, bins_ref in enumerate(sources):
            for r in range(0, height, 3 * PACK):
                place_rows(bins_ref, r, i * height + r, 3 * PACK)
        place_weights(height)
        tiles = [(r, min(TILE, parts * height - r)) for r in range(0, parts * height, TILE)]

        together = 4 if parts == 1 and levels % 4 == 0 else 2

        def some_levels(step, carry):
            some = [together * step + i for i in range(together)]
            for b, (grad, hess) in zip(some, sums_of(some, tiles)):
                grad_spot, hess_spot = spots_of(b)
                if has_init:
                    grad, hess = grad + init_ref[grad_spot, :], hess + init_ref[hess_spot, :]
                out_ref[grad_spot, :] = grad
                out_ref[hess_spot, :] = hess
            return carry

        lax.fori_loop(0, levels // together, some_levels, 0)

    def general():
        for i, bins_ref in enumerate(sources):

            def one_pack(p, carry):
                r = pl.multiple_of(p * PACK, PACK)
                place_rows(bins_ref, r, i * rows + r, PACK)
                return carry

            lax.fori_loop(0, rows // PACK, one_pack, 0)
        place_weights(rows)
        out_ref[...] = init_ref[...] if has_init else jnp.zeros(out_ref.shape, jnp.float32)
        step = 2 * TILE

        def group(g, carry):
            first = pl.multiple_of(g * step, step)

            def level(b, carry):
                ((grad, hess),) = sums_of([b], [(first, TILE), (first + TILE, TILE)])
                grad_spot, hess_spot = spots_of(b)
                out_ref[grad_spot, :] += grad
                out_ref[hess_spot, :] += hess
                return carry

            return lax.fori_loop(0, levels, level, carry)

        lax.fori_loop(0, parts * rows // step, group, 0)

    needed = tiles_in(sources[0], rows, kdim)
    for rows_ref in sources[1:]:
        needed = jnp.maximum(needed, tiles_in(rows_ref, rows, kdim))
    if FAST * PACK < rows:
        pl.when(needed <= FAST)(fast)
        pl.when(needed > FAST)(general)
    else:
        general()


def hist(first_column, width, levels, lanes, rows, kdim, sources, init=None, tie=()):
    parts = len(sources)
    operands = list(sources)
    if init is not None:
        operands.append(init)
    specs = [VMEM_SPEC] * len(operands) + [pl.BlockSpec(memory_space=pl.ANY)] * len(tie)
    height = levels * (kdim + 1)
    return pl.pallas_call(
        functools.partial(hist_kernel, first_column, width, levels, rows, parts, kdim, init is not None),
        in_specs=specs,
        out_specs=VMEM_SPEC,
        out_shape=jax.ShapeDtypeStruct((height, lanes), jnp.float32),
        scratch_shapes=[
            pltpu.VMEM((parts * rows, lanes), jnp.bfloat16),
            pltpu.VMEM((kdim + 16, parts * rows), jnp.bfloat16),
        ],
        compiler_params=pltpu.CompilerParams(vmem_limit_bytes=20 * MIB),
        cost_estimate=pl.CostEstimate(
            flops=parts * rows * lanes, bytes_accessed=parts * rows * lanes, transcendentals=0
        ),
        name="hist",
    )(*operands, *tie)


def source_of(place, child_ref, parent_ref):
    source = jnp.int32(0)
    for q in range(child_ref.shape[0]):
        source = jnp.where(child_ref[q] == place, parent_ref[q], source)
    return source


def repeat_lanes(x, width, lanes):
    if lanes > x.shape[1]:
        x = jnp.concatenate([x] * (lanes // x.shape[1]), axis=1)
    x = jnp.where(lax.broadcasted_iota(jnp.int32, x.shape, 1) < width, x[:, :lanes], 0)
    reach = width
    while reach < lanes:
        x = x + pltpu.roll(x, reach, 1)
        reach *= 2
    return x


def layout_kernel(width, levels, kdim, chunks, child_ref, owner_ref, low_ref, high_ref, sign_ref, parent_ref, hess_ref, tie_ref, *out_refs):
    del tie_ref
    grad_refs, hess_refs, bound_refs = out_refs[:chunks], out_refs[chunks : 2 * chunks], out_refs[2 * chunks : 3 * chunks]
    lanes = grad_refs[0].shape[1]
    slab = width * chunks
    owners = owner_ref.shape[0]
    z, core = lax.axis_index("dp"), lax.axis_index("sub")
    place = 2 * z + core
    mine = source_of(place, child_ref, owner_ref)
    twin = source_of(2 * z + 1 - core, child_ref, owner_ref)
    row = lax.broadcasted_iota(jnp.int32, (8, lanes), 0)
    route = jnp.where(row == 0, (mine // 2) ^ z, (twin // 2) ^ z)
    out_refs[-1][...] = jnp.where(row == 2, jnp.where(lax.rem(mine, 2) == core, 1, 0), route)
    slab_at = jnp.int32(0)
    for q in range(owners):
        slab_at = jnp.where(owner_ref[q] == place, q, slab_at)
    offset = lax.axis_index("feat") * (owners * slab) + slab_at * slab
    features = sign_ref.shape[1]
    signs = jnp.broadcast_to(sign_ref[...], (8, features))
    per_tile = 128 // width
    step = 128 // kdim
    for c in range(chunks):
        turned = pltpu.roll(signs, lax.rem(features - offset - c * width + features, features), 1)
        sign = repeat_lanes(turned[:, :128], width, lanes)[:1]
        bounds = []
        for child in range(2):
            low = low_ref[child].astype(jnp.float32) / 1024.0
            high = high_ref[child].astype(jnp.float32) / 1024.0
            middle = 0.5 * (low + high)
            bounds.append(jnp.where(sign < 0, middle, low))
            bounds.append(jnp.where(sign > 0, middle, high))
            bounds.append(jnp.where(sign > 0, middle, low))
            bounds.append(jnp.where(sign < 0, middle, high))
        bound_refs[c][...] = jnp.concatenate(bounds, axis=0)
        rows = hess_ref[c * width : (c + 1) * width, :]
        turned = jnp.concatenate([rows] * (128 // width), axis=0).T
        total = jnp.zeros((levels, lanes), jnp.float32)
        for j in range(lanes // width):
            piece = turned[j * levels : (j + 1) * levels, :]
            piece = jnp.concatenate([piece] * (lanes // 128), axis=1)
            group = lax.broadcasted_iota(jnp.int32, piece.shape, 1) // width
            total = jnp.where(group == j, piece, total)
        hess_refs[c][...] = total
        for tile in range(lanes // 128):
            for b in range(0, levels, step):
                rows = []
                for jj in range(per_tile):
                    bin_at = (tile * per_tile + jj) * levels + b
                    rows.append(parent_ref[c * width : (c + 1) * width, bin_at * kdim : bin_at * kdim + 128])
                block = jnp.concatenate(rows, axis=0) if per_tile > 1 else rows[0]
                grad_refs[c][b * kdim : b * kdim + 128, tile * 128 : (tile + 1) * 128] = block.T


def parent_layout(width, levels, lanes, kdim, chunks, child_owner, owners, low, high, signs, parent, hess, tie):
    shapes = [jax.ShapeDtypeStruct((levels * kdim, lanes), jnp.float32)] * chunks
    shapes += [jax.ShapeDtypeStruct((levels, lanes), jnp.float32)] * chunks
    shapes += [jax.ShapeDtypeStruct((8, lanes), jnp.float32)] * chunks
    shapes += [jax.ShapeDtypeStruct((8, lanes), jnp.int32)]
    out = pl.pallas_call(
        functools.partial(layout_kernel, width, levels, kdim, chunks),
        in_specs=[SMEM_SPEC] * 4 + [VMEM_SPEC] * 3 + [pl.BlockSpec(memory_space=pl.ANY)],
        out_specs=[VMEM_SPEC] * (3 * chunks + 1),
        out_shape=shapes,
        compiler_params=pltpu.CompilerParams(vmem_limit_bytes=16 * MIB),
        cost_estimate=pl.CostEstimate(flops=0, bytes_accessed=2 * parent.size * 4, transcendentals=0),
        name="parent_layout",
    )(child_owner, owners, low, high, signs.reshape(1, -1), parent, hess, tie)
    return out[:chunks], out[chunks : 2 * chunks], out[2 * chunks : 3 * chunks], out[-1]


def lane_prefix(total, width):
    lanes = total.shape[1]
    lane = lax.broadcasted_iota(jnp.int32, total.shape, 1)
    running = total
    reach = width
    while reach < lanes:
        running = running + jnp.where(lane >= reach, pltpu.roll(running, reach, 1), 0.0)
        reach *= 2
    whole = total
    reach = width
    while reach < lanes:
        whole = whole + pltpu.roll(whole, reach, 1)
        reach *= 2
    return running - total, running, whole


def gain_kernel(width, levels, kdim, last_ref, right_ref, left_ref, par_grad_ref, par_hess_ref, bound_ref, tie_ref, out_ref, grad_ref, hess_ref):
    del tie_ref
    hess_at = levels * kdim
    lanes = out_ref.shape[2]

    def small_at(start, size):
        return last_ref[pl.ds(start, size), :] + right_ref[pl.ds(start, size), :] + left_ref[pl.ds(start, size), :]

    small_hess = small_at(hess_at, levels)
    hess_ref[0] = small_hess
    hess_ref[1] = par_hess_ref[...] - small_hess

    def add_up(b, carry):
        g0, g1, h0, h1 = carry
        start = pl.multiple_of(b * kdim, kdim)
        small = small_at(start, kdim)
        g0 = g0 + small
        g1 = g1 + (par_grad_ref[pl.ds(start, kdim), :] - small)
        h0 = h0 + hess_ref[0, pl.ds(b, 1), :]
        h1 = h1 + hess_ref[1, pl.ds(b, 1), :]
        grad_ref[0, pl.ds(start, kdim), :] = g0
        grad_ref[1, pl.ds(start, kdim), :] = g1
        hess_ref[0, pl.ds(b, 1), :] = h0
        hess_ref[1, pl.ds(b, 1), :] = h1
        return g0, g1, h0, h1

    zero_g = jnp.zeros((kdim, lanes), jnp.float32)
    zero_h = jnp.zeros((1, lanes), jnp.float32)
    ends = lax.fori_loop(0, levels, add_up, (zero_g, zero_g, zero_h, zero_h), unroll=4)
    for c in range(2):
        low_left, high_left, low_right, high_right = [bound_ref[4 * c + i : 4 * c + i + 1, :] for i in range(4)]
        grad_before, _, grad_all = lane_prefix(ends[c], width)
        hess_rows = jnp.broadcast_to(ends[2 + c], (8, lanes))
        hess_before, _, hess_all = lane_prefix(hess_rows, width)
        hess_before, hess_all = hess_before[:1], hess_all[:1]

        def score(grad, hess, lower, upper):
            denom = jnp.maximum(hess, 0.0) + reg_lambda
            weight = jnp.clip(-grad / denom, lower, upper)
            return jnp.sum((2.0 * grad + denom * weight) * weight, axis=0, keepdims=True)

        def one_bin(b, carry):
            start = pl.multiple_of(b * kdim, kdim)
            grad_left = grad_ref[c, pl.ds(start, kdim), :] + grad_before
            hess_left = hess_ref[c, pl.ds(b, 1), :] + hess_before
            left = score(grad_left, hess_left, low_left, high_left)
            right = score(grad_all - grad_left, hess_all - hess_left, low_right, high_right)
            out_ref[c, pl.ds(b, 1), :] = (left + right) * (-1.0 / kdim)
            return carry

        lax.fori_loop(0, levels, one_bin, 0, unroll=4)


def gains_of(width, levels, lanes, kdim, last, right, left, par_grad, par_hess, bounds, tie):
    return pl.pallas_call(
        functools.partial(gain_kernel, width, levels, kdim),
        in_specs=[VMEM_SPEC] * 6 + [pl.BlockSpec(memory_space=pl.ANY)],
        out_specs=VMEM_SPEC,
        out_shape=jax.ShapeDtypeStruct((2, levels, lanes), jnp.float32),
        scratch_shapes=[
            pltpu.VMEM((2, levels * kdim, lanes), jnp.float32),
            pltpu.VMEM((2, levels, lanes), jnp.float32),
        ],
        compiler_params=pltpu.CompilerParams(vmem_limit_bytes=24 * MIB),
        cost_estimate=pl.CostEstimate(flops=50 * levels * kdim * lanes, bytes_accessed=16 * levels * kdim * lanes, transcendentals=0),
        name="gains",
    )(last, right, left, par_grad, par_hess, bounds, tie)


def chosen(shift, got):
    value = got[0]
    for s in range(1, len(got)):
        value = jnp.where(shift == s, got[s], value)
    return value


def finish_kernel(width, line, route_ref, *refs):
    out_ref = refs[-1]
    chunks = (len(refs) - 1) // (line + 1)
    slab = width * chunks
    lanes = route_ref.shape[1]
    shift, same = route_ref[:1, :], route_ref[2:3, :]
    total = jnp.zeros((128, 128), jnp.float32)
    column = lax.broadcasted_iota(jnp.int32, (128, 128), 1)
    for child in range(2):
        for c in range(chunks):
            got = [ref[child] for ref in refs[c * (line + 1) : (c + 1) * (line + 1)]]
            gain = jnp.where(same == 1, chosen(shift, got[:line]), got[line])
            at = child * slab + c * width
            pieces = []
            for j in range(lanes // width):
                turn = (at - j * width) % lanes
                turned = pltpu.roll(gain, turn, 1) if turn else gain
                pieces.append(turned[:, :128])
            stack = jnp.concatenate(pieces, axis=0)
            total = jnp.where((column >= at) & (column < at + width), stack, total)
    turned = total.T
    for child in range(2):
        out_ref[:, child, :] = turned[child * slab : (child + 1) * slab]


def finish(width, nbins, line, route, parts):
    flat = [x for part in parts for x in part]
    return pl.pallas_call(
        functools.partial(finish_kernel, width, line),
        in_specs=[VMEM_SPEC] * (1 + len(flat)),
        out_specs=VMEM_SPEC,
        out_shape=jax.ShapeDtypeStruct((width * len(parts), 2, nbins), jnp.float32),
        compiler_params=pltpu.CompilerParams(vmem_limit_bytes=16 * MIB),
        name="finish",
    )(route, *flat)


def one_of(z, members):
    hit = z == members[0]
    for m in members[1:]:
        hit = hit | (z == m)
    return hit


def sum_line(line, chunks, units, unit, set_up):
    plan = plan_of(line)
    z = lax.axis_index("dp")
    from_left = [None] * chunks
    from_right = [None] * chunks
    arrived = []

    def pick(kind, step, c):
        where_at = {}
        for zz in range(line):
            for p, role in enumerate(plan[zz]):
                if role[:2] == (kind, step):
                    where_at.setdefault(p, []).append(zz)
        spots = sorted(where_at)
        value = units[spots[0], c]
        for p in spots[1:]:
            value = jnp.where(one_of(z, where_at[p]), units[p, c], value)
        return value

    def tie_of(step, c):
        at = min(step * chunks + c - 3, (line - 2) * chunks - 1)
        return (arrived[at],) if at >= 0 else (units[0, chunks - 1],)

    last = line - 1
    for step in range(last):
        for c in range(chunks):
            if step > 0:
                units[step, c] = unit(step, c, tie_of(step, c))
            to_right = pick("R", step, c)
            to_left = pick("L", step, c)
            if step > 0:
                to_right = to_right + from_left[c]
                to_left = to_left + from_right[c]
            from_left[c] = lax.ppermute(to_right, "dp", [(i, i + 1) for i in range(step + 1)])
            from_right[c] = lax.ppermute(to_left, "dp", [(line - 1 - i, line - 2 - i) for i in range(step + 1)])
            arrived.append(from_left[c])
    layout = set_up(tie_of(last, 0)[0])
    return [unit(last, c, tie_of(last, c)) for c in range(chunks)], from_left, from_right, layout


def sum_line_of_4(line, chunks, units, unit, set_up):
    inward, outer, middle = [(0, 1), (3, 2)], [(0, 1), (1, 0), (2, 3), (3, 2)], [(1, 2), (2, 1)]
    a0, a1, a2, b1, b2, last = {}, {}, {}, {}, {}, {}
    final = chunks - 1
    for c in range(chunks):
        a0[c] = lax.ppermute(units[0, c], "dp", inward)
    for c in range(chunks):
        units[1, c] = unit(1, c, (units[1, c - 1] if c else units[0, final],))
        a1[c] = lax.ppermute(units[1, c], "dp", inward)
        b1[c] = lax.ppermute(sum_after(units[0, c], a0[c], units[1, c]), "dp", middle)
    for c in range(chunks):
        units[2, c] = unit(2, c, (units[2, c - 1], b1[c - 1], a1[c - 1]) if c else (units[1, final], a0[final]))
        a2[c] = lax.ppermute(units[2, c] + b1[c], "dp", outer)
    for c in range(chunks):
        last[c] = unit(3, c, (last[c - 1], a1[c]) if c else (units[2, final], b1[final]))
    for c in range(chunks):
        b2[c] = lax.ppermute(sum_after(units[1, c], a1[c], last[c - 1] if c else units[2, c]), "dp", middle)
    return last, a2, b2, set_up(last[final])


def per_device(bins, grads, hess, node_side, signs, child_owner, parent_owner, parent_grad, parent_hess, node_low, node_high):
    line = lax.axis_size("dp")
    kdim = grads.shape[1]
    nbins = parent_hess.shape[2]
    slab = parent_grad.shape[1]
    chunks = CHUNKS if slab >= 32 else 1
    width = slab // chunks
    lanes = min(256, width * nbins * kdim // 128)
    levels = nbins // (lanes // width)

    mine, send = prep(line, slab, parent_owner, bins, grads, hess, node_side)
    swap = [(0, 1), (1, 0)]
    theirs = lax.ppermute(send, "sub", swap)

    def unit(p, c, sources, init=None, tie=()):
        return hist(p * slab + c * width, width, levels, lanes, bins.shape[0], kdim, sources, init, tie)

    def set_up(tie):
        return parent_layout(
            width, levels, lanes, kdim, chunks, child_owner, parent_owner, node_low, node_high, signs, parent_grad[0], parent_hess[0], tie
        )

    units = {}
    units[0, 0] = unit(0, 0, [theirs], unit(0, 0, [mine]))
    for c in range(1, chunks):
        units[0, c] = unit(0, c, [mine, theirs], tie=(units[0, c - 1],))
    collect = sum_line_of_4 if line == 4 else sum_line
    last, from_left, from_right, layout = collect(line, chunks, units, lambda p, c, tie: unit(p, c, [mine, theirs], tie=tie), set_up)
    par_grad, par_hess, bounds, route = layout

    done = []
    for c in range(chunks):
        gain = gains_of(
            width, levels, lanes, kdim, last[c], from_left[c], from_right[c], par_grad[c], par_hess[c], bounds[c], last[chunks - 1]
        )
        got = [gain] + [lax.ppermute(gain, "dp", [(i, i ^ s) for i in range(line)]) for s in range(1, line)]
        crossed = lax.ppermute(chosen(route[1, 0], got), "sub", swap)
        done.append([*got, crossed])
    return finish(width, nbins, line, route, done)[None]


def solution(mesh):
    return jax.shard_map(
        per_device,
        mesh=mesh,
        in_specs=(
            P(("groups", "dp", "sub"), "feat"),
            P(("groups", "dp", "sub"), None),
            P(("groups", "dp", "sub")),
            P(("groups", "dp", "sub")),
            P("groups"),
            P("groups"),
            P("groups"),
            P(("groups", "dp", "sub"), "feat", None),
            P(("groups", "dp", "sub"), "feat", None),
            P("groups"),
            P("groups"),
        ),
        out_specs=P(("groups", "dp", "sub"), "feat", None, None),
        check_vma=False,
    )
```
